32 devices in a mesh: grp: 2 (over x), slab: 16 (over z, y, core).
Axes of the slice: x: 2, y: 2, z: 4, core: 2. Of those that a mesh axis runs over, the one named last changes fastest.
Arguments:
- thermal_state_values: float32 [64, 128], P(('grp', 'slab')), may hold values from -6 to 6
- thermal_kappa_values: float32 [32, 32], P(('grp', 'slab')), may hold values from 0.5 to 2
- nodal_heating_input: float32 [64, 128], P(('grp', 'slab')), may hold values from -24 to 24
- frozen_share_map: float32 [256, 2048], P('grp', 'slab'), may hold values from 0 to 1
- crystal_label_map: int32 [256, 2048], P('grp', 'slab'), may hold values from 0 to 7999
- growth_reach_table: int32 [8000, 6], replicated, may hold values from 1 to 4
- seed_site_slots: int32 [8192], P(('grp', 'slab')), may hold values from 0 to 16383
- seed_crystal_label: int32 [8192], P(('grp', 'slab')), may hold values from 0 to 7999
Outputs:
- new_temperature: float32 [64, 128], P(('grp', 'slab'))
- new_solid: float32 [256, 2048], P('grp', 'slab')
The draws below stay inside these ranges and needn't reach their ends.
Inputs may be any that keep to these rules, and one draw needn't show every extreme that they name: `seed_site_slots`: each entry is a cell of the brick of the device that holds the entry, numbered x * 8 * 16 + y * 16 + z in that brick's own coordinates; entries may repeat.
All inputs are finite; a program needn't handle non-finite values.
Results may differ from the reference program's by a relative error of at most 0.0001.
Values sent between devices are 32-bit elements; how exact they have to be, the bound alone decides.
No kernel may reach another device: no remote copies, remote signals or barrier semaphores. Data moves between devices by JAX's collectives and lax.ppermute only.
A program may use at most 128 MiB of HBM per device.

```python
import math
import jax
import jax.numpy as jnp
from jax import lax

HEX_COUNT_LATER = 2
NSD = 256
CPC = 8
NORI = 8000
EY = 16
NEX = 32
POINTS_ALONG_X = 64
POINTS_ALONG_Y = 32
POINTS_ALONG_Z = 4
NCX = 256
NCY = 128
NCZ = 16
BX = 128
BY = 8
BCELLS = 16384
SITES = 8192
N_SLAB = 16


def plant(values, stream_key, low, high):
    longest = values.shape.index(max(values.shape))
    spots = []
    for shift in (0, 1):
        where = [jax.random.randint(jax.random.fold_in(stream_key, axis), (), 0, length) for axis, length in enumerate(values.shape)]
        where[longest] = (where[longest] + shift) % values.shape[longest]
        spots.append(tuple(where))
    return values.at[spots[0]].set(low).at[spots[1]].set(high)


def steps_of(rng, dims, split, low, top_value):
    loudness, own = 1.0, jax.random.fold_in(rng, 6)
    for position, blocks in split:
        heights = jnp.exp(jax.random.uniform(jax.random.fold_in(own, position), (blocks,), jnp.float32, low / len(split), top_value / len(split)))
        loudness = loudness * jnp.repeat(heights, dims[position] // blocks).reshape([-1 if axis == position else 1 for axis in range(len(dims))])
    return loudness


def bell_draw(rng, extent, width, bound, pieces=(), kind=jnp.bfloat16):
    values = width * jax.random.normal(rng, extent, jnp.float32)
    if pieces:
        values = values * steps_of(rng, extent, pieces, -0.22, 0.18)
    return jnp.clip(values, -bound, bound).astype(kind)


def setup_inputs(seed: int = 0) -> dict:
    arg_keys = jax.random.split(jax.random.key(seed), 9)
    return {
        "thermal_state_values": bell_draw(arg_keys[0], (POINTS_ALONG_X, POINTS_ALONG_Y * POINTS_ALONG_Z), 1.0, 6.0, ((0, 32),), jnp.float32),
        "thermal_kappa_values": jnp.clip(jnp.exp(math.log(2.0) - 1.3862944 * jax.random.uniform(arg_keys[1], (NEX, EY * HEX_COUNT_LATER), jnp.float32) ** steps_of(arg_keys[1], (NEX, EY * HEX_COUNT_LATER), ((0, 32),), -0.2, 0.2)), 0.5, 2.0),
        "nodal_heating_input": bell_draw(arg_keys[2], (POINTS_ALONG_X, POINTS_ALONG_Y * POINTS_ALONG_Z), 4.0, 24.0, ((0, 32),), jnp.float32),
        "frozen_share_map": jnp.clip(1.0 * jax.random.uniform(arg_keys[3], (NCX, NCY * NCZ), jnp.float32) ** steps_of(arg_keys[3], (NCX, NCY * NCZ), ((0, 2), (1, 16)), -0.2, 0.2), 0.0, 1.0),
        "crystal_label_map": plant(jax.random.randint(arg_keys[4], (NCX, NCY * NCZ), 0, NORI), jax.random.fold_in(arg_keys[4], 1), 0, NORI - 1).astype(jnp.int32),
        "growth_reach_table": plant(jax.random.randint(arg_keys[5], (NORI, 6), 1, 5), jax.random.fold_in(arg_keys[5], 1), 1, 4).astype(jnp.int32),
        "seed_site_slots": plant(jax.random.randint(arg_keys[6], (SITES,), 0, BCELLS), jax.random.fold_in(arg_keys[6], 1), 0, BCELLS - 1).astype(jnp.int32),
        "seed_crystal_label": plant(jax.random.randint(arg_keys[7], (SITES,), 0, NORI), jax.random.fold_in(arg_keys[7], 1), 0, NORI - 1).astype(jnp.int32),
    }


HIGHEST = lax.Precision.HIGHEST
step_size = 0.004


def stiffness_table():
    derivative = jnp.array([[-3.0, 4.0, -1.0], [-1.0, 0.0, 1.0], [1.0, -4.0, 3.0]], jnp.float32)
    quad_weight = jnp.array([1.0 / 6.0, 2.0 / 3.0, 1.0 / 6.0], jnp.float32)
    identity = jnp.eye(3, dtype=jnp.float32)
    weight_cube = jnp.kron(jnp.kron(quad_weight, quad_weight), quad_weight)
    stiffness = jnp.zeros((27, 27), jnp.float32)
    for direction in range(3):
        factors = [identity, identity, identity]
        factors[direction] = derivative
        gradient = jnp.kron(jnp.kron(factors[0], factors[1]), factors[2])
        stiffness = stiffness + jnp.dot(gradient.T * weight_cube[None, :], gradient, precision=HIGHEST)
    return stiffness


def cell_basis(length):
    points = (jnp.arange(length, dtype=jnp.float32) + 0.5) / length
    columns = jnp.stack([2.0 * (points - 0.5) * (points - 1.0), -4.0 * points * (points - 1.0), 2.0 * points * (points - 0.5)], axis=1)
    return jnp.kron(jnp.kron(columns, columns), columns)


def split_axis(tensor, which_axis, length):
    return jnp.stack([lax.slice_in_dim(tensor, offset, offset + 2 * length - 1, 2, which_axis) for offset in range(3)], 0)


def element_nodes(extended, count_x, count_y, count_z):
    tensor = split_axis(extended, 0, count_x)
    tensor = split_axis(tensor, 2, count_y)
    tensor = split_axis(tensor, 4, count_z)
    return jnp.transpose(tensor, (2, 1, 0, 3, 4, 5))


def fold_axis(tensor, which_axis, length):
    first_part, middle, last_part = tensor[0], tensor[1], tensor[2]
    place_at = which_axis - 1
    plane_shape = list(first_part.shape)
    plane_shape[place_at] = 1
    zero_plane = jnp.zeros(plane_shape, tensor.dtype)
    even_nodes = jnp.concatenate([first_part, zero_plane], place_at) + jnp.concatenate([zero_plane, last_part], place_at)
    paired = jnp.stack([lax.slice_in_dim(even_nodes, 0, length, 1, place_at), middle], place_at + 1)
    full_shape = list(first_part.shape)
    full_shape[place_at] = 2 * length
    paired = paired.reshape(full_shape)
    return jnp.concatenate([paired, lax.slice_in_dim(even_nodes, length, length + 1, 1, place_at)], place_at)


def element_action(extended, kappa, stiffness, count_x, count_y, count_z):
    nodes = element_nodes(extended, count_x, count_y, count_z).reshape(27, -1)
    acted = jnp.dot(stiffness, nodes, precision=HIGHEST) * kappa.reshape(1, -1)
    acted = acted.reshape(3, 3, 3, count_x, count_y, count_z)
    acted = jnp.transpose(acted, (2, 0, 1, 3, 4, 5))
    acted = fold_axis(acted, 5, count_z)
    acted = jnp.transpose(acted, (1, 0, 2, 3, 4))
    acted = fold_axis(acted, 3, count_y)
    return fold_axis(acted, 1, count_x)


def extend_wrap(tensor, which_axis):
    return jnp.concatenate([tensor, lax.slice_in_dim(tensor, 0, 1, 1, which_axis)], which_axis)


def fold_wrap(tensor, which_axis):
    length = tensor.shape[which_axis] - 1
    head_plane = lax.slice_in_dim(tensor, 0, 1, 1, which_axis) + lax.slice_in_dim(tensor, length, length + 1, 1, which_axis)
    return jnp.concatenate([head_plane, lax.slice_in_dim(tensor, 1, length, 1, which_axis)], which_axis)


def apply_operator(present_values, thermal_kappa_values, stiffness):
    extended = extend_wrap(extend_wrap(extend_wrap(present_values, 0), 1), 2)
    acted = element_action(extended, thermal_kappa_values, stiffness, NEX, EY, HEX_COUNT_LATER)
    return fold_wrap(fold_wrap(fold_wrap(acted, 0), 1), 2)


def node_mass(length):
    return jnp.where(jnp.arange(length) % 2 == 0, 1.0 / 3.0, 2.0 / 3.0).astype(jnp.float32)


def reference(thermal_state_values, thermal_kappa_values, nodal_heating_input, frozen_share_map, crystal_label_map, growth_reach_table, seed_site_slots, seed_crystal_label):
    stiffness = stiffness_table()
    present_values = thermal_state_values.reshape(POINTS_ALONG_X, POINTS_ALONG_Y, POINTS_ALONG_Z)
    heat_source = nodal_heating_input.reshape(POINTS_ALONG_X, POINTS_ALONG_Y, POINTS_ALONG_Z)
    lumped_mass = node_mass(POINTS_ALONG_X)[:, None, None] * node_mass(POINTS_ALONG_Y)[None, :, None] * node_mass(POINTS_ALONG_Z)[None, None, :]
    rate_one = (heat_source - apply_operator(present_values, thermal_kappa_values, stiffness)) / lumped_mass
    middle = present_values + step_size * rate_one
    rate_two = (heat_source - apply_operator(middle, thermal_kappa_values, stiffness)) / lumped_mass
    new_field = present_values + 0.5 * step_size * (rate_one + rate_two)
    extended = extend_wrap(extend_wrap(extend_wrap(new_field, 0), 1), 2)
    nodes = element_nodes(extended, NEX, EY, HEX_COUNT_LATER).reshape(27, -1)
    cell_temp = jnp.dot(cell_basis(CPC), nodes, precision=HIGHEST).reshape(CPC, CPC, CPC, NEX, EY, HEX_COUNT_LATER)
    cell_temp = jnp.transpose(cell_temp, (3, 0, 4, 1, 5, 2)).reshape(NCX, NCY, NCZ)
    undercool = jnp.maximum(-cell_temp, 0.0)
    level_table = growth_reach_table.astype(jnp.float32) / 4.0
    grid_solid = frozen_share_map.reshape(NCX, NCY, NCZ)
    grid_orient = crystal_label_map.reshape(NCX, NCY, NCZ)
    offsets = ((0, 1), (0, -1), (1, 1), (1, -1), (2, 1), (2, -1))
    gathered = jnp.zeros((NCX, NCY, NCZ), jnp.float32)
    for direction in range(6):
        which_axis, offset = offsets[direction]
        weighted = grid_solid * jnp.take(level_table[:, direction], grid_orient)
        gathered = gathered + jnp.roll(weighted, -offset, which_axis)
    mean_level = jnp.sum(growth_reach_table.astype(jnp.float32), axis=1) / 6.0
    brick_index = jnp.arange(SITES, dtype=jnp.int32) // NSD
    global_x = (brick_index // N_SLAB) * BX + seed_site_slots // (BY * NCZ)
    global_y = (brick_index % N_SLAB) * BY + (seed_site_slots // NCZ) % BY
    global_z = seed_site_slots % NCZ
    flat_index = ((global_x * NCY + global_y) * NCZ + global_z).astype(jnp.int32)
    nucleation = jnp.zeros((NCX * NCY * NCZ,), jnp.float32).at[flat_index].add(jnp.take(mean_level, seed_crystal_label))
    nucleation = nucleation.reshape(NCX, NCY, NCZ)
    capture_rate = undercool * undercool * gathered + undercool * nucleation
    new_solid = grid_solid + (1.0 - grid_solid) * (1.0 - jnp.exp(-capture_rate))
    return new_field.reshape(POINTS_ALONG_X, POINTS_ALONG_Y * POINTS_ALONG_Z), new_solid.reshape(NCX, NCY * NCZ)
```

```python
import functools

import jax
import jax.numpy as jnp
import numpy as np
from jax import lax
from jax.experimental import pallas as pl
from jax.experimental.pallas import tpu as pltpu
from jax.sharding import PartitionSpec as P

HEX_COUNT_LATER = 2
CPC = 8
LANES = 128
HIGHEST = lax.Precision.HIGHEST
STEP = 0.004
AXES = ("grp", "slab")
VMEM = pl.BlockSpec(memory_space=pltpu.VMEM)
PARAMS = pltpu.CompilerParams(vmem_limit_bytes=48 * 1024 * 1024)


def up_to(value, unit):
    return -(-value // unit) * unit


def split_index(value, by):
    if by & (by - 1) == 0:
        return value >> (by.bit_length() - 1), value & (by - 1)
    quotient = lax.div(value, jnp.full_like(value, by))
    return quotient, value - quotient * by


def pick_codes(table_ref, labels):
    half = table_ref.shape[0]
    tile, lane = labels >> 7, labels & (LANES - 1)
    upper = tile >= half
    row = jnp.where(upper, tile - half, tile)
    found = jnp.zeros(labels.shape, jnp.int32)
    for r in range(half):
        line = jnp.broadcast_to(table_ref[r : r + 1, :], labels.shape)
        here = jnp.take_along_axis(line, lane, axis=1, mode="promise_in_bounds")
        found = jnp.where(row == r, here, found)
    return jnp.where(upper, found >> 12, found) & 4095


def level(code, direction):
    return (((code >> (2 * direction)) & 3) + 1).astype(jnp.float32)


def cells_kernel(
    depth, flat, table_ref, label_ref, frozen_ref, slot_ref, seed_ref,
    packed_ref, gathered_ref, nucleation_ref, faces_ref, line_ref, code_ref,
):
    count = table_ref.shape[1]
    half = packed_ref.shape[0]
    edge_x, wide = frozen_ref.shape
    place = lax.broadcasted_iota(jnp.int32, table_ref.shape, 0)
    line_ref[...] = jnp.zeros(line_ref.shape, jnp.int32)
    word = jnp.sum((table_ref[...] - 1) << (2 * place), axis=0, keepdims=True)
    line_ref[0:1, 0:count] = word
    for r in range(half):
        low = line_ref[0:1, r * LANES : (r + 1) * LANES]
        high = line_ref[0:1, (r + half) * LANES : (r + half + 1) * LANES]
        packed_ref[r : r + 1, :] = low | (high << 12)

    def look_up(chunk, carry):
        rows = pl.ds(pl.multiple_of(chunk * 8, 8), 8)
        for t in range(wide // LANES):
            lanes = pl.ds(t * LANES, LANES)
            code_ref[rows, lanes] = pick_codes(packed_ref, label_ref[rows, lanes])
        return carry

    lax.fori_loop(0, edge_x // 8, look_up, 0, unroll=4)
    frozen = frozen_ref[...] * 0.25
    code = code_ref[...]
    shares = [frozen * level(code, d) for d in range(6)]
    line_x = lax.broadcasted_iota(jnp.int32, (edge_x, wide), 0)
    lane = lax.broadcasted_iota(jnp.int32, (edge_x, wide), 1)
    deep = lane % depth if depth & (depth - 1) else lane & (depth - 1)
    total = jnp.where(line_x == edge_x - 1, 0.0, pltpu.roll(shares[0], edge_x - 1, 0))
    total += jnp.where(line_x == 0, 0.0, pltpu.roll(shares[1], 1, 0))
    total += jnp.where(lane >= flat - depth, 0.0, pltpu.roll(shares[2], wide - depth, 1))
    total += jnp.where(lane < depth, 0.0, pltpu.roll(shares[3], depth, 1))
    total += jnp.where(
        deep == depth - 1, pltpu.roll(shares[4], depth - 1, 1), pltpu.roll(shares[4], wide - 1, 1)
    )
    total += jnp.where(
        deep == 0, pltpu.roll(shares[5], wide - (depth - 1), 1), pltpu.roll(shares[5], 1, 1)
    )
    gathered_ref[...] = total
    sides = jnp.transpose(jnp.where(lane < depth, shares[2], shares[3]))
    faces_ref[0:depth, :] = sides[0:depth]
    faces_ref[depth : 2 * depth, :] = sides[flat - depth : flat]
    sites = seed_ref.shape[0]
    codes = pick_codes(packed_ref, seed_ref[...])
    worth = sum(level(codes, d) for d in range(6))
    site_x, site_lane = split_index(slot_ref[...], flat)
    at_x = lax.broadcasted_iota(jnp.int32, (edge_x, LANES), 0)
    at_lane = lax.broadcasted_iota(jnp.int32, (wide, LANES), 0)
    added = jnp.zeros((edge_x, wide), jnp.float32)
    for r in range(sites):
        left = jnp.where(at_x == site_x[r : r + 1], worth[r : r + 1], 0.0).astype(jnp.bfloat16)
        right = jnp.where(at_lane == site_lane[r : r + 1], 1.0, 0.0).astype(jnp.bfloat16)
        added += lax.dot_general(
            left, right, (((1,), (1,)), ((), ())), preferred_element_type=jnp.float32
        )
    nucleation_ref[...] = added * (1.0 / 6.0)


def spread_tables(width, plane):
    rows_y, deep = width // plane, plane // 2
    along = np.zeros((rows_y // 2, rows_y), np.float32)
    down = np.zeros((deep, plane), np.float32)
    for table in (along, down):
        for element in range(table.shape[0]):
            for local, weight in enumerate((1, 4, 1)):
                table[element, (2 * element + local) % table.shape[1]] += weight
    first_y = np.zeros_like(along)
    first_z = np.zeros_like(down)
    first_y[np.arange(rows_y // 2), 2 * np.arange(rows_y // 2)] = 1
    first_z[np.arange(deep), 2 * np.arange(deep)] = 1
    full = [np.kron(along, down), np.kron(first_y, down), np.kron(along, first_z)]
    out = np.zeros((width, 3 * width), np.float32)
    out[: width // 4] = np.concatenate(full, 1)
    return out


def advance(plane, even, odd, heat_even, heat_odd, kappa, spread):
    rows, width = even.shape
    up = lambda v: pltpu.roll(v, rows - 1, 0)
    down = lambda v: pltpu.roll(v, 1, 0)
    turn = lambda v, by: pltpu.roll(v, by % width, 1)
    lane = lax.broadcasted_iota(jnp.int32, (rows, width), 1)
    row_y, deep = split_index(lane, plane)
    lines = jnp.dot(kappa, spread, precision=HIGHEST, preferred_element_type=jnp.float32)
    lines = lines * (1.0 / 108.0)
    along_x, along_y, along_z = (lines[:, i * width : (i + 1) * width] for i in range(3))
    y_even, y_odd = along_y + down(along_y), 4.0 * along_y
    z_even, z_odd = along_z + down(along_z), 4.0 * along_z
    inverse = 27.0 * jnp.where(row_y & 1 == 1, 0.5, 1.0) * jnp.where(deep & 1 == 1, 0.5, 1.0)
    scale_even, scale_odd = inverse, 0.5 * inverse

    def bend(first, second, third, coefficient):
        curve = (4.0 * coefficient) * (first - 2.0 * second + third)
        slope = (3.0 * coefficient) * (third - first)
        return curve - slope, -2.0 * curve, curve + slope

    def in_plane(values, along_y, along_z):
        a, b, c = bend(values, turn(values, -plane), turn(values, -2 * plane), along_y)
        result = a + turn(b, plane) + turn(c, 2 * plane)
        third = jnp.where(deep == plane - 2, turn(values, plane - 2), turn(values, -2))
        a, b, c = bend(values, turn(values, -1), third, along_z)
        return result + a + turn(b, 1) + jnp.where(deep == 0, turn(c, 2 - plane), turn(c, 2))

    def missing(v_even, v_odd):
        a, b, c = bend(v_even, v_odd, up(v_even), along_x)
        k_even = a + down(c) + in_plane(v_even, y_even, z_even)
        k_odd = b + in_plane(v_odd, y_odd, z_odd)
        return heat_even - k_even, heat_odd - k_odd

    one_even, one_odd = missing(even, odd)
    two_even, two_odd = missing(
        even + (STEP * scale_even) * one_even, odd + (STEP * scale_odd) * one_odd
    )
    return (
        even + (0.5 * STEP * scale_even) * (one_even + two_even),
        odd + (0.5 * STEP * scale_odd) * (one_odd + two_odd),
    )


def heat_kernel(plane, layers, first_row, state_ref, spread_ref, new_ref, even_ref, odd_ref):
    even, odd = advance(plane, *(state_ref[i] for i in range(5)), spread_ref[...])
    even_ref[...] = even
    odd_ref[...] = odd
    start = first_row()
    for layer in range(layers):
        new_ref[2 * layer : 2 * layer + 1, :] = even_ref[pl.ds(start + layer, 1), :]
        new_ref[2 * layer + 1 : 2 * layer + 2, :] = odd_ref[pl.ds(start + layer, 1), :]


def basis(step):
    point = (step.astype(jnp.float32) + 0.5) / CPC
    return (
        2.0 * (point - 0.5) * (point - 1.0),
        -4.0 * point * (point - 1.0),
        2.0 * point * (point - 0.5),
    )


def finish_kernel(
    plane, depth, flat, layers, first_row, cell_row, wraps,
    state_ref, spread_ref, weave_ref, packed_ref, edge_ref, behind_ref, ahead_ref,
    gathered_ref, nucleation_ref, frozen_ref, *refs,
):
    solid_ref, even_ref, odd_ref, side_ref, extra_ref = refs[-5:]
    edge_x, wide = frozen_ref.shape
    rows = state_ref.shape[1]
    even, odd = advance(plane, *(state_ref[i] for i in range(5)), spread_ref[...])
    if first_row is not None:
        new_ref = refs[0]
        even_ref[:, 0 : even.shape[1]] = even
        odd_ref[:, 0 : even.shape[1]] = odd
        start = first_row()
        for layer in range(layers):
            new_ref[2 * layer : 2 * layer + 1, :] = even_ref[pl.ds(start + layer, 1), 0 : even.shape[1]]
            new_ref[2 * layer + 1 : 2 * layer + 2, :] = odd_ref[pl.ds(start + layer, 1), 0 : even.shape[1]]
    side_ref[...] = jnp.zeros(side_ref.shape, jnp.float32)
    side_ref[0:depth, :] = behind_ref[...]
    side_ref[flat - depth : flat, :] = ahead_ref[...]
    extra_ref[...] = gathered_ref[...] + jnp.transpose(side_ref[...])
    for t in range(wide // LANES):
        lanes = slice(t * LANES, (t + 1) * LANES)
        rough = jnp.concatenate([edge_ref[:, lanes], jnp.zeros((4, LANES), jnp.float32)], 0)
        codes = pick_codes(packed_ref, rough.astype(jnp.int32))
        behind = rough[0:1] * level(codes[1:2], 1) * 0.25
        ahead = rough[2:3] * level(codes[3:4], 0) * 0.25
        extra_ref[0:1, lanes] += behind
        extra_ref[edge_x - 1 : edge_x, lanes] += ahead
    weave = weave_ref[...]
    even_ref[:, 0:wide] = jnp.dot(even, weave, precision=HIGHEST, preferred_element_type=jnp.float32)
    odd_ref[:, 0:wide] = jnp.dot(odd, weave, precision=HIGHEST, preferred_element_type=jnp.float32)
    first, middle, last = basis(lax.broadcasted_iota(jnp.int32, (CPC, wide), 0))
    base = cell_row()
    for a in range(edge_x // CPC):
        cells = slice(a * CPC, (a + 1) * CPC)
        later = base + (a + 1)
        if wraps:
            later = lax.rem(later, rows)
        temperature = (
            first * even_ref[pl.ds(base + a, 1), 0:wide]
            + middle * odd_ref[pl.ds(base + a, 1), 0:wide]
            + last * even_ref[pl.ds(later, 1), 0:wide]
        )
        under = jnp.maximum(-temperature, 0.0)
        rate = under * (under * extra_ref[cells, :] + nucleation_ref[cells, :])
        frozen = frozen_ref[cells, :]
        solid_ref[cells, :] = frozen + (1.0 - frozen) * (1.0 - jnp.exp(-rate))


def weave_table(width, plane, depth, edge_y, start_y, first_cell, rows_total):
    wide = up_to(edge_y * depth, LANES)
    node, cell = jnp.arange(width)[:, None], jnp.arange(wide)[None, :]
    cell_y, cell_z = first_cell + cell // depth, cell % depth
    step_y = jnp.remainder(start_y + node // plane - 2 * (cell_y // CPC), rows_total)
    step_z = jnp.remainder(node % plane - 2 * (cell_z // CPC), plane)
    take = lambda step, at: sum(jnp.where(step == i, v, 0.0) for i, v in enumerate(basis(at % CPC)))
    return jnp.where(cell < edge_y * depth, take(step_y, cell_y) * take(step_z, cell_z), 0.0)


def lines(values, width):
    flat = values.reshape(-1)
    return jnp.pad(flat, (0, -flat.shape[0] % width)).reshape(-1, width)


def body(
    thermal_state_values,
    thermal_kappa_values,
    nodal_heating_input,
    frozen_share_map,
    crystal_label_map,
    growth_reach_table,
    seed_site_slots,
    seed_crystal_label,
):
    groups, slabs = lax.axis_size("grp"), lax.axis_size("slab")
    devices = groups * slabs
    group, slab = lax.axis_index("grp"), lax.axis_index("slab")
    me = group * slabs + slab
    layers, elements = thermal_kappa_values.shape
    plane = 2 * HEX_COUNT_LATER
    depth = CPC * HEX_COUNT_LATER
    flat = thermal_state_values.shape[1]
    rows_y = flat // plane
    edge_x, flat_cells = frozen_share_map.shape
    edge_y = flat_cells // depth
    wide = up_to(flat_cells, LANES)
    all_layers = layers * devices

    def swapped(array, bit):
        return lax.ppermute(array, AXES, [(i, i ^ (1 << bit)) for i in range(devices)])

    def widened(array):
        return jnp.pad(array, ((0, 0), (0, wide - flat_cells)))

    unit = layers * flat
    held = jnp.concatenate(
        [
            jnp.swapaxes(thermal_state_values.reshape(layers, 2, flat), 0, 1).reshape(2, unit),
            jnp.swapaxes(nodal_heating_input.reshape(layers, 2, flat), 0, 1).reshape(2, unit),
            jnp.pad(thermal_kappa_values, ((0, 0), (0, flat - elements))).reshape(1, unit),
        ],
        0,
    )
    frozen, label = widened(frozen_share_map), widened(crystal_label_map)
    low_edge = jnp.stack([frozen[0], label[0].astype(jnp.float32)])
    high_edge = jnp.stack([frozen[-1], label[-1].astype(jnp.float32)])
    seeds = up_to(seed_site_slots.shape[0], LANES)
    short = seeds - seed_site_slots.shape[0]
    packed, gathered, nucleation, faces = pl.pallas_call(
        functools.partial(cells_kernel, depth, flat_cells),
        out_shape=(
            jax.ShapeDtypeStruct((up_to(growth_reach_table.shape[0], 2 * LANES) // (2 * LANES), LANES), jnp.int32),
            jax.ShapeDtypeStruct((edge_x, wide), jnp.float32),
            jax.ShapeDtypeStruct((edge_x, wide), jnp.float32),
            jax.ShapeDtypeStruct((2 * depth, edge_x), jnp.float32),
        ),
        in_specs=[VMEM] * 5,
        out_specs=[VMEM] * 4,
        scratch_shapes=[
            pltpu.VMEM((8, up_to(growth_reach_table.shape[0], 2 * LANES)), jnp.int32),
            pltpu.VMEM((edge_x, wide), jnp.int32),
        ],
        compiler_params=PARAMS,
        name="cells",
    )(
        growth_reach_table.T,
        label,
        frozen,
        jnp.pad(seed_site_slots, (0, short), constant_values=-1).reshape(-1, LANES),
        jnp.pad(seed_crystal_label, (0, short)).reshape(-1, LANES),
    )

    held = held[:, None]
    to_behind, to_ahead = faces[:depth], faces[depth:]
    behind = ahead = edges = None
    for bit in reversed(range(devices.bit_length() - 1)):
        sent = [lines(held, unit)]
        if groups == 2 and 1 << bit == slabs:
            sent.append(lines(jnp.concatenate([high_edge, low_edge]), unit))
        low = (1 << bit) - 1
        goes_on = (slab & low) == low
        if bit > 0 and 1 << bit < slabs:
            face = jnp.where(goes_on, to_ahead, to_behind)
            sent.append(lines(face, unit))
        if bit == 0:
            sent += [lines(to_ahead, unit), lines(to_behind, unit)]
        got = swapped(jnp.concatenate(sent, 0), bit)
        parts, at = [], 0
        for part in sent:
            parts.append(got[at : at + part.shape[0]])
            at += part.shape[0]
        theirs = parts[0].reshape(held.shape)
        upper = (me >> bit) & 1 == 1
        held = jnp.stack(
            [jnp.where(upper, theirs, held), jnp.where(upper, held, theirs)], 2
        ).reshape(held.shape[0], 2 * held.shape[1], unit)
        if groups == 2 and 1 << bit == slabs:
            edges = parts[1].reshape(-1)[: 4 * wide].reshape(4, wide)
        if bit > 0 and 1 << bit < slabs:
            face = parts[1].reshape(-1)[: depth * edge_x].reshape(depth, edge_x)
            to_ahead = jnp.where(goes_on, face, to_ahead)
            to_behind = jnp.where((slab & low) == 0, face, to_behind)
        if bit == 0:
            behind, ahead = (
                part.reshape(-1)[: depth * edge_x].reshape(depth, edge_x) for part in parts[1:]
            )
    if edges is None:
        ring = [(i, (i + 1) % groups) for i in range(groups)]
        edges = jnp.concatenate(
            [
                lax.ppermute(high_edge, "grp", ring),
                lax.ppermute(low_edge, "grp", [(j, i) for i, j in ring]),
            ]
        )
    held = held.reshape(5, all_layers, flat)

    def window(first_layer, need_layers, first_element, need_elements):
        rows, width = up_to(need_layers, 8), up_to(need_elements * 2 * plane, LANES)
        part, start_layer, start_y = held, 0, 0
        if 2 * rows <= all_layers:
            start_layer = first_layer
            part = lax.dynamic_slice_in_dim(
                jnp.concatenate([part, part[:, : rows]], 1),
                jnp.remainder(start_layer, all_layers), rows, 1,
            )
        if 2 * width <= flat:
            start_y = 2 * first_element
            shifted = lambda v, by, size: lax.dynamic_slice_in_dim(
                jnp.concatenate([v, v[..., :size]], -1), by, size, v.ndim - 1
            )
            start = jnp.remainder(first_element, rows_y // 2)
            part = jnp.concatenate(
                [
                    shifted(part[:4], start * 2 * plane, width),
                    jnp.pad(
                        shifted(part[4:, :, :elements], start * HEX_COUNT_LATER, width // 4),
                        ((0, 0), (0, 0), (0, width - width // 4)),
                    ),
                ],
                0,
            )
        return part, start_layer, start_y

    brick_layers = edge_x // CPC
    first_cell = slab * edge_y
    state, start_layer, start_y = window(
        group * brick_layers - 2,
        brick_layers + 5,
        first_cell // CPC - 2,
        (edge_y + CPC - 2) // CPC + 6,
    )
    width = state.shape[2]
    whole = state.shape == held.shape
    weave = weave_table(width, plane, depth, edge_y, start_y, first_cell, rows_y)

    def place(start, layer):
        if not isinstance(start, int):
            return lambda: 2
        return lambda: layer(lax.axis_index("grp"), lax.axis_index("slab"))

    own_layer = lambda g, s: (g * slabs + s) * layers
    cell_row = place(start_layer, lambda g, s: g * brick_layers)
    own_row = place(start_layer, own_layer)
    new_shape = jax.ShapeDtypeStruct((2 * layers, flat), jnp.float32)
    solid_shape = jax.ShapeDtypeStruct((edge_x, wide), jnp.float32)
    span = max(width, wide)
    results = pl.pallas_call(
        functools.partial(
            finish_kernel, plane, depth, flat_cells, layers,
            own_row if whole else None, cell_row, isinstance(start_layer, int),
        ),
        out_shape=(new_shape, solid_shape) if whole else (solid_shape,),
        in_specs=[VMEM] * 10,
        out_specs=(VMEM,) * (1 + whole),
        scratch_shapes=[
            pltpu.VMEM((state.shape[1], span), jnp.float32),
            pltpu.VMEM((state.shape[1], span), jnp.float32),
            pltpu.VMEM((wide, edge_x), jnp.float32),
            pltpu.VMEM((edge_x, wide), jnp.float32),
        ],
        compiler_params=PARAMS,
        name="finish",
    )(
        state, jnp.asarray(spread_tables(width, plane)), weave, packed, edges,
        behind, ahead, gathered, nucleation, frozen,
    )
    if whole:
        new_field, new_solid = results
    else:
        (new_solid,) = results
        state, start_layer, _ = window(me * layers - 2, layers + 4, 0, rows_y // 2)
        own_row = place(start_layer, own_layer)
        new_field = pl.pallas_call(
            functools.partial(heat_kernel, plane, layers, own_row),
            out_shape=new_shape,
            in_specs=[VMEM] * 2,
            out_specs=VMEM,
            scratch_shapes=[pltpu.VMEM(state.shape[1:], jnp.float32)] * 2,
            compiler_params=PARAMS,
            name="heat",
        )(state, jnp.asarray(spread_tables(flat, plane)))
    return new_field, new_solid[:, :flat_cells]


def solution(mesh):
    in_specs = (
        P(("grp", "slab"), None),
        P(("grp", "slab"), None),
        P(("grp", "slab"), None),
        P("grp", "slab"),
        P("grp", "slab"),
        P(),
        P(("grp", "slab")),
        P(("grp", "slab")),
    )
    out_specs = (P(("grp", "slab"), None), P("grp", "slab"))
    return jax.shard_map(body, mesh=mesh, in_specs=in_specs, out_specs=out_specs, check_vma=False)
```

```python
import functools

import jax
import jax.numpy as jnp
import numpy as np
from jax import lax
from jax.experimental import pallas as pl
from jax.experimental.pallas import tpu as pltpu
from jax.sharding import PartitionSpec as P

HEX_COUNT_LATER = 2
CPC = 8
LANES = 128
HIGHEST = lax.Precision.HIGHEST
STEP = 0.004
AXES = ("grp", "slab")
VMEM = pl.BlockSpec(memory_space=pltpu.VMEM)
HBM = pl.BlockSpec(memory_space=pltpu.HBM)
PARAMS = pltpu.CompilerParams(vmem_limit_bytes=48 * 1024 * 1024)


def up_to(value, unit):
    return -(-value // unit) * unit


def split_index(value, by):
    if by & (by - 1) == 0:
        return value >> (by.bit_length() - 1), value & (by - 1)
    quotient = lax.div(value, jnp.full_like(value, by))
    return quotient, value - quotient * by


def pack_kernel(
    state_ref, heat_ref, kappa_ref, frozen_ref, label_ref, held_ref, edge_ref,
    state, heat, kappa, frozen, label, sems,
):
    layers, elements = kappa.shape
    flat = state.shape[1]
    edge_x = frozen_ref.shape[0]
    top, bottom = pl.ds(0, 8), pl.ds(edge_x - 8, 8)
    copies = [
        pltpu.make_async_copy(source, target, sems.at[i])
        for i, (source, target) in enumerate(
            [
                (state_ref, state),
                (heat_ref, heat),
                (kappa_ref, kappa),
                (frozen_ref.at[top, :], frozen.at[0]),
                (frozen_ref.at[bottom, :], frozen.at[1]),
                (label_ref.at[top, :], label.at[0]),
                (label_ref.at[bottom, :], label.at[1]),
            ]
        )
    ]
    for copy in copies:
        copy.start()
    held_ref[4:5, :] = jnp.zeros((1, held_ref.shape[1]), jnp.float32)
    for copy in copies:
        copy.wait()
    for layer in range(layers):
        lanes = slice(layer * flat, (layer + 1) * flat)
        for parity in range(2):
            row = slice(2 * layer + parity, 2 * layer + parity + 1)
            held_ref[parity : parity + 1, lanes] = state[row, :]
            held_ref[2 + parity : 3 + parity, lanes] = heat[row, :]
        held_ref[4:5, layer * flat : layer * flat + elements] = kappa[layer : layer + 1, :]
    edge_ref[0:1, :] = frozen[1, 7:8, :]
    edge_ref[1:2, :] = label[1, 7:8, :].astype(jnp.float32)
    edge_ref[2:3, :] = frozen[0, 0:1, :]
    edge_ref[3:4, :] = label[0, 0:1, :].astype(jnp.float32)


def pick_codes(table_ref, labels):
    half = table_ref.shape[0]
    tile, lane = labels >> 7, labels & (LANES - 1)
    upper = tile >= half
    row = jnp.where(upper, tile - half, tile)
    found = jnp.zeros(labels.shape, jnp.int32)
    for r in range(half):
        line = jnp.broadcast_to(table_ref[r : r + 1, :], labels.shape)
        here = jnp.take_along_axis(line, lane, axis=1, mode="promise_in_bounds")
        found = jnp.where(row == r, here, found)
    return jnp.where(upper, found >> 12, found) & 4095


def level(code, direction):
    return (((code >> (2 * direction)) & 3) + 1).astype(jnp.float32)


def cells_kernel(
    depth, flat, table_hbm, label_hbm, frozen_hbm, slot_hbm, seed_hbm, spread_hbm,
    packed_ref, gathered_ref, nucleation_ref, faces_ref, frozen_ref, spread_ref,
    line_ref, code_ref, table_ref, label_ref, slot_ref, seed_ref, sems,
):
    get_table, get_label, get_frozen, get_slot, get_seed, get_spread = [
        pltpu.make_async_copy(source, target, sems.at[i])
        for i, (source, target) in enumerate(
            [
                (table_hbm, table_ref),
                (label_hbm, label_ref),
                (frozen_hbm, frozen_ref),
                (slot_hbm, slot_ref),
                (seed_hbm, seed_ref),
                (spread_hbm, spread_ref),
            ]
        )
    ]
    for copy in (get_table, get_label, get_frozen, get_slot, get_seed, get_spread):
        copy.start()
    count = table_ref.shape[1]
    half = packed_ref.shape[0]
    edge_x, wide = frozen_ref.shape
    place = lax.broadcasted_iota(jnp.int32, table_ref.shape, 0)
    line_ref[...] = jnp.zeros(line_ref.shape, jnp.int32)
    get_table.wait()
    word = jnp.sum((table_ref[...] - 1) << (2 * place), axis=0, keepdims=True)
    line_ref[0:1, 0:count] = word
    for r in range(half):
        low = line_ref[0:1, r * LANES : (r + 1) * LANES]
        high = line_ref[0:1, (r + half) * LANES : (r + half + 1) * LANES]
        packed_ref[r : r + 1, :] = low | (high << 12)

    def look_up(chunk, carry):
        rows = pl.ds(pl.multiple_of(chunk * 8, 8), 8)
        for t in range(wide // LANES):
            lanes = pl.ds(t * LANES, LANES)
            code_ref[rows, lanes] = pick_codes(packed_ref, label_ref[rows, lanes])
        return carry

    get_label.wait()
    lax.fori_loop(0, edge_x // 8, look_up, 0, unroll=4)
    get_frozen.wait()
    frozen = frozen_ref[...] * 0.25
    code = code_ref[...]
    shares = [frozen * level(code, d) for d in range(6)]
    line_x = lax.broadcasted_iota(jnp.int32, (edge_x, wide), 0)
    lane = lax.broadcasted_iota(jnp.int32, (edge_x, wide), 1)
    deep = lane % depth if depth & (depth - 1) else lane & (depth - 1)
    total = jnp.where(line_x == edge_x - 1, 0.0, pltpu.roll(shares[0], edge_x - 1, 0))
    total += jnp.where(line_x == 0, 0.0, pltpu.roll(shares[1], 1, 0))
    total += jnp.where(lane >= flat - depth, 0.0, pltpu.roll(shares[2], wide - depth, 1))
    total += jnp.where(lane < depth, 0.0, pltpu.roll(shares[3], depth, 1))
    total += jnp.where(
        deep == depth - 1, pltpu.roll(shares[4], depth - 1, 1), pltpu.roll(shares[4], wide - 1, 1)
    )
    total += jnp.where(
        deep == 0, pltpu.roll(shares[5], wide - (depth - 1), 1), pltpu.roll(shares[5], 1, 1)
    )
    gathered_ref[...] = total
    sides = jnp.transpose(jnp.where(lane < depth, shares[2], shares[3]))
    faces_ref[0:depth, :] = sides[0:depth]
    faces_ref[depth : 2 * depth, :] = sides[flat - depth : flat]
    for copy in (get_slot, get_seed, get_spread):
        copy.wait()
    sites = seed_ref.shape[0]
    codes = pick_codes(packed_ref, seed_ref[...])
    worth = sum(level(codes, d) for d in range(6))
    site_x, site_lane = split_index(slot_ref[...], flat)
    at_x = lax.broadcasted_iota(jnp.int32, (edge_x, LANES), 0)
    at_lane = lax.broadcasted_iota(jnp.int32, (wide, LANES), 0)
    added = jnp.zeros((edge_x, wide), jnp.float32)
    for r in range(sites):
        left = jnp.where(at_x == site_x[r : r + 1], worth[r : r + 1], 0.0).astype(jnp.bfloat16)
        right = jnp.where(at_lane == site_lane[r : r + 1], 1.0, 0.0).astype(jnp.bfloat16)
        added += lax.dot_general(
            left, right, (((1,), (1,)), ((), ())), preferred_element_type=jnp.float32
        )
    nucleation_ref[...] = added * (1.0 / 6.0)


def spread_tables(width, plane):
    rows_y, deep = width // plane, plane // 2
    along = np.zeros((rows_y // 2, rows_y), np.float32)
    down = np.zeros((deep, plane), np.float32)
    for table in (along, down):
        for element in range(table.shape[0]):
            for local, weight in enumerate((1, 4, 1)):
                table[element, (2 * element + local) % table.shape[1]] += weight
    first_y = np.zeros_like(along)
    first_z = np.zeros_like(down)
    first_y[np.arange(rows_y // 2), 2 * np.arange(rows_y // 2)] = 1
    first_z[np.arange(deep), 2 * np.arange(deep)] = 1
    full = [np.kron(along, down), np.kron(first_y, down), np.kron(along, first_z)]
    out = np.zeros((width, 3 * width), np.float32)
    out[: width // 4] = np.concatenate(full, 1)
    return out


def advance(plane, even, odd, heat_even, heat_odd, kappa, spread):
    rows, width = even.shape
    up = lambda v: pltpu.roll(v, rows - 1, 0)
    down = lambda v: pltpu.roll(v, 1, 0)
    turn = lambda v, by: pltpu.roll(v, by % width, 1)
    lane = lax.broadcasted_iota(jnp.int32, (rows, width), 1)
    row_y, deep = split_index(lane, plane)
    lines = jnp.dot(kappa, spread, precision=HIGHEST, preferred_element_type=jnp.float32)
    lines = lines * (1.0 / 108.0)
    along_x, along_y, along_z = (lines[:, i * width : (i + 1) * width] for i in range(3))
    y_even, y_odd = along_y + down(along_y), 4.0 * along_y
    z_even, z_odd = along_z + down(along_z), 4.0 * along_z
    inverse = 27.0 * jnp.where(row_y & 1 == 1, 0.5, 1.0) * jnp.where(deep & 1 == 1, 0.5, 1.0)
    scale_even, scale_odd = inverse, 0.5 * inverse

    def bend(first, second, third, coefficient):
        curve = (4.0 * coefficient) * (first - 2.0 * second + third)
        slope = (3.0 * coefficient) * (third - first)
        return curve - slope, -2.0 * curve, curve + slope

    def in_plane(values, along_y, along_z):
        a, b, c = bend(values, turn(values, -plane), turn(values, -2 * plane), along_y)
        result = a + turn(b, plane) + turn(c, 2 * plane)
        third = jnp.where(deep == plane - 2, turn(values, plane - 2), turn(values, -2))
        a, b, c = bend(values, turn(values, -1), third, along_z)
        return result + a + turn(b, 1) + jnp.where(deep == 0, turn(c, 2 - plane), turn(c, 2))

    def missing(v_even, v_odd):
        a, b, c = bend(v_even, v_odd, up(v_even), along_x)
        k_even = a + down(c) + in_plane(v_even, y_even, z_even)
        k_odd = b + in_plane(v_odd, y_odd, z_odd)
        return heat_even - k_even, heat_odd - k_odd

    one_even, one_odd = missing(even, odd)
    two_even, two_odd = missing(
        even + (STEP * scale_even) * one_even, odd + (STEP * scale_odd) * one_odd
    )
    return (
        even + (0.5 * STEP * scale_even) * (one_even + two_even),
        odd + (0.5 * STEP * scale_odd) * (one_odd + two_odd),
    )


def heat_kernel(plane, layers, first_row, state_ref, spread_ref, new_ref, even_ref, odd_ref):
    even, odd = advance(plane, *(state_ref[i] for i in range(5)), spread_ref[...])
    even_ref[...] = even
    odd_ref[...] = odd
    start = first_row()
    for layer in range(layers):
        new_ref[2 * layer : 2 * layer + 1, :] = even_ref[pl.ds(start + layer, 1), :]
        new_ref[2 * layer + 1 : 2 * layer + 2, :] = odd_ref[pl.ds(start + layer, 1), :]


def basis(step):
    point = (step.astype(jnp.float32) + 0.5) / CPC
    return (
        2.0 * (point - 0.5) * (point - 1.0),
        -4.0 * point * (point - 1.0),
        2.0 * point * (point - 0.5),
    )


def finish_kernel(
    plane, depth, flat, layers, first_row, cell_row, wraps,
    state_ref, spread_ref, weave_ref, packed_ref, edge_ref, behind_ref, ahead_ref,
    gathered_ref, nucleation_ref, frozen_ref, *refs,
):
    solid_ref, even_ref, odd_ref, side_ref, extra_ref = refs[-5:]
    edge_x, wide = frozen_ref.shape
    rows = state_ref.shape[1]
    even, odd = advance(plane, *(state_ref[i] for i in range(5)), spread_ref[...])
    if first_row is not None:
        new_ref = refs[0]
        even_ref[:, 0 : even.shape[1]] = even
        odd_ref[:, 0 : even.shape[1]] = odd
        start = first_row()
        for layer in range(layers):
            new_ref[2 * layer : 2 * layer + 1, :] = even_ref[pl.ds(start + layer, 1), 0 : even.shape[1]]
            new_ref[2 * layer + 1 : 2 * layer + 2, :] = odd_ref[pl.ds(start + layer, 1), 0 : even.shape[1]]
    side_ref[...] = jnp.zeros(side_ref.shape, jnp.float32)
    side_ref[0:depth, :] = behind_ref[...]
    side_ref[flat - depth : flat, :] = ahead_ref[...]
    extra_ref[...] = gathered_ref[...] + jnp.transpose(side_ref[...])
    for t in range(wide // LANES):
        lanes = slice(t * LANES, (t + 1) * LANES)
        rough = jnp.concatenate([edge_ref[:, lanes], jnp.zeros((4, LANES), jnp.float32)], 0)
        codes = pick_codes(packed_ref, rough.astype(jnp.int32))
        behind = rough[0:1] * level(codes[1:2], 1) * 0.25
        ahead = rough[2:3] * level(codes[3:4], 0) * 0.25
        extra_ref[0:1, lanes] += behind
        extra_ref[edge_x - 1 : edge_x, lanes] += ahead
    weave = weave_ref[...]
    even_ref[:, 0:wide] = jnp.dot(even, weave, precision=HIGHEST, preferred_element_type=jnp.float32)
    odd_ref[:, 0:wide] = jnp.dot(odd, weave, precision=HIGHEST, preferred_element_type=jnp.float32)
    first, middle, last = basis(lax.broadcasted_iota(jnp.int32, (CPC, wide), 0))
    base = cell_row()
    for a in range(edge_x // CPC):
        cells = slice(a * CPC, (a + 1) * CPC)
        later = base + (a + 1)
        if wraps:
            later = lax.rem(later, rows)
        temperature = (
            first * even_ref[pl.ds(base + a, 1), 0:wide]
            + middle * odd_ref[pl.ds(base + a, 1), 0:wide]
            + last * even_ref[pl.ds(later, 1), 0:wide]
        )
        under = jnp.maximum(-temperature, 0.0)
        rate = under * (under * extra_ref[cells, :] + nucleation_ref[cells, :])
        frozen = frozen_ref[cells, :]
        solid_ref[cells, :] = frozen + (1.0 - frozen) * (1.0 - jnp.exp(-rate))


def weave_table(width, plane, depth, edge_y, start_y, first_cell, rows_total):
    wide = up_to(edge_y * depth, LANES)
    node, cell = jnp.arange(width)[:, None], jnp.arange(wide)[None, :]
    cell_y, cell_z = first_cell + cell // depth, cell % depth
    step_y = jnp.remainder(start_y + node // plane - 2 * (cell_y // CPC), rows_total)
    step_z = jnp.remainder(node % plane - 2 * (cell_z // CPC), plane)
    take = lambda step, at: sum(jnp.where(step == i, v, 0.0) for i, v in enumerate(basis(at % CPC)))
    return jnp.where(cell < edge_y * depth, take(step_y, cell_y) * take(step_z, cell_z), 0.0)


def lines(values, width):
    flat = values.reshape(-1)
    return jnp.pad(flat, (0, -flat.shape[0] % width)).reshape(-1, width)


def body(
    thermal_state_values,
    thermal_kappa_values,
    nodal_heating_input,
    frozen_share_map,
    crystal_label_map,
    growth_reach_table,
    seed_site_slots,
    seed_crystal_label,
):
    groups, slabs = lax.axis_size("grp"), lax.axis_size("slab")
    devices = groups * slabs
    group, slab = lax.axis_index("grp"), lax.axis_index("slab")
    me = group * slabs + slab
    layers, elements = thermal_kappa_values.shape
    plane = 2 * HEX_COUNT_LATER
    depth = CPC * HEX_COUNT_LATER
    flat = thermal_state_values.shape[1]
    rows_y = flat // plane
    edge_x, flat_cells = frozen_share_map.shape
    edge_y = flat_cells // depth
    wide = up_to(flat_cells, LANES)
    all_layers = layers * devices

    def exchanged(parts, flips):
        sizes = np.cumsum([part.shape[0] for part in parts])
        pairs = [(i, i ^ flips) for i in range(devices)]
        got = lax.ppermute(jnp.concatenate(parts, 0), AXES, pairs)
        return [got[end - part.shape[0] : end] for part, end in zip(parts, sizes)]

    def widened(array):
        return jnp.pad(array, ((0, 0), (0, wide - flat_cells)))

    unit = layers * flat
    count = growth_reach_table.shape[0]
    frozen, label = widened(frozen_share_map), widened(crystal_label_map)
    held, edge_rows = pl.pallas_call(
        pack_kernel,
        out_shape=(
            jax.ShapeDtypeStruct((5, unit), jnp.float32),
            jax.ShapeDtypeStruct((4, wide), jnp.float32),
        ),
        in_specs=[HBM] * 5,
        out_specs=(VMEM, VMEM),
        scratch_shapes=[
            pltpu.VMEM(thermal_state_values.shape, jnp.float32),
            pltpu.VMEM(nodal_heating_input.shape, jnp.float32),
            pltpu.VMEM(thermal_kappa_values.shape, jnp.float32),
            pltpu.VMEM((2, 8, wide), jnp.float32),
            pltpu.VMEM((2, 8, wide), jnp.int32),
            pltpu.SemaphoreType.DMA((7,)),
        ],
        compiler_params=PARAMS,
        name="pack",
    )(thermal_state_values, nodal_heating_input, thermal_kappa_values, frozen, label)
    high_edge, low_edge = edge_rows[:2], edge_rows[2:]

    brick_layers = edge_x // CPC
    need_y = (edge_y + CPC - 2) // CPC + 6
    width = up_to(need_y * 2 * plane, LANES)
    if 2 * width > flat:
        width = flat
    seeds = up_to(seed_site_slots.shape[0], LANES)
    short = seeds - seed_site_slots.shape[0]
    table_lanes = up_to(count, 2 * LANES)
    packed, gathered, nucleation, faces, frozen, spread = pl.pallas_call(
        functools.partial(cells_kernel, depth, flat_cells),
        out_shape=(
            jax.ShapeDtypeStruct((table_lanes // (2 * LANES), LANES), jnp.int32),
            jax.ShapeDtypeStruct((edge_x, wide), jnp.float32),
            jax.ShapeDtypeStruct((edge_x, wide), jnp.float32),
            jax.ShapeDtypeStruct((2 * depth, edge_x), jnp.float32),
            jax.ShapeDtypeStruct((edge_x, wide), jnp.float32),
            jax.ShapeDtypeStruct((width, 3 * width), jnp.float32),
        ),
        in_specs=[HBM] * 6,
        out_specs=[VMEM] * 6,
        scratch_shapes=[
            pltpu.VMEM((8, table_lanes), jnp.int32),
            pltpu.VMEM((edge_x, wide), jnp.int32),
            pltpu.VMEM((growth_reach_table.shape[1], count), jnp.int32),
            pltpu.VMEM((edge_x, wide), jnp.int32),
            pltpu.VMEM((seeds // LANES, LANES), jnp.int32),
            pltpu.VMEM((seeds // LANES, LANES), jnp.int32),
            pltpu.SemaphoreType.DMA((6,)),
        ],
        compiler_params=PARAMS,
        name="cells",
    )(
        growth_reach_table.T,
        label,
        frozen,
        jnp.pad(seed_site_slots, (0, short), constant_values=-1).reshape(-1, LANES),
        jnp.pad(seed_crystal_label, (0, short)).reshape(-1, LANES),
        jnp.asarray(spread_tables(width, plane)),
    )

    core, pair = me & 1, slab >> 1
    to_behind, to_ahead = faces[:depth], faces[depth:]
    onward = jnp.where(core == 1, to_ahead, 0.0)
    backward = jnp.where(core == 0, to_behind, 0.0)
    held, edges = held[:, None], None
    as_face = lambda part: part.reshape(-1)[: depth * edge_x].reshape(depth, edge_x)
    for bit in reversed(range(1, devices.bit_length() - 1)):
        sent = [lines(held, unit)]
        rides = 1 << bit < slabs
        low = (1 << (bit - 1)) - 1
        moves_on, moves_back = (pair & low) == low, (pair & low) == 0
        if groups == 2 and 1 << bit == slabs:
            sent.append(lines(edge_rows, unit))
        elif rides and low:
            sent.append(lines(jnp.where(moves_on, onward, backward), unit))
        elif rides:
            sent += [lines(onward, unit), lines(backward, unit)]
        theirs, *parts = exchanged(sent, (1 << bit) | 1)
        theirs = theirs.reshape(held.shape)
        upper = (me >> bit) & 1 == 1
        held = jnp.stack(
            [jnp.where(upper, theirs, held), jnp.where(upper, held, theirs)], 2
        ).reshape(held.shape[0], 2 * held.shape[1], unit)
        if groups == 2 and 1 << bit == slabs:
            edges = parts[0].reshape(-1)[: 4 * wide].reshape(4, wide)
        elif rides and low:
            onward = jnp.where(moves_on, as_face(parts[0]), onward)
            backward = jnp.where(moves_back, as_face(parts[0]), backward)
        elif rides:
            onward, backward = as_face(parts[0]), as_face(parts[1])
    across = jnp.where(core == 0, to_ahead, to_behind)
    passing = jnp.where(core == 1, onward, backward)
    sent = [lines(held, unit), lines(across, unit), lines(passing, unit)]
    if edges is not None:
        sent.append(lines(edges, unit))
    theirs, *parts = exchanged(sent, 1)
    across = as_face(parts[0])
    passing = as_face(parts[1]) + jnp.where(core == 0, onward, backward)
    behind = jnp.where(core == 0, passing, across)
    ahead = jnp.where(core == 0, across, passing)
    if edges is not None:
        edges = parts[2].reshape(-1)[: 4 * wide].reshape(4, wide)
    odd_count = np.array([bin(i).count("1") & 1 for i in range(devices // 2)], np.int32)
    mine = sum((me >> bit) & 1 for bit in range(devices.bit_length() - 1)) & 1
    even_first = (jnp.asarray(odd_count) == mine)[None, :, None]
    theirs = theirs.reshape(held.shape)
    held = jnp.stack(
        [jnp.where(even_first, held, theirs), jnp.where(even_first, theirs, held)], 2
    )
    if edges is None:
        ring = [(i, (i + 1) % groups) for i in range(groups)]
        edges = jnp.concatenate(
            [
                lax.ppermute(high_edge, "grp", ring),
                lax.ppermute(low_edge, "grp", [(j, i) for i, j in ring]),
            ]
        )
    held = held.reshape(5, all_layers, flat)

    def window(first_layer, need_layers, first_element, need_elements):
        rows, width = up_to(need_layers, 8), up_to(need_elements * 2 * plane, LANES)
        part, start_layer, start_y = held, 0, 0
        if 2 * rows <= all_layers:
            start_layer = first_layer
            part = lax.dynamic_slice_in_dim(
                jnp.concatenate([part, part[:, : rows]], 1),
                jnp.remainder(start_layer, all_layers), rows, 1,
            )
        if 2 * width <= flat:
            start_y = 2 * first_element
            shifted = lambda v, by, size: lax.dynamic_slice_in_dim(
                jnp.concatenate([v, v[..., :size]], -1), by, size, v.ndim - 1
            )
            start = jnp.remainder(first_element, rows_y // 2)
            part = jnp.concatenate(
                [
                    shifted(part[:4], start * 2 * plane, width),
                    jnp.pad(
                        shifted(part[4:, :, :elements], start * HEX_COUNT_LATER, width // 4),
                        ((0, 0), (0, 0), (0, width - width // 4)),
                    ),
                ],
                0,
            )
        return part, start_layer, start_y

    first_cell = slab * edge_y
    state, start_layer, start_y = window(
        group * brick_layers - 2,
        brick_layers + 5,
        first_cell // CPC - 2,
        need_y,
    )
    whole = state.shape == held.shape
    weave = weave_table(width, plane, depth, edge_y, start_y, first_cell, rows_y)

    def place(start, layer):
        if not isinstance(start, int):
            return lambda: 2
        return lambda: layer(lax.axis_index("grp"), lax.axis_index("slab"))

    own_layer = lambda g, s: (g * slabs + s) * layers
    cell_row = place(start_layer, lambda g, s: g * brick_layers)
    own_row = place(start_layer, own_layer)
    new_shape = jax.ShapeDtypeStruct((2 * layers, flat), jnp.float32)
    solid_shape = jax.ShapeDtypeStruct((edge_x, wide), jnp.float32)
    span = max(width, wide)
    results = pl.pallas_call(
        functools.partial(
            finish_kernel, plane, depth, flat_cells, layers,
            own_row if whole else None, cell_row, isinstance(start_layer, int),
        ),
        out_shape=(new_shape, solid_shape) if whole else (solid_shape,),
        in_specs=[VMEM] * 10,
        out_specs=(VMEM,) * (1 + whole),
        scratch_shapes=[
            pltpu.VMEM((state.shape[1], span), jnp.float32),
            pltpu.VMEM((state.shape[1], span), jnp.float32),
            pltpu.VMEM((wide, edge_x), jnp.float32),
            pltpu.VMEM((edge_x, wide), jnp.float32),
        ],
        compiler_params=PARAMS,
        name="finish",
    )(
        state, spread, weave, packed, edges,
        behind, ahead, gathered, nucleation, frozen,
    )
    if whole:
        new_field, new_solid = results
    else:
        (new_solid,) = results
        state, start_layer, _ = window(me * layers - 2, layers + 4, 0, rows_y // 2)
        own_row = place(start_layer, own_layer)
        new_field = pl.pallas_call(
            functools.partial(heat_kernel, plane, layers, own_row),
            out_shape=new_shape,
            in_specs=[VMEM] * 2,
            out_specs=VMEM,
            scratch_shapes=[pltpu.VMEM(state.shape[1:], jnp.float32)] * 2,
            compiler_params=PARAMS,
            name="heat",
        )(state, jnp.asarray(spread_tables(flat, plane)))
    return new_field, new_solid[:, :flat_cells]


def solution(mesh):
    in_specs = (
        P(("grp", "slab"), None),
        P(("grp", "slab"), None),
        P(("grp", "slab"), None),
        P("grp", "slab"),
        P("grp", "slab"),
        P(),
        P(("grp", "slab")),
        P(("grp", "slab")),
    )
    out_specs = (P(("grp", "slab"), None), P("grp", "slab"))
    return jax.shard_map(body, mesh=mesh, in_specs=in_specs, out_specs=out_specs, check_vma=False)
```

```python
import functools

import jax
import jax.numpy as jnp
import numpy as np
from jax import lax
from jax.experimental import pallas as pl
from jax.experimental.pallas import tpu as pltpu
from jax.sharding import PartitionSpec as P

HEX_COUNT_LATER = 2
CPC = 8
LANES = 128
HIGHEST = lax.Precision.HIGHEST
STEP = 0.004
AXES = ("grp", "slab")
VMEM = pl.BlockSpec(memory_space=pltpu.VMEM)
HBM = pl.BlockSpec(memory_space=pltpu.HBM)
PARAMS = pltpu.CompilerParams(vmem_limit_bytes=48 * 1024 * 1024)


def in_hbm(array):
    return pltpu.with_memory_space_constraint(array, pltpu.HBM)


def up_to(value, unit):
    return -(-value // unit) * unit


def split_index(value, by):
    if by & (by - 1) == 0:
        return value >> (by.bit_length() - 1), value & (by - 1)
    quotient = lax.div(value, jnp.full_like(value, by))
    return quotient, value - quotient * by


def pack_kernel(
    state_ref, heat_ref, kappa_ref, frozen_ref, label_ref, held_ref, edge_ref,
    state, heat, kappa, frozen, label, sems,
):
    layers, elements = kappa.shape
    flat = state.shape[1]
    edge_x = frozen_ref.shape[0]
    top, bottom = pl.ds(0, 8), pl.ds(edge_x - 8, 8)
    copies = [
        pltpu.make_async_copy(source, target, sems.at[i])
        for i, (source, target) in enumerate(
            [
                (state_ref, state),
                (heat_ref, heat),
                (kappa_ref, kappa),
                (frozen_ref.at[top, :], frozen.at[0]),
                (frozen_ref.at[bottom, :], frozen.at[1]),
                (label_ref.at[top, :], label.at[0]),
                (label_ref.at[bottom, :], label.at[1]),
            ]
        )
    ]
    for copy in copies:
        copy.start()
    held_ref[4:5, :] = jnp.zeros((1, held_ref.shape[1]), jnp.float32)
    for copy in copies:
        copy.wait()
    for layer in range(layers):
        lanes = slice(layer * flat, (layer + 1) * flat)
        for parity in range(2):
            row = slice(2 * layer + parity, 2 * layer + parity + 1)
            held_ref[parity : parity + 1, lanes] = state[row, :]
            held_ref[2 + parity : 3 + parity, lanes] = heat[row, :]
        held_ref[4:5, layer * flat : layer * flat + elements] = kappa[layer : layer + 1, :]
    edge_ref[0:1, :] = frozen[1, 7:8, :]
    edge_ref[1:2, :] = label[1, 7:8, :].astype(jnp.float32)
    edge_ref[2:3, :] = frozen[0, 0:1, :]
    edge_ref[3:4, :] = label[0, 0:1, :].astype(jnp.float32)


def pick_codes(table_ref, labels):
    half = table_ref.shape[0]
    tile, lane = labels >> 7, labels & (LANES - 1)
    upper = tile >= half
    row = jnp.where(upper, tile - half, tile)
    found = jnp.zeros(labels.shape, jnp.int32)
    for r in range(half):
        line = jnp.broadcast_to(table_ref[r : r + 1, :], labels.shape)
        here = jnp.take_along_axis(line, lane, axis=1, mode="promise_in_bounds")
        found = jnp.where(row == r, here, found)
    return jnp.where(upper, found >> 12, found) & 4095


def level(code, direction):
    return (((code >> (2 * direction)) & 3) + 1).astype(jnp.float32)


def cells_kernel(
    depth, flat, table_hbm, label_hbm, frozen_hbm, slot_hbm, seed_hbm, spread_hbm,
    packed_ref, gathered_ref, nucleation_ref, faces_ref, frozen_ref, spread_ref,
    line_ref, code_ref, table_ref, label_ref, slot_ref, seed_ref, sems,
):
    get_table, get_label, get_frozen, get_slot, get_seed, get_spread = [
        pltpu.make_async_copy(source, target, sems.at[i])
        for i, (source, target) in enumerate(
            [
                (table_hbm, table_ref),
                (label_hbm, label_ref),
                (frozen_hbm, frozen_ref),
                (slot_hbm, slot_ref),
                (seed_hbm, seed_ref),
                (spread_hbm, spread_ref),
            ]
        )
    ]
    for copy in (get_table, get_label, get_frozen, get_slot, get_seed, get_spread):
        copy.start()
    count = table_ref.shape[1]
    half = packed_ref.shape[0]
    edge_x, wide = frozen_ref.shape
    place = lax.broadcasted_iota(jnp.int32, table_ref.shape, 0)
    line_ref[...] = jnp.zeros(line_ref.shape, jnp.int32)
    get_table.wait()
    word = jnp.sum((table_ref[...] - 1) << (2 * place), axis=0, keepdims=True)
    line_ref[0:1, 0:count] = word
    for r in range(half):
        low = line_ref[0:1, r * LANES : (r + 1) * LANES]
        high = line_ref[0:1, (r + half) * LANES : (r + half + 1) * LANES]
        packed_ref[r : r + 1, :] = low | (high << 12)

    def look_up(chunk, carry):
        rows = pl.ds(pl.multiple_of(chunk * 8, 8), 8)
        for t in range(wide // LANES):
            lanes = pl.ds(t * LANES, LANES)
            code_ref[rows, lanes] = pick_codes(packed_ref, label_ref[rows, lanes])
        return carry

    get_label.wait()
    lax.fori_loop(0, edge_x // 8, look_up, 0, unroll=4)
    get_frozen.wait()
    frozen = frozen_ref[...] * 0.25
    code = code_ref[...]
    shares = [frozen * level(code, d) for d in range(6)]
    line_x = lax.broadcasted_iota(jnp.int32, (edge_x, wide), 0)
    lane = lax.broadcasted_iota(jnp.int32, (edge_x, wide), 1)
    deep = lane % depth if depth & (depth - 1) else lane & (depth - 1)
    total = jnp.where(line_x == edge_x - 1, 0.0, pltpu.roll(shares[0], edge_x - 1, 0))
    total += jnp.where(line_x == 0, 0.0, pltpu.roll(shares[1], 1, 0))
    total += jnp.where(lane >= flat - depth, 0.0, pltpu.roll(shares[2], wide - depth, 1))
    total += jnp.where(lane < depth, 0.0, pltpu.roll(shares[3], depth, 1))
    total += jnp.where(
        deep == depth - 1, pltpu.roll(shares[4], depth - 1, 1), pltpu.roll(shares[4], wide - 1, 1)
    )
    total += jnp.where(
        deep == 0, pltpu.roll(shares[5], wide - (depth - 1), 1), pltpu.roll(shares[5], 1, 1)
    )
    gathered_ref[...] = total
    sides = jnp.transpose(jnp.where(lane < depth, shares[2], shares[3]))
    faces_ref[0:depth, :] = sides[0:depth]
    faces_ref[depth : 2 * depth, :] = sides[flat - depth : flat]
    for copy in (get_slot, get_seed, get_spread):
        copy.wait()
    sites = seed_ref.shape[0]
    codes = pick_codes(packed_ref, seed_ref[...])
    worth = sum(level(codes, d) for d in range(6))
    site_x, site_lane = split_index(slot_ref[...], flat)
    at_x = lax.broadcasted_iota(jnp.int32, (edge_x, LANES), 0)
    at_lane = lax.broadcasted_iota(jnp.int32, (wide, LANES), 0)
    added = jnp.zeros((edge_x, wide), jnp.float32)
    for r in range(sites):
        left = jnp.where(at_x == site_x[r : r + 1], worth[r : r + 1], 0.0).astype(jnp.bfloat16)
        right = jnp.where(at_lane == site_lane[r : r + 1], 1.0, 0.0).astype(jnp.bfloat16)
        added += lax.dot_general(
            left, right, (((1,), (1,)), ((), ())), preferred_element_type=jnp.float32
        )
    nucleation_ref[...] = added * (1.0 / 6.0)


def spread_tables(width, plane):
    rows_y, deep = width // plane, plane // 2
    along = np.zeros((rows_y // 2, rows_y), np.float32)
    down = np.zeros((deep, plane), np.float32)
    for table in (along, down):
        for element in range(table.shape[0]):
            for local, weight in enumerate((1, 4, 1)):
                table[element, (2 * element + local) % table.shape[1]] += weight
    first_y = np.zeros_like(along)
    first_z = np.zeros_like(down)
    first_y[np.arange(rows_y // 2), 2 * np.arange(rows_y // 2)] = 1
    first_z[np.arange(deep), 2 * np.arange(deep)] = 1
    full = [np.kron(along, down), np.kron(first_y, down), np.kron(along, first_z)]
    out = np.zeros((width, 3 * width), np.float32)
    out[: width // 4] = np.concatenate(full, 1)
    return out


def advance(plane, even, odd, heat_even, heat_odd, kappa, spread):
    rows, width = even.shape
    up = lambda v: pltpu.roll(v, rows - 1, 0)
    down = lambda v: pltpu.roll(v, 1, 0)
    turn = lambda v, by: pltpu.roll(v, by % width, 1)
    lane = lax.broadcasted_iota(jnp.int32, (rows, width), 1)
    row_y, deep = split_index(lane, plane)
    lines = jnp.dot(kappa, spread, precision=HIGHEST, preferred_element_type=jnp.float32)
    lines = lines * (1.0 / 108.0)
    along_x, along_y, along_z = (lines[:, i * width : (i + 1) * width] for i in range(3))
    y_even, y_odd = along_y + down(along_y), 4.0 * along_y
    z_even, z_odd = along_z + down(along_z), 4.0 * along_z
    inverse = 27.0 * jnp.where(row_y & 1 == 1, 0.5, 1.0) * jnp.where(deep & 1 == 1, 0.5, 1.0)
    scale_even, scale_odd = inverse, 0.5 * inverse

    def bend(first, second, third, coefficient):
        curve = (4.0 * coefficient) * (first - 2.0 * second + third)
        slope = (3.0 * coefficient) * (third - first)
        return curve - slope, -2.0 * curve, curve + slope

    def in_plane(values, along_y, along_z):
        a, b, c = bend(values, turn(values, -plane), turn(values, -2 * plane), along_y)
        result = a + turn(b, plane) + turn(c, 2 * plane)
        third = jnp.where(deep == plane - 2, turn(values, plane - 2), turn(values, -2))
        a, b, c = bend(values, turn(values, -1), third, along_z)
        return result + a + turn(b, 1) + jnp.where(deep == 0, turn(c, 2 - plane), turn(c, 2))

    def missing(v_even, v_odd):
        a, b, c = bend(v_even, v_odd, up(v_even), along_x)
        k_even = a + down(c) + in_plane(v_even, y_even, z_even)
        k_odd = b + in_plane(v_odd, y_odd, z_odd)
        return heat_even - k_even, heat_odd - k_odd

    one_even, one_odd = missing(even, odd)
    two_even, two_odd = missing(
        even + (STEP * scale_even) * one_even, odd + (STEP * scale_odd) * one_odd
    )
    return (
        even + (0.5 * STEP * scale_even) * (one_even + two_even),
        odd + (0.5 * STEP * scale_odd) * (one_odd + two_odd),
    )


def heat_kernel(plane, layers, first_row, state_ref, spread_ref, new_ref, even_ref, odd_ref):
    even, odd = advance(plane, *(state_ref[i] for i in range(5)), spread_ref[...])
    even_ref[...] = even
    odd_ref[...] = odd
    start = first_row()
    for layer in range(layers):
        new_ref[2 * layer : 2 * layer + 1, :] = even_ref[pl.ds(start + layer, 1), :]
        new_ref[2 * layer + 1 : 2 * layer + 2, :] = odd_ref[pl.ds(start + layer, 1), :]


def basis(step):
    point = (step.astype(jnp.float32) + 0.5) / CPC
    return (
        2.0 * (point - 0.5) * (point - 1.0),
        -4.0 * point * (point - 1.0),
        2.0 * point * (point - 0.5),
    )


def finish_kernel(
    plane, depth, flat, layers, first_row, cell_row, wraps,
    state_ref, spread_ref, weave_ref, packed_ref, edge_ref, behind_ref, ahead_ref,
    gathered_ref, nucleation_ref, frozen_ref, *refs,
):
    solid_ref, even_ref, odd_ref, side_ref, extra_ref = refs[-5:]
    edge_x, wide = frozen_ref.shape
    rows = state_ref.shape[1]
    even, odd = advance(plane, *(state_ref[i] for i in range(5)), spread_ref[...])
    if first_row is not None:
        new_ref = refs[0]
        even_ref[:, 0 : even.shape[1]] = even
        odd_ref[:, 0 : even.shape[1]] = odd
        start = first_row()
        for layer in range(layers):
            new_ref[2 * layer : 2 * layer + 1, :] = even_ref[pl.ds(start + layer, 1), 0 : even.shape[1]]
            new_ref[2 * layer + 1 : 2 * layer + 2, :] = odd_ref[pl.ds(start + layer, 1), 0 : even.shape[1]]
    side_ref[...] = jnp.zeros(side_ref.shape, jnp.float32)
    side_ref[0:depth, :] = behind_ref[...]
    side_ref[flat - depth : flat, :] = ahead_ref[...]
    extra_ref[...] = gathered_ref[...] + jnp.transpose(side_ref[...])
    for t in range(wide // LANES):
        lanes = slice(t * LANES, (t + 1) * LANES)
        rough = jnp.concatenate([edge_ref[:, lanes], jnp.zeros((4, LANES), jnp.float32)], 0)
        codes = pick_codes(packed_ref, rough.astype(jnp.int32))
        behind = rough[0:1] * level(codes[1:2], 1) * 0.25
        ahead = rough[2:3] * level(codes[3:4], 0) * 0.25
        extra_ref[0:1, lanes] += behind
        extra_ref[edge_x - 1 : edge_x, lanes] += ahead
    weave = weave_ref[...]
    even_ref[:, 0:wide] = jnp.dot(even, weave, precision=HIGHEST, preferred_element_type=jnp.float32)
    odd_ref[:, 0:wide] = jnp.dot(odd, weave, precision=HIGHEST, preferred_element_type=jnp.float32)
    first, middle, last = basis(lax.broadcasted_iota(jnp.int32, (CPC, wide), 0))
    base = cell_row()
    for a in range(edge_x // CPC):
        cells = slice(a * CPC, (a + 1) * CPC)
        later = base + (a + 1)
        if wraps:
            later = lax.rem(later, rows)
        temperature = (
            first * even_ref[pl.ds(base + a, 1), 0:wide]
            + middle * odd_ref[pl.ds(base + a, 1), 0:wide]
            + last * even_ref[pl.ds(later, 1), 0:wide]
        )
        under = jnp.maximum(-temperature, 0.0)
        rate = under * (under * extra_ref[cells, :] + nucleation_ref[cells, :])
        frozen = frozen_ref[cells, :]
        solid_ref[cells, :] = frozen + (1.0 - frozen) * (1.0 - jnp.exp(-rate))


def weave_table(width, plane, depth, edge_y, start_y, first_cell, rows_total):
    wide = up_to(edge_y * depth, LANES)
    node, cell = jnp.arange(width)[:, None], jnp.arange(wide)[None, :]
    cell_y, cell_z = first_cell + cell // depth, cell % depth
    step_y = jnp.remainder(start_y + node // plane - 2 * (cell_y // CPC), rows_total)
    step_z = jnp.remainder(node % plane - 2 * (cell_z // CPC), plane)
    take = lambda step, at: sum(jnp.where(step == i, v, 0.0) for i, v in enumerate(basis(at % CPC)))
    return jnp.where(cell < edge_y * depth, take(step_y, cell_y) * take(step_z, cell_z), 0.0)


def lines(values, width):
    flat = values.reshape(-1)
    return jnp.pad(flat, (0, -flat.shape[0] % width)).reshape(-1, width)


def body(
    thermal_state_values,
    thermal_kappa_values,
    nodal_heating_input,
    frozen_share_map,
    crystal_label_map,
    growth_reach_table,
    seed_site_slots,
    seed_crystal_label,
):
    groups, slabs = lax.axis_size("grp"), lax.axis_size("slab")
    devices = groups * slabs
    group, slab = lax.axis_index("grp"), lax.axis_index("slab")
    me = group * slabs + slab
    layers, elements = thermal_kappa_values.shape
    plane = 2 * HEX_COUNT_LATER
    depth = CPC * HEX_COUNT_LATER
    flat = thermal_state_values.shape[1]
    rows_y = flat // plane
    edge_x, flat_cells = frozen_share_map.shape
    edge_y = flat_cells // depth
    wide = up_to(flat_cells, LANES)
    all_layers = layers * devices

    def exchanged(parts, flips):
        sizes = np.cumsum([part.shape[0] for part in parts])
        pairs = [(i, i ^ flips) for i in range(devices)]
        got = lax.ppermute(jnp.concatenate(parts, 0), AXES, pairs)
        return [got[end - part.shape[0] : end] for part, end in zip(parts, sizes)]

    def widened(array):
        return jnp.pad(array, ((0, 0), (0, wide - flat_cells)))

    unit = layers * flat
    count = growth_reach_table.shape[0]
    frozen, label = widened(frozen_share_map), widened(crystal_label_map)
    held, edge_rows = pl.pallas_call(
        pack_kernel,
        out_shape=(
            jax.ShapeDtypeStruct((5, unit), jnp.float32),
            jax.ShapeDtypeStruct((4, wide), jnp.float32),
        ),
        in_specs=[HBM] * 5,
        out_specs=(VMEM, VMEM),
        scratch_shapes=[
            pltpu.VMEM(thermal_state_values.shape, jnp.float32),
            pltpu.VMEM(nodal_heating_input.shape, jnp.float32),
            pltpu.VMEM(thermal_kappa_values.shape, jnp.float32),
            pltpu.VMEM((2, 8, wide), jnp.float32),
            pltpu.VMEM((2, 8, wide), jnp.int32),
            pltpu.SemaphoreType.DMA((7,)),
        ],
        compiler_params=PARAMS,
        name="pack",
    )(*map(in_hbm, (thermal_state_values, nodal_heating_input, thermal_kappa_values, frozen, label)))
    high_edge, low_edge = edge_rows[:2], edge_rows[2:]

    brick_layers = edge_x // CPC
    need_y = (edge_y + CPC - 2) // CPC + 6
    width = up_to(need_y * 2 * plane, LANES)
    if 2 * width > flat:
        width = flat
    seeds = up_to(seed_site_slots.shape[0], LANES)
    short = seeds - seed_site_slots.shape[0]
    table_lanes = up_to(count, 2 * LANES)
    packed, gathered, nucleation, faces, frozen, spread = pl.pallas_call(
        functools.partial(cells_kernel, depth, flat_cells),
        out_shape=(
            jax.ShapeDtypeStruct((table_lanes // (2 * LANES), LANES), jnp.int32),
            jax.ShapeDtypeStruct((edge_x, wide), jnp.float32),
            jax.ShapeDtypeStruct((edge_x, wide), jnp.float32),
            jax.ShapeDtypeStruct((2 * depth, edge_x), jnp.float32),
            jax.ShapeDtypeStruct((edge_x, wide), jnp.float32),
            jax.ShapeDtypeStruct((width, 3 * width), jnp.float32),
        ),
        in_specs=[HBM] * 6,
        out_specs=[VMEM] * 6,
        scratch_shapes=[
            pltpu.VMEM((8, table_lanes), jnp.int32),
            pltpu.VMEM((edge_x, wide), jnp.int32),
            pltpu.VMEM((growth_reach_table.shape[1], count), jnp.int32),
            pltpu.VMEM((edge_x, wide), jnp.int32),
            pltpu.VMEM((seeds // LANES, LANES), jnp.int32),
            pltpu.VMEM((seeds // LANES, LANES), jnp.int32),
            pltpu.SemaphoreType.DMA((6,)),
        ],
        compiler_params=PARAMS,
        name="cells",
    )(
        in_hbm(growth_reach_table.T),
        in_hbm(label),
        in_hbm(frozen),
        in_hbm(jnp.pad(seed_site_slots, (0, short), constant_values=-1).reshape(-1, LANES)),
        in_hbm(jnp.pad(seed_crystal_label, (0, short)).reshape(-1, LANES)),
        in_hbm(jnp.asarray(spread_tables(width, plane))),
    )

    core, pair = me & 1, slab >> 1
    to_behind, to_ahead = faces[:depth], faces[depth:]
    onward = jnp.where(core == 1, to_ahead, 0.0)
    backward = jnp.where(core == 0, to_behind, 0.0)
    held, edges = held[:, None], None
    as_face = lambda part: part.reshape(-1)[: depth * edge_x].reshape(depth, edge_x)
    for bit in reversed(range(1, devices.bit_length() - 1)):
        sent = [lines(held, unit)]
        rides = 1 << bit < slabs
        low = (1 << (bit - 1)) - 1
        moves_on, moves_back = (pair & low) == low, (pair & low) == 0
        if groups == 2 and 1 << bit == slabs:
            sent.append(lines(edge_rows, unit))
        elif rides and low:
            sent.append(lines(jnp.where(moves_on, onward, backward), unit))
        elif rides:
            sent += [lines(onward, unit), lines(backward, unit)]
        theirs, *parts = exchanged(sent, (1 << bit) | 1)
        theirs = theirs.reshape(held.shape)
        upper = (me >> bit) & 1 == 1
        held = jnp.stack(
            [jnp.where(upper, theirs, held), jnp.where(upper, held, theirs)], 2
        ).reshape(held.shape[0], 2 * held.shape[1], unit)
        if groups == 2 and 1 << bit == slabs:
            edges = parts[0].reshape(-1)[: 4 * wide].reshape(4, wide)
        elif rides and low:
            onward = jnp.where(moves_on, as_face(parts[0]), onward)
            backward = jnp.where(moves_back, as_face(parts[0]), backward)
        elif rides:
            onward, backward = as_face(parts[0]), as_face(parts[1])
    across = jnp.where(core == 0, to_ahead, to_behind)
    passing = jnp.where(core == 1, onward, backward)
    sent = [lines(held, unit), lines(across, unit), lines(passing, unit)]
    if edges is not None:
        sent.append(lines(edges, unit))
    theirs, *parts = exchanged(sent, 1)
    across = as_face(parts[0])
    passing = as_face(parts[1]) + jnp.where(core == 0, onward, backward)
    behind = jnp.where(core == 0, passing, across)
    ahead = jnp.where(core == 0, across, passing)
    if edges is not None:
        edges = parts[2].reshape(-1)[: 4 * wide].reshape(4, wide)
    odd_count = lambda number: lax.population_count(number) & 1
    pairs_held = jnp.arange(devices // 2, dtype=jnp.int32)
    even_first = (odd_count(pairs_held) == odd_count(me))[None, :, None]
    theirs = theirs.reshape(held.shape)
    held = jnp.stack(
        [jnp.where(even_first, held, theirs), jnp.where(even_first, theirs, held)], 2
    )
    if edges is None:
        ring = [(i, (i + 1) % groups) for i in range(groups)]
        edges = jnp.concatenate(
            [
                lax.ppermute(high_edge, "grp", ring),
                lax.ppermute(low_edge, "grp", [(j, i) for i, j in ring]),
            ]
        )
    held = held.reshape(5, all_layers, flat)

    def window(first_layer, need_layers, first_element, need_elements):
        rows, width = up_to(need_layers, 8), up_to(need_elements * 2 * plane, LANES)
        part, start_layer, start_y = held, 0, 0
        if 2 * rows <= all_layers:
            start_layer = first_layer
            part = lax.dynamic_slice_in_dim(
                jnp.concatenate([part, part[:, : rows]], 1),
                jnp.remainder(start_layer, all_layers), rows, 1,
            )
        if 2 * width <= flat:
            start_y = 2 * first_element
            shifted = lambda v, by, size: lax.dynamic_slice_in_dim(
                jnp.concatenate([v, v[..., :size]], -1), by, size, v.ndim - 1
            )
            start = jnp.remainder(first_element, rows_y // 2)
            part = jnp.concatenate(
                [
                    shifted(part[:4], start * 2 * plane, width),
                    jnp.pad(
                        shifted(part[4:, :, :elements], start * HEX_COUNT_LATER, width // 4),
                        ((0, 0), (0, 0), (0, width - width // 4)),
                    ),
                ],
                0,
            )
        return part, start_layer, start_y

    first_cell = slab * edge_y
    state, start_layer, start_y = window(
        group * brick_layers - 2,
        brick_layers + 5,
        first_cell // CPC - 2,
        need_y,
    )
    whole = state.shape == held.shape
    weave = weave_table(width, plane, depth, edge_y, start_y, first_cell, rows_y)

    def place(start, layer):
        if not isinstance(start, int):
            return lambda: 2
        return lambda: layer(lax.axis_index("grp"), lax.axis_index("slab"))

    own_layer = lambda g, s: (g * slabs + s) * layers
    cell_row = place(start_layer, lambda g, s: g * brick_layers)
    own_row = place(start_layer, own_layer)
    new_shape = jax.ShapeDtypeStruct((2 * layers, flat), jnp.float32)
    solid_shape = jax.ShapeDtypeStruct((edge_x, wide), jnp.float32)
    span = max(width, wide)
    results = pl.pallas_call(
        functools.partial(
            finish_kernel, plane, depth, flat_cells, layers,
            own_row if whole else None, cell_row, isinstance(start_layer, int),
        ),
        out_shape=(new_shape, solid_shape) if whole else (solid_shape,),
        in_specs=[VMEM] * 10,
        out_specs=(VMEM,) * (1 + whole),
        scratch_shapes=[
            pltpu.VMEM((state.shape[1], span), jnp.float32),
            pltpu.VMEM((state.shape[1], span), jnp.float32),
            pltpu.VMEM((wide, edge_x), jnp.float32),
            pltpu.VMEM((edge_x, wide), jnp.float32),
        ],
        compiler_params=PARAMS,
        name="finish",
    )(
        state, spread, weave, packed, edges,
        behind, ahead, gathered, nucleation, frozen,
    )
    if whole:
        new_field, new_solid = results
    else:
        (new_solid,) = results
        state, start_layer, _ = window(me * layers - 2, layers + 4, 0, rows_y // 2)
        own_row = place(start_layer, own_layer)
        new_field = pl.pallas_call(
            functools.partial(heat_kernel, plane, layers, own_row),
            out_shape=new_shape,
            in_specs=[VMEM] * 2,
            out_specs=VMEM,
            scratch_shapes=[pltpu.VMEM(state.shape[1:], jnp.float32)] * 2,
            compiler_params=PARAMS,
            name="heat",
        )(state, jnp.asarray(spread_tables(flat, plane)))
    return new_field, new_solid[:, :flat_cells]


def solution(mesh):
    in_specs = (
        P(("grp", "slab"), None),
        P(("grp", "slab"), None),
        P(("grp", "slab"), None),
        P("grp", "slab"),
        P("grp", "slab"),
        P(),
        P(("grp", "slab")),
        P(("grp", "slab")),
    )
    out_specs = (P(("grp", "slab"), None), P("grp", "slab"))
    return jax.shard_map(body, mesh=mesh, in_specs=in_specs, out_specs=out_specs, check_vma=False)
```

```python
import functools

import jax
import jax.numpy as jnp
import numpy as np
from jax import lax
from jax.experimental import pallas as pl
from jax.experimental.pallas import tpu as pltpu
from jax.sharding import PartitionSpec as P

HEX_COUNT_LATER = 2
CPC = 8
LANES = 128
HIGHEST = lax.Precision.HIGHEST
STEP = 0.004
AXES = ("grp", "slab")
VMEM = pl.BlockSpec(memory_space=pltpu.VMEM)
HBM = pl.BlockSpec(memory_space=pltpu.HBM)
PARAMS = pltpu.CompilerParams(vmem_limit_bytes=48 * 1024 * 1024)


def in_hbm(array):
    return pltpu.with_memory_space_constraint(array, pltpu.HBM)


def up_to(value, unit):
    return -(-value // unit) * unit


def split_index(value, by):
    if by & (by - 1) == 0:
        return value >> (by.bit_length() - 1), value & (by - 1)
    quotient = lax.div(value, jnp.full_like(value, by))
    return quotient, value - quotient * by


def pack_kernel(
    state_ref, heat_ref, kappa_ref, frozen_ref, label_ref, held_ref, edge_ref,
    state, heat, kappa, frozen, label, sems,
):
    layers, elements = kappa.shape
    flat = state.shape[1]
    edge_x = frozen_ref.shape[0]
    top, bottom = pl.ds(0, 8), pl.ds(edge_x - 8, 8)
    copies = started(
        [
            (state_ref, state),
            (heat_ref, heat),
            (kappa_ref, kappa),
            (frozen_ref.at[top, :], frozen.at[0]),
            (frozen_ref.at[bottom, :], frozen.at[1]),
            (label_ref.at[top, :], label.at[0]),
            (label_ref.at[bottom, :], label.at[1]),
        ],
        sems,
    )
    held_ref[4:5, :] = jnp.zeros((1, held_ref.shape[1]), jnp.float32)
    for copy in copies:
        copy.wait()
    for layer in range(layers):
        lanes = slice(layer * flat, (layer + 1) * flat)
        for parity in range(2):
            row = slice(2 * layer + parity, 2 * layer + parity + 1)
            held_ref[parity : parity + 1, lanes] = state[row, :]
            held_ref[2 + parity : 3 + parity, lanes] = heat[row, :]
        held_ref[4:5, layer * flat : layer * flat + elements] = kappa[layer : layer + 1, :]
    edge_ref[0:1, :] = frozen[1, 7:8, :]
    edge_ref[1:2, :] = label[1, 7:8, :].astype(jnp.float32)
    edge_ref[2:3, :] = frozen[0, 0:1, :]
    edge_ref[3:4, :] = label[0, 0:1, :].astype(jnp.float32)


def pick_codes(table_ref, labels):
    half = table_ref.shape[0]
    tile, lane = labels >> 7, labels & (LANES - 1)
    upper = tile >= half
    row = jnp.where(upper, tile - half, tile)
    found = jnp.zeros(labels.shape, jnp.int32)
    for r in range(half):
        line = jnp.broadcast_to(table_ref[r : r + 1, :], labels.shape)
        here = jnp.take_along_axis(line, lane, axis=1, mode="promise_in_bounds")
        found = jnp.where(row == r, here, found)
    return jnp.where(upper, found >> 12, found) & 4095


def level(code, direction):
    return (((code >> (2 * direction)) & 3) + 1).astype(jnp.float32)


def started(pairs, sems):
    copies = [pltpu.make_async_copy(*pair, sems.at[i]) for i, pair in enumerate(pairs)]
    for copy in copies:
        copy.start()
    return copies


def faces_kernel(
    depth, flat, table_hbm, label_hbm, frozen_hbm,
    packed_ref, label_ref, frozen_ref, faces_ref, line_ref, table_ref, sems,
):
    get_table, get_label, get_frozen = started(
        [(table_hbm, table_ref), (label_hbm, label_ref), (frozen_hbm, frozen_ref)], sems
    )
    count = table_ref.shape[1]
    half = packed_ref.shape[0]
    edge_x = frozen_ref.shape[0]
    place = lax.broadcasted_iota(jnp.int32, table_ref.shape, 0)
    line_ref[...] = jnp.zeros(line_ref.shape, jnp.int32)
    get_label.wait()
    get_frozen.wait()
    label = jnp.transpose(label_ref[...])
    label = jnp.concatenate([label[0:depth], label[flat - depth : flat]], 0)
    frozen = jnp.transpose(frozen_ref[...])
    frozen = 0.25 * jnp.concatenate([frozen[0:depth], frozen[flat - depth : flat]], 0)
    get_table.wait()
    word = jnp.sum((table_ref[...] - 1) << (2 * place), axis=0, keepdims=True)
    line_ref[0:1, 0:count] = word
    for r in range(half):
        low = line_ref[0:1, r * LANES : (r + 1) * LANES]
        high = line_ref[0:1, (r + half) * LANES : (r + half + 1) * LANES]
        packed_ref[r : r + 1, :] = low | (high << 12)
    for t in range(edge_x // LANES):
        lanes = slice(t * LANES, (t + 1) * LANES)
        for part in range(2 * depth // 8):
            rows = slice(part * 8, part * 8 + 8)
            code = pick_codes(packed_ref, label[rows, lanes])
            faces_ref[rows, lanes] = frozen[rows, lanes] * level(code, 2 if part * 8 < depth else 3)


def cells_kernel(
    depth, flat, packed_ref, label_ref, frozen_ref, slot_hbm, seed_hbm, spread_hbm,
    gathered_ref, nucleation_ref, spread_ref, code_ref, slot_ref, seed_ref, sems,
):
    copies = started([(slot_hbm, slot_ref), (seed_hbm, seed_ref), (spread_hbm, spread_ref)], sems)
    edge_x, wide = frozen_ref.shape

    def look_up(chunk, carry):
        rows = pl.ds(pl.multiple_of(chunk * 8, 8), 8)
        for t in range(wide // LANES):
            lanes = pl.ds(t * LANES, LANES)
            code_ref[rows, lanes] = pick_codes(packed_ref, label_ref[rows, lanes])
        return carry

    lax.fori_loop(0, edge_x // 8, look_up, 0, unroll=16)
    frozen = frozen_ref[...] * 0.25
    code = code_ref[...]
    shares = [frozen * level(code, d) for d in range(6)]
    line_x = lax.broadcasted_iota(jnp.int32, (edge_x, wide), 0)
    lane = lax.broadcasted_iota(jnp.int32, (edge_x, wide), 1)
    deep = split_index(lane, depth)[1]
    total = jnp.where(line_x == edge_x - 1, 0.0, pltpu.roll(shares[0], edge_x - 1, 0))
    total += jnp.where(line_x == 0, 0.0, pltpu.roll(shares[1], 1, 0))
    total += jnp.where(lane >= flat - depth, 0.0, pltpu.roll(shares[2], wide - depth, 1))
    total += jnp.where(lane < depth, 0.0, pltpu.roll(shares[3], depth, 1))
    total += jnp.where(
        deep == depth - 1, pltpu.roll(shares[4], depth - 1, 1), pltpu.roll(shares[4], wide - 1, 1)
    )
    total += jnp.where(
        deep == 0, pltpu.roll(shares[5], wide - (depth - 1), 1), pltpu.roll(shares[5], 1, 1)
    )
    gathered_ref[...] = total
    for copy in copies:
        copy.wait()
    sites = seed_ref.shape[0]
    codes = pick_codes(packed_ref, seed_ref[...])
    worth = sum(level(codes, d) for d in range(6))
    site_x, site_lane = split_index(slot_ref[...], flat)
    at_x = lax.broadcasted_iota(jnp.int32, (edge_x, LANES), 0)
    at_lane = lax.broadcasted_iota(jnp.int32, (wide, LANES), 0)
    added = jnp.zeros((edge_x, wide), jnp.float32)
    for r in range(sites):
        left = jnp.where(at_x == site_x[r : r + 1], worth[r : r + 1], 0.0).astype(jnp.bfloat16)
        right = jnp.where(at_lane == site_lane[r : r + 1], 1.0, 0.0).astype(jnp.bfloat16)
        added += lax.dot_general(
            left, right, (((1,), (1,)), ((), ())), preferred_element_type=jnp.float32
        )
    nucleation_ref[...] = added * (1.0 / 6.0)


def spread_tables(width, plane):
    rows_y, deep = width // plane, plane // 2
    along = np.zeros((rows_y // 2, rows_y), np.float32)
    down = np.zeros((deep, plane), np.float32)
    for table in (along, down):
        for element in range(table.shape[0]):
            for local, weight in enumerate((1, 4, 1)):
                table[element, (2 * element + local) % table.shape[1]] += weight
    first_y = np.zeros_like(along)
    first_z = np.zeros_like(down)
    first_y[np.arange(rows_y // 2), 2 * np.arange(rows_y // 2)] = 1
    first_z[np.arange(deep), 2 * np.arange(deep)] = 1
    full = [np.kron(along, down), np.kron(first_y, down), np.kron(along, first_z)]
    out = np.zeros((width, 3 * width), jnp.bfloat16)
    out[: 3 * (width // 4)] = np.concatenate([np.concatenate(full, 1)] * 3, 0)
    return out


def pieces(values):
    out = []
    for _ in range(3):
        out.append(values.astype(jnp.bfloat16).astype(jnp.float32))
        values = values - out[-1]
    return out


def advance(plane, even, odd, heat_even, heat_odd, kappa, spread):
    rows, width = even.shape
    up = lambda v: pltpu.roll(v, rows - 1, 0)
    down = lambda v: pltpu.roll(v, 1, 0)
    turn = lambda v, by: pltpu.roll(v, by % width, 1)
    lane = lax.broadcasted_iota(jnp.int32, (rows, width), 1)
    row_y, deep = split_index(lane, plane)
    first, second, third = pieces(kappa)
    joined = first + turn(second, width // 4) + turn(third, 2 * (width // 4))
    lines = jnp.dot(joined.astype(jnp.bfloat16), spread, preferred_element_type=jnp.float32)
    lines = lines * (1.0 / 108.0)
    along_x, along_y, along_z = (lines[:, i * width : (i + 1) * width] for i in range(3))
    y_even, y_odd = along_y + down(along_y), 4.0 * along_y
    z_even, z_odd = along_z + down(along_z), 4.0 * along_z
    inverse = 27.0 * jnp.where(row_y & 1 == 1, 0.5, 1.0) * jnp.where(deep & 1 == 1, 0.5, 1.0)
    scale_even, scale_odd = inverse, 0.5 * inverse

    def bend(first, second, third, coefficient):
        curve = (4.0 * coefficient) * (first - 2.0 * second + third)
        slope = (3.0 * coefficient) * (third - first)
        return curve - slope, -2.0 * curve, curve + slope

    def in_plane(values, along_y, along_z):
        a, b, c = bend(values, turn(values, -plane), turn(values, -2 * plane), along_y)
        result = a + turn(b, plane) + turn(c, 2 * plane)
        third = jnp.where(deep == plane - 2, turn(values, plane - 2), turn(values, -2))
        a, b, c = bend(values, turn(values, -1), third, along_z)
        return result + a + turn(b, 1) + jnp.where(deep == 0, turn(c, 2 - plane), turn(c, 2))

    def missing(v_even, v_odd):
        a, b, c = bend(v_even, v_odd, up(v_even), along_x)
        k_even = a + down(c) + in_plane(v_even, y_even, z_even)
        k_odd = b + in_plane(v_odd, y_odd, z_odd)
        return heat_even - k_even, heat_odd - k_odd

    one_even, one_odd = missing(even, odd)
    two_even, two_odd = missing(
        even + (STEP * scale_even) * one_even, odd + (STEP * scale_odd) * one_odd
    )
    return (
        even + (0.5 * STEP * scale_even) * (one_even + two_even),
        odd + (0.5 * STEP * scale_odd) * (one_odd + two_odd),
    )


def heat_kernel(plane, layers, first_row, state_ref, spread_ref, new_ref, even_ref, odd_ref):
    even, odd = advance(plane, *(state_ref[i] for i in range(5)), spread_ref[...])
    even_ref[...] = even
    odd_ref[...] = odd
    start = first_row()
    for layer in range(layers):
        new_ref[2 * layer : 2 * layer + 1, :] = even_ref[pl.ds(start + layer, 1), :]
        new_ref[2 * layer + 1 : 2 * layer + 2, :] = odd_ref[pl.ds(start + layer, 1), :]


def basis(step):
    point = (step.astype(jnp.float32) + 0.5) / CPC
    return (
        2.0 * (point - 0.5) * (point - 1.0),
        -4.0 * point * (point - 1.0),
        2.0 * point * (point - 0.5),
    )


def finish_kernel(
    plane, depth, flat, layers, group_lanes, sizes, first_row, cell_row, first_lane, wraps,
    mine_ref, theirs_ref, across_ref, passing_ref, edge_ref, kept_ref, spread_ref, weave_ref,
    packed_ref, gathered_ref, nucleation_ref, frozen_ref, *refs,
):
    solid_ref, state_ref, even_ref, odd_ref, side_ref, extra_ref = refs[-6:]
    edge_x, wide = frozen_ref.shape
    _, rows, width = state_ref.shape
    heat_rows, across_row, passing_row, edge_row, devices = sizes
    core = lax.axis_index("slab") & 1
    if heat_rows:
        me = lax.axis_index("grp") * lax.axis_size("slab") + lax.axis_index("slab")
        for p, off in enumerate(arrival_order(devices)):
            source, block = (mine_ref, p) if p < devices // 2 else (theirs_ref, p - devices // 2)
            for c in range(5):
                for layer in range(layers):
                    state_ref[c, pl.ds((me ^ off) * layers + layer, 1), :] = source[
                        block * 5 + c : block * 5 + c + 1, layer * width : (layer + 1) * width
                    ]
        state = [state_ref[i] for i in range(5)]
    else:
        state = [mine_ref[i] for i in range(5)]
    side_ref[...] = jnp.zeros(side_ref.shape, jnp.float32)
    there = jnp.where(core == 0, 0, flat - depth)
    side_ref[pl.ds(pl.multiple_of(there, 8), depth), :] = (
        kept_ref[...] + passing_ref[passing_row : passing_row + depth, :]
    )
    side_ref[pl.ds(pl.multiple_of(flat - depth - there, 8), depth), :] = across_ref[
        across_row : across_row + depth, :
    ]
    extra_ref[...] = gathered_ref[...] + jnp.transpose(side_ref[...])
    for t in range(wide // LANES):
        lanes = slice(t * LANES, (t + 1) * LANES)
        rough = jnp.concatenate(
            [edge_ref[edge_row : edge_row + 4, lanes], jnp.zeros((4, LANES), jnp.float32)], 0
        )
        codes = pick_codes(packed_ref, rough.astype(jnp.int32))
        behind = rough[0:1] * level(codes[1:2], 1) * 0.25
        ahead = rough[2:3] * level(codes[3:4], 0) * 0.25
        extra_ref[0:1, lanes] += behind
        extra_ref[edge_x - 1 : edge_x, lanes] += ahead
    even, odd = advance(plane, *state, spread_ref[...])
    if first_row is not None:
        new_ref = refs[0]
        even_ref[:, 0:width] = even
        odd_ref[:, 0:width] = odd
        start = first_row()
        for layer in range(layers):
            new_ref[2 * layer : 2 * layer + 1, :] = even_ref[pl.ds(start + layer, 1), 0:width]
            new_ref[2 * layer + 1 : 2 * layer + 2, :] = odd_ref[pl.ds(start + layer, 1), 0:width]
    both = jnp.concatenate([even, odd], 0)
    both = pltpu.roll(both, first_lane(), 1)
    span = weave_ref.shape[0]
    if span > width:
        both = jnp.concatenate([both, jnp.zeros((2 * rows, span - width), jnp.float32)], 1)
    lane = lax.broadcasted_iota(jnp.int32, both.shape, 1)
    first, second, third = pieces(jnp.where(lane < group_lanes, both, 0.0))
    joined = first
    for i, piece in enumerate((second, third, first, second)):
        joined = joined + pltpu.roll(piece, (i + 1) * group_lanes, 1)
    woven = jnp.dot(
        joined.astype(jnp.bfloat16), weave_ref[...], preferred_element_type=jnp.float32
    )
    even_ref[:, 0:wide] = woven[:rows]
    odd_ref[:, 0:wide] = woven[rows:]
    first, middle, last = basis(lax.broadcasted_iota(jnp.int32, (CPC, wide), 0))
    base = cell_row()
    for a in range(edge_x // CPC):
        cells = slice(a * CPC, (a + 1) * CPC)
        later = base + (a + 1)
        if wraps:
            later = lax.rem(later, rows)
        temperature = (
            first * even_ref[pl.ds(base + a, 1), 0:wide]
            + middle * odd_ref[pl.ds(base + a, 1), 0:wide]
            + last * even_ref[pl.ds(later, 1), 0:wide]
        )
        under = jnp.maximum(-temperature, 0.0)
        rate = under * (under * extra_ref[cells, :] + nucleation_ref[cells, :])
        frozen = frozen_ref[cells, :]
        solid_ref[cells, :] = frozen + (1.0 - frozen) * (1.0 - jnp.exp(-rate))


def weave_table(group_lanes, plane, depth, edge_y, first_step, wide):
    node, cell = jnp.arange(group_lanes)[:, None], jnp.arange(wide)[None, :]
    cell_y, cell_z = first_step + cell // depth, cell % depth
    step_y = node // plane - 2 * (cell_y // CPC)
    step_z = jnp.remainder(node % plane - 2 * (cell_z // CPC), plane)
    take = lambda step, at: sum(jnp.where(step == i, v, 0.0) for i, v in enumerate(basis(at % CPC)))
    full = jnp.where(cell < edge_y * depth, take(step_y, cell_y) * take(step_z, cell_z), 0.0)
    high = jnp.floor(full * 128.0) * (1.0 / 128.0)
    both = jnp.stack([high, high, high, full - high, full - high]).reshape(5 * group_lanes, wide)
    short = up_to(5 * group_lanes, LANES) - 5 * group_lanes
    return jnp.pad(both, ((0, short), (0, 0))).astype(jnp.bfloat16)


def arrival_order(devices):
    offs = [0]
    for bit in reversed(range(1, devices.bit_length() - 1)):
        offs += [off ^ (1 << bit) ^ 1 for off in offs]
    return offs + [off ^ 1 for off in offs]


def lines(values, width):
    flat = values.reshape(-1)
    return jnp.pad(flat, (0, -flat.shape[0] % width)).reshape(-1, width)


def body(
    thermal_state_values,
    thermal_kappa_values,
    nodal_heating_input,
    frozen_share_map,
    crystal_label_map,
    growth_reach_table,
    seed_site_slots,
    seed_crystal_label,
):
    groups, slabs = lax.axis_size("grp"), lax.axis_size("slab")
    devices = groups * slabs
    group, slab = lax.axis_index("grp"), lax.axis_index("slab")
    me = group * slabs + slab
    layers, elements = thermal_kappa_values.shape
    plane = 2 * HEX_COUNT_LATER
    depth = CPC * HEX_COUNT_LATER
    flat = thermal_state_values.shape[1]
    rows_y = flat // plane
    edge_x, flat_cells = frozen_share_map.shape
    edge_y = flat_cells // depth
    wide = up_to(flat_cells, LANES)
    all_layers = layers * devices

    def exchanged(parts, flips):
        at = [0]
        for part in parts[:-1]:
            at.append(at[-1] + part.shape[0])
        sent = jnp.concatenate(parts, 0) if len(parts) > 1 else parts[0]
        return sent, lax.ppermute(sent, AXES, [(i, i ^ flips) for i in range(devices)]), at

    def widened(array):
        return jnp.pad(array, ((0, 0), (0, wide - flat_cells)))

    unit = layers * flat
    count = growth_reach_table.shape[0]
    frozen, label = widened(frozen_share_map), widened(crystal_label_map)
    held, edge_rows = pl.pallas_call(
        pack_kernel,
        out_shape=(
            jax.ShapeDtypeStruct((5, unit), jnp.float32),
            jax.ShapeDtypeStruct((4, wide), jnp.float32),
        ),
        in_specs=[HBM] * 5,
        out_specs=(VMEM, VMEM),
        scratch_shapes=[
            pltpu.VMEM(thermal_state_values.shape, jnp.float32),
            pltpu.VMEM(nodal_heating_input.shape, jnp.float32),
            pltpu.VMEM(thermal_kappa_values.shape, jnp.float32),
            pltpu.VMEM((2, 8, wide), jnp.float32),
            pltpu.VMEM((2, 8, wide), jnp.int32),
            pltpu.SemaphoreType.DMA((7,)),
        ],
        compiler_params=PARAMS,
        name="pack",
    )(*map(in_hbm, (thermal_state_values, nodal_heating_input, thermal_kappa_values, frozen, label)))
    high_edge, low_edge = edge_rows[:2], edge_rows[2:]

    brick_layers = edge_x // CPC
    need_y = (edge_y + CPC - 2) // CPC + 6
    width = up_to(need_y * 2 * plane, LANES)
    if 2 * width > flat:
        width = flat
    table_lanes = up_to(count, 2 * LANES)
    packed, label, frozen, faces = pl.pallas_call(
        functools.partial(faces_kernel, depth, flat_cells),
        out_shape=(
            jax.ShapeDtypeStruct((table_lanes // (2 * LANES), LANES), jnp.int32),
            jax.ShapeDtypeStruct((edge_x, wide), jnp.int32),
            jax.ShapeDtypeStruct((edge_x, wide), jnp.float32),
            jax.ShapeDtypeStruct((2 * depth, edge_x), jnp.float32),
        ),
        in_specs=[HBM] * 3,
        out_specs=[VMEM] * 4,
        scratch_shapes=[
            pltpu.VMEM((8, table_lanes), jnp.int32),
            pltpu.VMEM((growth_reach_table.shape[1], count), jnp.int32),
            pltpu.SemaphoreType.DMA((3,)),
        ],
        compiler_params=PARAMS,
        name="faces",
    )(in_hbm(growth_reach_table.T), in_hbm(label), in_hbm(frozen))
    seeds = up_to(seed_site_slots.shape[0], LANES)
    short = seeds - seed_site_slots.shape[0]
    gathered, nucleation, spread = pl.pallas_call(
        functools.partial(cells_kernel, depth, flat_cells),
        out_shape=(
            jax.ShapeDtypeStruct((edge_x, wide), jnp.float32),
            jax.ShapeDtypeStruct((edge_x, wide), jnp.float32),
            jax.ShapeDtypeStruct((width, 3 * width), jnp.bfloat16),
        ),
        in_specs=[VMEM] * 3 + [HBM] * 3,
        out_specs=[VMEM] * 3,
        scratch_shapes=[
            pltpu.VMEM((edge_x, wide), jnp.int32),
            pltpu.VMEM((seeds // LANES, LANES), jnp.int32),
            pltpu.VMEM((seeds // LANES, LANES), jnp.int32),
            pltpu.SemaphoreType.DMA((3,)),
        ],
        compiler_params=PARAMS,
        name="cells",
    )(
        packed,
        label,
        frozen,
        in_hbm(jnp.pad(seed_site_slots, (0, short), constant_values=-1).reshape(-1, LANES)),
        in_hbm(jnp.pad(seed_crystal_label, (0, short)).reshape(-1, LANES)),
        in_hbm(jnp.asarray(spread_tables(width, plane))),
    )

    core, pair = me & 1, slab >> 1
    to_behind, to_ahead = faces[:depth], faces[depth:]
    onward = jnp.where(core == 1, to_ahead, 0.0)
    backward = jnp.where(core == 0, to_behind, 0.0)
    heat, edges = [held], None
    as_face = lambda part: part.reshape(-1)[: depth * edge_x].reshape(depth, edge_x)
    for bit in reversed(range(1, devices.bit_length() - 1)):
        rides = 1 << bit < slabs
        low = (1 << (bit - 1)) - 1
        moves_on, moves_back = (pair & low) == low, (pair & low) == 0
        extra = []
        if groups == 2 and 1 << bit == slabs:
            extra = [lines(edge_rows, unit)]
        elif rides and low:
            extra = [lines(jnp.where(moves_on, onward, backward), unit)]
        elif rides:
            extra = [lines(onward, unit), lines(backward, unit)]
        sent, got, at = exchanged(heat + extra, (1 << bit) | 1)
        heat_rows = sum(part.shape[0] for part in heat)
        heat = [sent[:heat_rows], got[:heat_rows]]
        parts = [got[row : row + part.shape[0]] for row, part in zip(at[len(at) - len(extra) :], extra)]
        if groups == 2 and 1 << bit == slabs:
            edges = parts[0].reshape(-1)[: 4 * wide].reshape(4, wide)
        elif rides and low:
            onward = jnp.where(moves_on, as_face(parts[0]), onward)
            backward = jnp.where(moves_back, as_face(parts[0]), backward)
        elif rides:
            onward, backward = as_face(parts[0]), as_face(parts[1])
    extra = [
        lines(jnp.where(core == 0, to_ahead, to_behind), unit),
        lines(jnp.where(core == 1, onward, backward), unit),
    ]
    if edges is not None:
        extra.append(lines(edges, unit))
    kept = jnp.where(core == 0, onward, backward)
    sent, got, at = exchanged(heat + extra, 1)
    heat_rows = sum(part.shape[0] for part in heat)
    at = at[len(heat) :]
    across, passing = (as_face(got[row : row + part.shape[0]]) for row, part in zip(at, extra[:2]))
    if edges is not None:
        edges = got[at[2] : at[2] + extra[2].shape[0]].reshape(-1)[: 4 * wide].reshape(4, wide)
    if edges is None:
        ring = [(i, (i + 1) % groups) for i in range(groups)]
        edges = jnp.concatenate(
            [
                lax.ppermute(high_edge, "grp", ring),
                lax.ppermute(low_edge, "grp", [(j, i) for i, j in ring]),
            ]
        )
    brick_layers = edge_x // CPC
    first_cell = slab * edge_y
    first_element = first_cell // CPC
    need_layers = brick_layers + 5
    whole = width == flat and 2 * up_to(need_layers, 8) > all_layers
    direct = whole and edge_x == unit and wide == unit and groups == 2
    if direct:
        inputs = (sent, got, got, got, got)
        sizes = (heat_rows, *at, devices)
        start_layer = start_y = 0
    else:
        order = np.argsort(arrival_order(devices))
        blocks = jnp.concatenate([sent[:heat_rows], got[:heat_rows]], 0).reshape(devices, 5, layers, flat)
        blocks = jnp.take(blocks, jnp.asarray(order)[jnp.arange(devices) ^ me], axis=0)
        held = jnp.moveaxis(blocks, 1, 0).reshape(5, all_layers, flat)

        def window(first_layer, need_layers, first_element, need_elements):
            rows, lanes = up_to(need_layers, 8), up_to(need_elements * 2 * plane, LANES)
            part, start_layer, start_y = held, 0, 0
            if 2 * rows <= all_layers:
                start_layer = first_layer
                part = lax.dynamic_slice_in_dim(
                    jnp.concatenate([part, part[:, :rows]], 1),
                    jnp.remainder(start_layer, all_layers), rows, 1,
                )
            if 2 * lanes <= flat:
                start_y = 2 * first_element
                shifted = lambda v, by, size: lax.dynamic_slice_in_dim(
                    jnp.concatenate([v, v[..., :size]], -1), by, size, v.ndim - 1
                )
                start = jnp.remainder(first_element, rows_y // 2)
                part = jnp.concatenate(
                    [
                        shifted(part[:4], start * 2 * plane, lanes),
                        jnp.pad(
                            shifted(part[4:, :, :elements], start * HEX_COUNT_LATER, lanes // 4),
                            ((0, 0), (0, 0), (0, lanes - lanes // 4)),
                        ),
                    ],
                    0,
                )
            return part, start_layer, start_y

        state, start_layer, start_y = window(
            group * brick_layers - 2, need_layers, first_element - 2, need_y
        )
        inputs = (state, state, across, passing, edges)
        sizes = (0, 0, 0, 0, devices)
    if edge_y % CPC == 0 or CPC % edge_y == 0:
        covered = max(edge_y // CPC, 1)
    else:
        covered = (edge_y + CPC - 2) // CPC + 1
    group_lanes = up_to((2 * covered + 1) * plane, 16)
    weave = weave_table(group_lanes, plane, depth, edge_y, first_cell % CPC, wide)

    def place(start, layer):
        if not isinstance(start, int):
            return lambda: 2
        return lambda: layer(lax.axis_index("grp"), lax.axis_index("slab"))

    own_layer = lambda g, s: (g * slabs + s) * layers
    cell_row = place(start_layer, lambda g, s: g * brick_layers)
    own_row = place(start_layer, own_layer)
    if isinstance(start_y, int):
        first_lane = lambda: lax.rem(
            width - (lax.axis_index("slab") * edge_y // CPC) * 2 * plane, width
        )
    else:
        first_lane = lambda: width - 4 * plane
    rows = all_layers if direct else state.shape[1]
    new_shape = jax.ShapeDtypeStruct((2 * layers, flat), jnp.float32)
    solid_shape = jax.ShapeDtypeStruct((edge_x, wide), jnp.float32)
    span = max(width, wide)
    results = pl.pallas_call(
        functools.partial(
            finish_kernel, plane, depth, flat_cells, layers, group_lanes, sizes,
            own_row if whole else None, cell_row, first_lane, isinstance(start_layer, int),
        ),
        out_shape=(new_shape, solid_shape) if whole else (solid_shape,),
        in_specs=[VMEM] * 12,
        out_specs=(VMEM,) * (1 + whole),
        scratch_shapes=[
            pltpu.VMEM((5, rows, width), jnp.float32),
            pltpu.VMEM((rows, span), jnp.float32),
            pltpu.VMEM((rows, span), jnp.float32),
            pltpu.VMEM((wide, edge_x), jnp.float32),
            pltpu.VMEM((edge_x, wide), jnp.float32),
        ],
        compiler_params=PARAMS,
        name="finish",
    )(*inputs, kept, spread, weave, packed, gathered, nucleation, frozen)
    if whole:
        new_field, new_solid = results
    else:
        (new_solid,) = results
        state, start_layer, _ = window(me * layers - 2, layers + 4, 0, rows_y // 2)
        own_row = place(start_layer, own_layer)
        new_field = pl.pallas_call(
            functools.partial(heat_kernel, plane, layers, own_row),
            out_shape=new_shape,
            in_specs=[VMEM] * 2,
            out_specs=VMEM,
            scratch_shapes=[pltpu.VMEM(state.shape[1:], jnp.float32)] * 2,
            compiler_params=PARAMS,
            name="heat",
        )(state, jnp.asarray(spread_tables(flat, plane)))
    return new_field, new_solid[:, :flat_cells]


def solution(mesh):
    in_specs = (
        P(("grp", "slab"), None),
        P(("grp", "slab"), None),
        P(("grp", "slab"), None),
        P("grp", "slab"),
        P("grp", "slab"),
        P(),
        P(("grp", "slab")),
        P(("grp", "slab")),
    )
    out_specs = (P(("grp", "slab"), None), P("grp", "slab"))
    return jax.shard_map(body, mesh=mesh, in_specs=in_specs, out_specs=out_specs, check_vma=False)
```

```python
import functools

import jax
import jax.numpy as jnp
import numpy as np
from jax import lax
from jax.experimental import pallas as pl
from jax.experimental.pallas import tpu as pltpu
from jax.sharding import PartitionSpec as P

HEX_COUNT_LATER = 2
CPC = 8
LANES = 128
CHUNKS = 4
HIGHEST = lax.Precision.HIGHEST
STEP = 0.004
AXES = ("grp", "slab")
VMEM = pl.BlockSpec(memory_space=pltpu.VMEM)
HBM = pl.BlockSpec(memory_space=pltpu.HBM)
PARAMS = pltpu.CompilerParams(vmem_limit_bytes=48 * 1024 * 1024)


def in_hbm(array):
    return pltpu.with_memory_space_constraint(array, pltpu.HBM)


def up_to(value, unit):
    return -(-value // unit) * unit


def split_index(value, by):
    if by & (by - 1) == 0:
        return value >> (by.bit_length() - 1), value & (by - 1)
    quotient = lax.div(value, jnp.full_like(value, by))
    return quotient, value - quotient * by


def pack_kernel(
    state_ref, heat_ref, kappa_ref, frozen_ref, label_ref, held_ref, edge_ref,
    state, heat, kappa, frozen, label, sems,
):
    layers, elements = kappa.shape
    flat = state.shape[1]
    edge_x = frozen_ref.shape[0]
    top, bottom = pl.ds(0, 8), pl.ds(edge_x - 8, 8)
    copies = started(
        [
            (state_ref, state),
            (heat_ref, heat),
            (kappa_ref, kappa),
            (frozen_ref.at[top, :], frozen.at[0]),
            (frozen_ref.at[bottom, :], frozen.at[1]),
            (label_ref.at[top, :], label.at[0]),
            (label_ref.at[bottom, :], label.at[1]),
        ],
        sems,
    )
    held_ref[4:5, :] = jnp.zeros((1, held_ref.shape[1]), jnp.float32)
    for copy in copies:
        copy.wait()
    for layer in range(layers):
        lanes = slice(layer * flat, (layer + 1) * flat)
        for parity in range(2):
            row = slice(2 * layer + parity, 2 * layer + parity + 1)
            held_ref[parity : parity + 1, lanes] = state[row, :]
            held_ref[2 + parity : 3 + parity, lanes] = heat[row, :]
        held_ref[4:5, layer * flat : layer * flat + elements] = kappa[layer : layer + 1, :]
    edge_ref[0:1, :] = frozen[1, 7:8, :]
    edge_ref[1:2, :] = label[1, 7:8, :].astype(jnp.float32)
    edge_ref[2:3, :] = frozen[0, 0:1, :]
    edge_ref[3:4, :] = label[0, 0:1, :].astype(jnp.float32)


def pick_codes(table_ref, labels):
    half = table_ref.shape[0]
    tile, lane = labels >> 7, labels & (LANES - 1)
    upper = tile >= half
    row = jnp.where(upper, tile - half, tile)
    found = jnp.zeros(labels.shape, jnp.int32)
    for r in range(half):
        line = jnp.broadcast_to(table_ref[r : r + 1, :], labels.shape)
        here = jnp.take_along_axis(line, lane, axis=1, mode="promise_in_bounds")
        found = jnp.where(row == r, here, found)
    return jnp.where(upper, found >> 12, found) & 4095


def level(code, direction):
    return (((code >> (2 * direction)) & 3) + 1).astype(jnp.float32)


def started(pairs, sems):
    copies = [pltpu.make_async_copy(*pair, sems.at[i]) for i, pair in enumerate(pairs)]
    for copy in copies:
        copy.start()
    return copies


def faces_kernel(
    depth, flat, table_hbm, label_hbm, frozen_hbm,
    packed_ref, label_ref, frozen_ref, faces_ref, line_ref, table_ref, sems,
):
    get_table, get_label, get_frozen = started(
        [(table_hbm, table_ref), (label_hbm, label_ref), (frozen_hbm, frozen_ref)], sems
    )
    count = table_ref.shape[1]
    half = packed_ref.shape[0]
    edge_x = frozen_ref.shape[0]
    place = lax.broadcasted_iota(jnp.int32, table_ref.shape, 0)
    line_ref[...] = jnp.zeros(line_ref.shape, jnp.int32)
    get_label.wait()
    get_frozen.wait()
    label = jnp.transpose(label_ref[...])
    label = jnp.concatenate([label[0:depth], label[flat - depth : flat]], 0)
    frozen = jnp.transpose(frozen_ref[...])
    frozen = 0.25 * jnp.concatenate([frozen[0:depth], frozen[flat - depth : flat]], 0)
    get_table.wait()
    word = jnp.sum((table_ref[...] - 1) << (2 * place), axis=0, keepdims=True)
    line_ref[0:1, 0:count] = word
    for r in range(half):
        low = line_ref[0:1, r * LANES : (r + 1) * LANES]
        high = line_ref[0:1, (r + half) * LANES : (r + half + 1) * LANES]
        packed_ref[r : r + 1, :] = low | (high << 12)
    for t in range(edge_x // LANES):
        lanes = slice(t * LANES, (t + 1) * LANES)
        for part in range(2 * depth // 8):
            rows = slice(part * 8, part * 8 + 8)
            code = pick_codes(packed_ref, label[rows, lanes])
            faces_ref[rows, lanes] = frozen[rows, lanes] * level(code, 2 if part * 8 < depth else 3)


def cells_kernel(
    depth, flat, packed_ref, label_ref, frozen_ref, faces_ref, gathered_ref, onward_ref, code_ref
):
    onward_ref[...] = faces_ref[...]
    edge_x, wide = frozen_ref.shape

    def look_up(chunk, carry):
        rows = pl.ds(pl.multiple_of(chunk * 8, 8), 8)
        for t in range(wide // LANES):
            lanes = pl.ds(t * LANES, LANES)
            code_ref[rows, lanes] = pick_codes(packed_ref, label_ref[rows, lanes])
        return carry

    lax.fori_loop(0, edge_x // 8, look_up, 0, unroll=16)
    frozen = frozen_ref[...] * 0.25
    code = code_ref[...]
    shares = [frozen * level(code, d) for d in range(6)]
    line_x = lax.broadcasted_iota(jnp.int32, (edge_x, wide), 0)
    lane = lax.broadcasted_iota(jnp.int32, (edge_x, wide), 1)
    deep = split_index(lane, depth)[1]
    total = jnp.where(line_x == edge_x - 1, 0.0, pltpu.roll(shares[0], edge_x - 1, 0))
    total += jnp.where(line_x == 0, 0.0, pltpu.roll(shares[1], 1, 0))
    total += jnp.where(lane >= flat - depth, 0.0, pltpu.roll(shares[2], wide - depth, 1))
    total += jnp.where(lane < depth, 0.0, pltpu.roll(shares[3], depth, 1))
    total += jnp.where(
        deep == depth - 1, pltpu.roll(shares[4], depth - 1, 1), pltpu.roll(shares[4], wide - 1, 1)
    )
    total += jnp.where(
        deep == 0, pltpu.roll(shares[5], wide - (depth - 1), 1), pltpu.roll(shares[5], 1, 1)
    )
    gathered_ref[...] = total


def sites_kernel(
    flat, packed_ref, edge_ref, faces_ref, slot_hbm, seed_hbm, spread_hbm,
    nucleation_ref, ends_ref, spread_ref, onward_ref, slot_ref, seed_ref, sems,
):
    copies = started([(slot_hbm, slot_ref), (seed_hbm, seed_ref), (spread_hbm, spread_ref)], sems)
    onward_ref[...] = faces_ref[...]
    edge_x, wide = nucleation_ref.shape
    for t in range(wide // LANES):
        lanes = slice(t * LANES, (t + 1) * LANES)
        rough = jnp.concatenate([edge_ref[:, lanes], jnp.zeros((4, LANES), jnp.float32)], 0)
        codes = pick_codes(packed_ref, rough.astype(jnp.int32))
        ends_ref[0:1, lanes] = rough[0:1] * level(codes[1:2], 1) * 0.25
        ends_ref[1:2, lanes] = rough[2:3] * level(codes[3:4], 0) * 0.25
    for copy in copies:
        copy.wait()
    sites = seed_ref.shape[0]
    codes = pick_codes(packed_ref, seed_ref[...])
    worth = sum(level(codes, d) for d in range(6))
    site_x, site_lane = split_index(slot_ref[...], flat)
    at_x = lax.broadcasted_iota(jnp.int32, (edge_x, LANES), 0)
    at_lane = lax.broadcasted_iota(jnp.int32, (wide, LANES), 0)
    added = jnp.zeros((edge_x, wide), jnp.float32)
    for r in range(sites):
        left = jnp.where(at_x == site_x[r : r + 1], worth[r : r + 1], 0.0).astype(jnp.bfloat16)
        right = jnp.where(at_lane == site_lane[r : r + 1], 1.0, 0.0).astype(jnp.bfloat16)
        added += lax.dot_general(
            left, right, (((1,), (1,)), ((), ())), preferred_element_type=jnp.float32
        )
    nucleation_ref[...] = added * (1.0 / 6.0)


def spread_tables(width, plane):
    rows_y, deep = width // plane, plane // 2
    along = np.zeros((rows_y // 2, rows_y), np.float32)
    down = np.zeros((deep, plane), np.float32)
    for table in (along, down):
        for element in range(table.shape[0]):
            for local, weight in enumerate((1, 4, 1)):
                table[element, (2 * element + local) % table.shape[1]] += weight
    first_y = np.zeros_like(along)
    first_z = np.zeros_like(down)
    first_y[np.arange(rows_y // 2), 2 * np.arange(rows_y // 2)] = 1
    first_z[np.arange(deep), 2 * np.arange(deep)] = 1
    full = [np.kron(along, down), np.kron(first_y, down), np.kron(along, first_z)]
    out = np.zeros((width, 3 * width), jnp.bfloat16)
    out[: 3 * (width // 4)] = np.concatenate([np.concatenate(full, 1)] * 3, 0)
    return out


def pieces(values):
    out = []
    for _ in range(3):
        out.append(values.astype(jnp.bfloat16).astype(jnp.float32))
        values = values - out[-1]
    return out


def advance(plane, even, odd, heat_even, heat_odd, kappa, spread):
    rows, width = even.shape
    up = lambda v: pltpu.roll(v, rows - 1, 0)
    down = lambda v: pltpu.roll(v, 1, 0)
    turn = lambda v, by: pltpu.roll(v, by % width, 1)
    lane = lax.broadcasted_iota(jnp.int32, (rows, width), 1)
    row_y, deep = split_index(lane, plane)
    first, second, third = pieces(kappa)
    joined = first + turn(second, width // 4) + turn(third, 2 * (width // 4))
    lines = jnp.dot(joined.astype(jnp.bfloat16), spread, preferred_element_type=jnp.float32)
    lines = lines * (1.0 / 108.0)
    along_x, along_y, along_z = (lines[:, i * width : (i + 1) * width] for i in range(3))
    y_even, y_odd = along_y + down(along_y), 4.0 * along_y
    z_even, z_odd = along_z + down(along_z), 4.0 * along_z
    inverse = 27.0 * jnp.where(row_y & 1 == 1, 0.5, 1.0) * jnp.where(deep & 1 == 1, 0.5, 1.0)
    scale_even, scale_odd = inverse, 0.5 * inverse

    def bend(first, second, third, coefficient):
        curve = (4.0 * coefficient) * (first - 2.0 * second + third)
        slope = (3.0 * coefficient) * (third - first)
        return curve - slope, -2.0 * curve, curve + slope

    def in_plane(values, along_y, along_z):
        a, b, c = bend(values, turn(values, -plane), turn(values, -2 * plane), along_y)
        result = a + turn(b, plane) + turn(c, 2 * plane)
        third = jnp.where(deep == plane - 2, turn(values, plane - 2), turn(values, -2))
        a, b, c = bend(values, turn(values, -1), third, along_z)
        return result + a + turn(b, 1) + jnp.where(deep == 0, turn(c, 2 - plane), turn(c, 2))

    def missing(v_even, v_odd):
        a, b, c = bend(v_even, v_odd, up(v_even), along_x)
        k_even = a + down(c) + in_plane(v_even, y_even, z_even)
        k_odd = b + in_plane(v_odd, y_odd, z_odd)
        return heat_even - k_even, heat_odd - k_odd

    one_even, one_odd = missing(even, odd)
    two_even, two_odd = missing(
        even + (STEP * scale_even) * one_even, odd + (STEP * scale_odd) * one_odd
    )
    return (
        even + (0.5 * STEP * scale_even) * (one_even + two_even),
        odd + (0.5 * STEP * scale_odd) * (one_odd + two_odd),
    )


def heat_kernel(plane, layers, first_row, state_ref, spread_ref, new_ref, even_ref, odd_ref):
    even, odd = advance(plane, *(state_ref[i] for i in range(5)), spread_ref[...])
    even_ref[...] = even
    odd_ref[...] = odd
    start = first_row()
    for layer in range(layers):
        new_ref[2 * layer : 2 * layer + 1, :] = even_ref[pl.ds(start + layer, 1), :]
        new_ref[2 * layer + 1 : 2 * layer + 2, :] = odd_ref[pl.ds(start + layer, 1), :]


def basis(step):
    point = (step.astype(jnp.float32) + 0.5) / CPC
    return (
        2.0 * (point - 0.5) * (point - 1.0),
        -4.0 * point * (point - 1.0),
        2.0 * point * (point - 0.5),
    )


def finish_kernel(
    plane, depth, flat, layers, group_lanes, sizes, first_layer, first_row, cell_row, first_lane,
    wraps, mine_ref, theirs_ref, across_ref, passing_ref, edge_ref, kept_ref, spread_ref, weave_ref,
    packed_ref, gathered_ref, nucleation_ref, frozen_ref, *refs,
):
    solid_out, state_ref, even_ref, odd_ref, side_ref, extra_ref, solid_ref, new_ref, sems = refs[-9:]
    edge_x, wide = frozen_ref.shape
    _, all_rows, width = state_ref.shape
    rows = even_ref.shape[0]
    heat_rows, across_row, passing_row, edge_row, devices = sizes
    core = lax.axis_index("slab") & 1
    if heat_rows:
        me = lax.axis_index("grp") * lax.axis_size("slab") + lax.axis_index("slab")
        for p, off in enumerate(arrival_order(devices)):
            source, block = (mine_ref, p) if p < devices // 2 else (theirs_ref, p - devices // 2)
            row = lax.rem((me ^ off) * layers + (all_rows - first_layer()), all_rows)
            for c in range(5):
                for layer in range(layers):
                    state_ref[c, pl.ds(row + layer, 1), :] = source[
                        block * 5 + c : block * 5 + c + 1, layer * width : (layer + 1) * width
                    ]
        state = [state_ref[i, 0:rows, :] for i in range(5)]
    else:
        state = [mine_ref[i] for i in range(5)]
    side_ref[...] = jnp.zeros(side_ref.shape, jnp.float32)
    there = jnp.where(core == 0, 0, flat - depth)
    side_ref[pl.ds(pl.multiple_of(there, 8), depth), :] = (
        kept_ref[...] + passing_ref[passing_row : passing_row + depth, :]
    )
    side_ref[pl.ds(pl.multiple_of(flat - depth - there, 8), depth), :] = across_ref[
        across_row : across_row + depth, :
    ]
    extra_ref[...] = gathered_ref[...] + jnp.transpose(side_ref[...])
    extra_ref[0:1, :] += edge_ref[edge_row : edge_row + 1, 0:wide]
    extra_ref[edge_x - 1 : edge_x, :] += edge_ref[edge_row + 1 : edge_row + 2, 0:wide]
    even, odd = advance(plane, *state, spread_ref[...])
    if first_row is not None:
        even_ref[:, 0:width] = even
        odd_ref[:, 0:width] = odd
        start = first_row()
        for layer in range(layers):
            new_ref[2 * layer : 2 * layer + 1, :] = even_ref[pl.ds(start + layer, 1), 0:width]
            new_ref[2 * layer + 1 : 2 * layer + 2, :] = odd_ref[pl.ds(start + layer, 1), 0:width]
        new_copy = pltpu.make_async_copy(new_ref, refs[0], sems.at[CHUNKS])
        new_copy.start()
    both = jnp.concatenate([even, odd], 0)
    both = pltpu.roll(both, first_lane(), 1)
    span = weave_ref.shape[0]
    if span > width:
        both = jnp.concatenate([both, jnp.zeros((2 * rows, span - width), jnp.float32)], 1)
    lane = lax.broadcasted_iota(jnp.int32, both.shape, 1)
    first, second, third = pieces(jnp.where(lane < group_lanes, both, 0.0))
    joined = first
    for i, piece in enumerate((second, third, first, second)):
        joined = joined + pltpu.roll(piece, (i + 1) * group_lanes, 1)
    woven = jnp.dot(
        joined.astype(jnp.bfloat16), weave_ref[...], preferred_element_type=jnp.float32
    )
    even_ref[:, 0:wide] = woven[:rows]
    odd_ref[:, 0:wide] = woven[rows:]
    first, middle, last = basis(lax.broadcasted_iota(jnp.int32, (CPC, wide), 0))
    base = cell_row()
    elements = edge_x // CPC
    copies = []
    for a in range(elements):
        cells = slice(a * CPC, (a + 1) * CPC)
        later = base + (a + 1)
        if wraps:
            later = lax.rem(later, rows)
        temperature = (
            first * even_ref[pl.ds(base + a, 1), 0:wide]
            + middle * odd_ref[pl.ds(base + a, 1), 0:wide]
            + last * even_ref[pl.ds(later, 1), 0:wide]
        )
        under = jnp.maximum(-temperature, 0.0)
        rate = under * (under * extra_ref[cells, :] + nucleation_ref[cells, :])
        frozen = frozen_ref[cells, :]
        solid_ref[cells, :] = frozen + (1.0 - frozen) * (1.0 - jnp.exp(-rate))
        done = (a + 1) * CHUNKS // elements
        if done > len(copies):
            low = copies[-1][1] if copies else 0
            part = pl.ds(low, (a + 1) * CPC - low)
            copy = pltpu.make_async_copy(
                solid_ref.at[part, :], solid_out.at[part, :], sems.at[len(copies)]
            )
            copy.start()
            copies.append((copy, (a + 1) * CPC))
    for copy, _ in copies:
        copy.wait()
    if first_row is not None:
        new_copy.wait()


def weave_table(group_lanes, plane, depth, edge_y, first_step, wide):
    node, cell = jnp.arange(group_lanes)[:, None], jnp.arange(wide)[None, :]
    cell_y, cell_z = first_step + cell // depth, cell % depth
    step_y = node // plane - 2 * (cell_y // CPC)
    step_z = jnp.remainder(node % plane - 2 * (cell_z // CPC), plane)
    take = lambda step, at: sum(jnp.where(step == i, v, 0.0) for i, v in enumerate(basis(at % CPC)))
    full = jnp.where(cell < edge_y * depth, take(step_y, cell_y) * take(step_z, cell_z), 0.0)
    high = jnp.floor(full * 128.0) * (1.0 / 128.0)
    both = jnp.stack([high, high, high, full - high, full - high]).reshape(5 * group_lanes, wide)
    short = up_to(5 * group_lanes, LANES) - 5 * group_lanes
    return jnp.pad(both, ((0, short), (0, 0))).astype(jnp.bfloat16)


def arrival_order(devices):
    offs = [0]
    for bit in reversed(range(1, devices.bit_length() - 1)):
        offs += [off ^ (1 << bit) ^ 1 for off in offs]
    return offs + [off ^ 1 for off in offs]


def lines(values, width):
    flat = values.reshape(-1)
    return jnp.pad(flat, (0, -flat.shape[0] % width)).reshape(-1, width)


def body(
    thermal_state_values,
    thermal_kappa_values,
    nodal_heating_input,
    frozen_share_map,
    crystal_label_map,
    growth_reach_table,
    seed_site_slots,
    seed_crystal_label,
):
    groups, slabs = lax.axis_size("grp"), lax.axis_size("slab")
    devices = groups * slabs
    group, slab = lax.axis_index("grp"), lax.axis_index("slab")
    me = group * slabs + slab
    layers, elements = thermal_kappa_values.shape
    plane = 2 * HEX_COUNT_LATER
    depth = CPC * HEX_COUNT_LATER
    flat = thermal_state_values.shape[1]
    rows_y = flat // plane
    edge_x, flat_cells = frozen_share_map.shape
    edge_y = flat_cells // depth
    wide = up_to(flat_cells, LANES)
    all_layers = layers * devices

    def exchanged(parts, flips):
        at = [0]
        for part in parts[:-1]:
            at.append(at[-1] + part.shape[0])
        total = at[-1] + parts[-1].shape[0]
        sent = sum(
            jnp.pad(part, ((row, total - row - part.shape[0]), (0, 0)))
            for row, part in zip(at, parts)
        )
        return sent, lax.ppermute(sent, AXES, [(i, i ^ flips) for i in range(devices)]), at

    def widened(array):
        return jnp.pad(array, ((0, 0), (0, wide - flat_cells)))

    unit = layers * flat
    count = growth_reach_table.shape[0]
    frozen, label = widened(frozen_share_map), widened(crystal_label_map)
    held, edge_rows = pl.pallas_call(
        pack_kernel,
        out_shape=(
            jax.ShapeDtypeStruct((5, unit), jnp.float32),
            jax.ShapeDtypeStruct((4, wide), jnp.float32),
        ),
        in_specs=[HBM] * 5,
        out_specs=(VMEM, VMEM),
        scratch_shapes=[
            pltpu.VMEM(thermal_state_values.shape, jnp.float32),
            pltpu.VMEM(nodal_heating_input.shape, jnp.float32),
            pltpu.VMEM(thermal_kappa_values.shape, jnp.float32),
            pltpu.VMEM((2, 8, wide), jnp.float32),
            pltpu.VMEM((2, 8, wide), jnp.int32),
            pltpu.SemaphoreType.DMA((7,)),
        ],
        compiler_params=PARAMS,
        name="pack",
    )(*map(in_hbm, (thermal_state_values, nodal_heating_input, thermal_kappa_values, frozen, label)))
    high_edge, low_edge = edge_rows[:2], edge_rows[2:]

    brick_layers = edge_x // CPC
    need_y = (edge_y + CPC - 2) // CPC + 6
    width = up_to(need_y * 2 * plane, LANES)
    if 2 * width > flat:
        width = flat
    table_lanes = up_to(count, 2 * LANES)
    packed, label, frozen, faces = pl.pallas_call(
        functools.partial(faces_kernel, depth, flat_cells),
        out_shape=(
            jax.ShapeDtypeStruct((table_lanes // (2 * LANES), LANES), jnp.int32),
            jax.ShapeDtypeStruct((edge_x, wide), jnp.int32),
            jax.ShapeDtypeStruct((edge_x, wide), jnp.float32),
            jax.ShapeDtypeStruct((2 * depth, edge_x), jnp.float32),
        ),
        in_specs=[HBM] * 3,
        out_specs=[VMEM] * 4,
        scratch_shapes=[
            pltpu.VMEM((8, table_lanes), jnp.int32),
            pltpu.VMEM((growth_reach_table.shape[1], count), jnp.int32),
            pltpu.SemaphoreType.DMA((3,)),
        ],
        compiler_params=PARAMS,
        name="faces",
    )(in_hbm(growth_reach_table.T), in_hbm(label), in_hbm(frozen))
    gathered, faces_later = pl.pallas_call(
        functools.partial(cells_kernel, depth, flat_cells),
        out_shape=(
            jax.ShapeDtypeStruct((edge_x, wide), jnp.float32),
            jax.ShapeDtypeStruct((2 * depth, edge_x), jnp.float32),
        ),
        in_specs=[VMEM] * 4,
        out_specs=[VMEM] * 2,
        scratch_shapes=[pltpu.VMEM((edge_x, wide), jnp.int32)],
        compiler_params=PARAMS,
        name="cells",
    )(packed, label, frozen, faces)
    seeds = up_to(seed_site_slots.shape[0], LANES)
    short = seeds - seed_site_slots.shape[0]

    def sites(edges):
        return pl.pallas_call(
            functools.partial(sites_kernel, flat_cells),
            out_shape=(
                jax.ShapeDtypeStruct((edge_x, wide), jnp.float32),
                jax.ShapeDtypeStruct((2, wide), jnp.float32),
                jax.ShapeDtypeStruct((width, 3 * width), jnp.bfloat16),
                jax.ShapeDtypeStruct((2 * depth, edge_x), jnp.float32),
            ),
            in_specs=[VMEM] * 3 + [HBM] * 3,
            out_specs=[VMEM] * 4,
            scratch_shapes=[
                pltpu.VMEM((seeds // LANES, LANES), jnp.int32),
                pltpu.VMEM((seeds // LANES, LANES), jnp.int32),
                pltpu.SemaphoreType.DMA((3,)),
            ],
            compiler_params=PARAMS,
            name="sites",
        )(
            packed,
            edges,
            faces_later,
            in_hbm(jnp.pad(seed_site_slots, (0, short), constant_values=-1).reshape(-1, LANES)),
            in_hbm(jnp.pad(seed_crystal_label, (0, short)).reshape(-1, LANES)),
            in_hbm(jnp.asarray(spread_tables(width, plane))),
        )

    core, pair = me & 1, slab >> 1

    def packets(faces):
        return jnp.where(core == 1, faces[depth:], 0.0), jnp.where(core == 0, faces[:depth], 0.0)

    onward, backward = packets(faces)
    heat, edges = [held], None
    if groups > 2:
        ring = [(i, (i + 1) % groups) for i in range(groups)]
        edges = jnp.concatenate(
            [
                lax.ppermute(high_edge, "grp", ring),
                lax.ppermute(low_edge, "grp", [(j, i) for i, j in ring]),
            ]
        )
    moved, ends = 0, None
    as_face = lambda part: part.reshape(-1)[: depth * edge_x].reshape(depth, edge_x)
    for bit in reversed(range(1, devices.bit_length() - 1)):
        rides = 1 << bit < slabs
        low = (1 << (bit - 1)) - 1
        moves_on, moves_back = (pair & low) == low, (pair & low) == 0
        extra = []
        if groups == 2 and 1 << bit == slabs:
            extra = [lines(edge_rows, unit)]
        elif rides and low:
            extra = [lines(jnp.where(moves_on, onward, backward), unit)]
        elif rides:
            extra = [lines(onward, unit), lines(backward, unit)]
        sent, got, at = exchanged(heat + extra, (1 << bit) | 1)
        heat_rows = sum(part.shape[0] for part in heat)
        heat = [sent[:heat_rows], got[:heat_rows]]
        parts = [got[row : row + part.shape[0]] for row, part in zip(at[len(at) - len(extra) :], extra)]
        if groups == 2 and 1 << bit == slabs:
            edges = parts[0].reshape(-1)[: 4 * wide].reshape(4, wide)
        elif rides and low:
            if moved == 0:
                onward, backward = packets(faces_later)
            onward = jnp.where(moves_on, as_face(parts[0]), onward)
            backward = jnp.where(moves_back, as_face(parts[0]), backward)
            moved += 1
        elif rides:
            onward, backward = as_face(parts[0]), as_face(parts[1])
        if edges is not None and ends is None:
            nucleation, ends, spread, faces_last = sites(edges)
    extra = [
        lines(jnp.where(core == 0, faces_last[depth:], faces_last[:depth]), unit),
        lines(jnp.where(core == 1, onward, backward), unit),
    ]
    if groups == 2:
        extra.append(lines(ends, unit))
    kept = jnp.where(core == 0, onward, backward)
    sent, got, at = exchanged(heat + extra, 1)
    heat_rows = sum(part.shape[0] for part in heat)
    at = at[len(heat) :]
    across, passing = (as_face(got[row : row + part.shape[0]]) for row, part in zip(at, extra[:2]))
    if groups == 2:
        ends = got[at[2] : at[2] + extra[2].shape[0]].reshape(-1)[: 2 * wide].reshape(2, wide)
    brick_layers = edge_x // CPC
    first_cell = slab * edge_y
    first_element = first_cell // CPC
    need_layers = brick_layers + 5
    whole = width == flat and 2 * up_to(need_layers, 8) > all_layers
    direct = whole and edge_x == unit and wide == unit and groups == 2
    if direct:
        inputs = (sent, got, got, got, got)
        sizes = (heat_rows, *at, devices)
        start_layer, start_y = group * brick_layers - 2, 0
        rows = min(up_to(need_layers, 8), all_layers)
    else:
        order = np.argsort(arrival_order(devices))
        blocks = jnp.concatenate([sent[:heat_rows], got[:heat_rows]], 0).reshape(devices, 5, layers, flat)
        blocks = jnp.take(blocks, jnp.asarray(order)[jnp.arange(devices) ^ me], axis=0)
        held = jnp.moveaxis(blocks, 1, 0).reshape(5, all_layers, flat)

        def window(first_layer, need_layers, first_element, need_elements):
            rows, lanes = up_to(need_layers, 8), up_to(need_elements * 2 * plane, LANES)
            part, start_layer, start_y = held, 0, 0
            if 2 * rows <= all_layers:
                start_layer = first_layer
                part = lax.dynamic_slice_in_dim(
                    jnp.concatenate([part, part[:, :rows]], 1),
                    jnp.remainder(start_layer, all_layers), rows, 1,
                )
            if 2 * lanes <= flat:
                start_y = 2 * first_element
                shifted = lambda v, by, size: lax.dynamic_slice_in_dim(
                    jnp.concatenate([v, v[..., :size]], -1), by, size, v.ndim - 1
                )
                start = jnp.remainder(first_element, rows_y // 2)
                part = jnp.concatenate(
                    [
                        shifted(part[:4], start * 2 * plane, lanes),
                        jnp.pad(
                            shifted(part[4:, :, :elements], start * HEX_COUNT_LATER, lanes // 4),
                            ((0, 0), (0, 0), (0, lanes - lanes // 4)),
                        ),
                    ],
                    0,
                )
            return part, start_layer, start_y

        state, start_layer, start_y = window(
            group * brick_layers - 2, need_layers, first_element - 2, need_y
        )
        inputs = (state, state, across, passing, ends)
        sizes = (0, 0, 0, 0, devices)
        rows = state.shape[1]
    if edge_y % CPC == 0 or CPC % edge_y == 0:
        covered = max(edge_y // CPC, 1)
    else:
        covered = (edge_y + CPC - 2) // CPC + 1
    group_lanes = up_to((2 * covered + 1) * plane, 16)
    weave = weave_table(group_lanes, plane, depth, edge_y, first_cell % CPC, wide)

    def place(start, layer):
        if not isinstance(start, int):
            return lambda: 2
        return lambda: layer(lax.axis_index("grp"), lax.axis_index("slab"))

    def first_layer():
        return lax.rem(lax.axis_index("grp") * brick_layers + (all_layers - 2), all_layers)

    own_layer = lambda g, s: (g * slabs + s) * layers
    cell_row = place(start_layer, lambda g, s: g * brick_layers)
    own_row = place(start_layer, own_layer)
    if direct:
        own_row = lambda: lax.axis_index("slab") * layers + 2
    if isinstance(start_y, int):
        first_lane = lambda: lax.rem(
            width - (lax.axis_index("slab") * edge_y // CPC) * 2 * plane, width
        )
    else:
        first_lane = lambda: width - 4 * plane
    new_shape = jax.ShapeDtypeStruct((2 * layers, flat), jnp.float32)
    solid_shape = jax.ShapeDtypeStruct((edge_x, wide), jnp.float32)
    span = max(width, wide)
    results = pl.pallas_call(
        functools.partial(
            finish_kernel, plane, depth, flat_cells, layers, group_lanes, sizes,
            first_layer, own_row if whole else None, cell_row, first_lane,
            isinstance(start_layer, int),
        ),
        out_shape=(new_shape, solid_shape) if whole else (solid_shape,),
        in_specs=[VMEM] * 12,
        out_specs=(HBM,) * (1 + whole),
        scratch_shapes=[
            pltpu.VMEM((5, all_layers if direct else rows, width), jnp.float32),
            pltpu.VMEM((rows, span), jnp.float32),
            pltpu.VMEM((rows, span), jnp.float32),
            pltpu.VMEM((wide, edge_x), jnp.float32),
            pltpu.VMEM((edge_x, wide), jnp.float32),
            pltpu.VMEM((edge_x, wide), jnp.float32),
            pltpu.VMEM(new_shape.shape, jnp.float32),
            pltpu.SemaphoreType.DMA((CHUNKS + 1,)),
        ],
        compiler_params=PARAMS,
        name="finish",
    )(*inputs, kept, spread, weave, packed, gathered, nucleation, frozen)
    if whole:
        new_field, new_solid = results
    else:
        (new_solid,) = results
        state, start_layer, _ = window(me * layers - 2, layers + 4, 0, rows_y // 2)
        own_row = place(start_layer, own_layer)
        new_field = pl.pallas_call(
            functools.partial(heat_kernel, plane, layers, own_row),
            out_shape=new_shape,
            in_specs=[VMEM] * 2,
            out_specs=VMEM,
            scratch_shapes=[pltpu.VMEM(state.shape[1:], jnp.float32)] * 2,
            compiler_params=PARAMS,
            name="heat",
        )(state, jnp.asarray(spread_tables(flat, plane)))
    return new_field, new_solid[:, :flat_cells]


def solution(mesh):
    in_specs = (
        P(("grp", "slab"), None),
        P(("grp", "slab"), None),
        P(("grp", "slab"), None),
        P("grp", "slab"),
        P("grp", "slab"),
        P(),
        P(("grp", "slab")),
        P(("grp", "slab")),
    )
    out_specs = (P(("grp", "slab"), None), P("grp", "slab"))
    return jax.shard_map(body, mesh=mesh, in_specs=in_specs, out_specs=out_specs, check_vma=False)
```

```python
import functools

import jax
import jax.numpy as jnp
import numpy as np
from jax import lax
from jax.experimental import pallas as pl
from jax.experimental.pallas import tpu as pltpu
from jax.sharding import PartitionSpec as P

HEX_COUNT_LATER = 2
CPC = 8
LANES = 128
CHUNKS = 4
HIGHEST = lax.Precision.HIGHEST
STEP = 0.004
AXES = ("grp", "slab")
VMEM = pl.BlockSpec(memory_space=pltpu.VMEM)
HBM = pl.BlockSpec(memory_space=pltpu.HBM)
PARAMS = pltpu.CompilerParams(vmem_limit_bytes=48 * 1024 * 1024)


def in_hbm(array):
    return pltpu.with_memory_space_constraint(array, pltpu.HBM)


def up_to(value, unit):
    return -(-value // unit) * unit


def split_index(value, by):
    if by & (by - 1) == 0:
        return value >> (by.bit_length() - 1), value & (by - 1)
    quotient = lax.div(value, jnp.full_like(value, by))
    return quotient, value - quotient * by


def pack_kernel(
    state_ref, heat_ref, kappa_ref, frozen_ref, label_ref, held_ref, *refs
):
    state, heat, kappa, frozen, label, sems = refs[-6:]
    edge_ref = refs[0] if len(refs) > 6 else held_ref.at[5:9, :]
    layers, elements = kappa.shape
    flat = state.shape[1]
    edge_x = frozen_ref.shape[0]
    top, bottom = pl.ds(0, 8), pl.ds(edge_x - 8, 8)
    copies = started(
        [
            (state_ref, state),
            (heat_ref, heat),
            (kappa_ref, kappa),
            (frozen_ref.at[top, :], frozen.at[0]),
            (frozen_ref.at[bottom, :], frozen.at[1]),
            (label_ref.at[top, :], label.at[0]),
            (label_ref.at[bottom, :], label.at[1]),
        ],
        sems,
    )
    held_ref[4:5, :] = jnp.zeros((1, held_ref.shape[1]), jnp.float32)
    for copy in copies:
        copy.wait()
    for layer in range(layers):
        lanes = slice(layer * flat, (layer + 1) * flat)
        for parity in range(2):
            row = slice(2 * layer + parity, 2 * layer + parity + 1)
            held_ref[parity : parity + 1, lanes] = state[row, :]
            held_ref[2 + parity : 3 + parity, lanes] = heat[row, :]
        held_ref[4:5, layer * flat : layer * flat + elements] = kappa[layer : layer + 1, :]
    edge_ref[0:1, :] = frozen[1, 7:8, :]
    edge_ref[1:2, :] = label[1, 7:8, :].astype(jnp.float32)
    edge_ref[2:3, :] = frozen[0, 0:1, :]
    edge_ref[3:4, :] = label[0, 0:1, :].astype(jnp.float32)


def pick_codes(table_ref, labels):
    half = table_ref.shape[0]
    tile, lane = labels >> 7, labels & (LANES - 1)
    upper = tile >= half
    row = jnp.where(upper, tile - half, tile)
    found = jnp.zeros(labels.shape, jnp.int32)
    for r in range(half):
        line = jnp.broadcast_to(table_ref[r : r + 1, :], labels.shape)
        here = jnp.take_along_axis(line, lane, axis=1, mode="promise_in_bounds")
        found = jnp.where(row == r, here, found)
    return jnp.where(upper, found >> 12, found) & 4095


def level(code, direction):
    return (((code >> (2 * direction)) & 3) + 1).astype(jnp.float32)


def started(pairs, sems):
    copies = [pltpu.make_async_copy(*pair, sems.at[i]) for i, pair in enumerate(pairs)]
    for copy in copies:
        copy.start()
    return copies


def faces_kernel(
    depth, flat, table_hbm, label_hbm, frozen_hbm,
    packed_ref, label_ref, frozen_ref, faces_ref, line_ref, table_ref, sems,
):
    get_table, get_label, get_frozen = started(
        [(table_hbm, table_ref), (label_hbm, label_ref), (frozen_hbm, frozen_ref)], sems
    )
    count = table_ref.shape[1]
    half = packed_ref.shape[0]
    edge_x = frozen_ref.shape[0]
    place = lax.broadcasted_iota(jnp.int32, table_ref.shape, 0)
    line_ref[...] = jnp.zeros(line_ref.shape, jnp.int32)
    get_label.wait()
    get_frozen.wait()
    label = jnp.transpose(label_ref[...])
    label = jnp.concatenate([label[0:depth], label[flat - depth : flat]], 0)
    frozen = jnp.transpose(frozen_ref[...])
    frozen = 0.25 * jnp.concatenate([frozen[0:depth], frozen[flat - depth : flat]], 0)
    get_table.wait()
    word = jnp.sum((table_ref[...] - 1) << (2 * place), axis=0, keepdims=True)
    line_ref[0:1, 0:count] = word
    for r in range(half):
        low = line_ref[0:1, r * LANES : (r + 1) * LANES]
        high = line_ref[0:1, (r + half) * LANES : (r + half + 1) * LANES]
        packed_ref[r : r + 1, :] = low | (high << 12)
    for t in range(edge_x // LANES):
        lanes = slice(t * LANES, (t + 1) * LANES)
        for part in range(2 * depth // 8):
            rows = slice(part * 8, part * 8 + 8)
            code = pick_codes(packed_ref, label[rows, lanes])
            faces_ref[rows, lanes] = frozen[rows, lanes] * level(code, 2 if part * 8 < depth else 3)


def cells_kernel(
    depth, flat, packed_ref, label_ref, frozen_ref, faces_ref, gathered_ref, onward_ref, code_ref
):
    onward_ref[...] = faces_ref[...]
    edge_x, wide = frozen_ref.shape

    def look_up(chunk, carry):
        rows = pl.ds(pl.multiple_of(chunk * 8, 8), 8)
        for t in range(wide // LANES):
            lanes = pl.ds(t * LANES, LANES)
            code_ref[rows, lanes] = pick_codes(packed_ref, label_ref[rows, lanes])
        return carry

    lax.fori_loop(0, edge_x // 8, look_up, 0, unroll=16)
    frozen = frozen_ref[...] * 0.25
    code = code_ref[...]
    shares = [frozen * level(code, d) for d in range(6)]
    line_x = lax.broadcasted_iota(jnp.int32, (edge_x, wide), 0)
    lane = lax.broadcasted_iota(jnp.int32, (edge_x, wide), 1)
    deep = split_index(lane, depth)[1]
    total = jnp.where(line_x == edge_x - 1, 0.0, pltpu.roll(shares[0], edge_x - 1, 0))
    total += jnp.where(line_x == 0, 0.0, pltpu.roll(shares[1], 1, 0))
    total += jnp.where(lane >= flat - depth, 0.0, pltpu.roll(shares[2], wide - depth, 1))
    total += jnp.where(lane < depth, 0.0, pltpu.roll(shares[3], depth, 1))
    total += jnp.where(
        deep == depth - 1, pltpu.roll(shares[4], depth - 1, 1), pltpu.roll(shares[4], wide - 1, 1)
    )
    total += jnp.where(
        deep == 0, pltpu.roll(shares[5], wide - (depth - 1), 1), pltpu.roll(shares[5], 1, 1)
    )
    gathered_ref[...] = total


def sites_kernel(
    flat, packed_ref, edge_ref, faces_ref, slot_hbm, seed_hbm, spread_hbm,
    nucleation_ref, ends_ref, spread_ref, onward_ref, slot_ref, seed_ref, sems,
):
    copies = started([(slot_hbm, slot_ref), (seed_hbm, seed_ref), (spread_hbm, spread_ref)], sems)
    onward_ref[...] = faces_ref[...]
    edge_x, wide = nucleation_ref.shape
    for t in range(wide // LANES):
        lanes = slice(t * LANES, (t + 1) * LANES)
        rough = jnp.concatenate([edge_ref[:, lanes], jnp.zeros((4, LANES), jnp.float32)], 0)
        codes = pick_codes(packed_ref, rough.astype(jnp.int32))
        ends_ref[0:1, lanes] = rough[0:1] * level(codes[1:2], 1) * 0.25
        ends_ref[1:2, lanes] = rough[2:3] * level(codes[3:4], 0) * 0.25
    for copy in copies:
        copy.wait()
    sites = seed_ref.shape[0]
    codes = pick_codes(packed_ref, seed_ref[...])
    worth = sum(level(codes, d) for d in range(6))
    site_x, site_lane = split_index(slot_ref[...], flat)
    at_x = lax.broadcasted_iota(jnp.int32, (edge_x, LANES), 0)
    at_lane = lax.broadcasted_iota(jnp.int32, (wide, LANES), 0)
    added = jnp.zeros((edge_x, wide), jnp.float32)
    for r in range(sites):
        left = jnp.where(at_x == site_x[r : r + 1], worth[r : r + 1], 0.0).astype(jnp.bfloat16)
        right = jnp.where(at_lane == site_lane[r : r + 1], 1.0, 0.0).astype(jnp.bfloat16)
        added += lax.dot_general(
            left, right, (((1,), (1,)), ((), ())), preferred_element_type=jnp.float32
        )
    nucleation_ref[...] = added * (1.0 / 6.0)


def spread_tables(width, plane):
    rows_y, deep = width // plane, plane // 2

    def tables(count):
        spread, after, before = (np.zeros((count // 2, count), np.float32) for _ in range(3))
        for element in range(count // 2):
            for local, weight in enumerate((1, 4, 1)):
                spread[element, (2 * element + local) % count] += weight
            for local in range(2):
                after[element, (2 * element + local) % count] += 1
                before[element, (2 * element + local + 1) % count] += 1
        return spread, after, before

    spread_y, after_y, before_y = tables(rows_y)
    spread_z, after_z, before_z = tables(plane)
    full = [
        np.kron(spread_y, spread_z),
        np.kron(after_y, spread_z),
        np.kron(before_y, spread_z),
        np.kron(spread_y, after_z),
        np.kron(spread_y, before_z),
    ]
    half = lambda count: np.where(np.arange(count) % 2 == 1, 0.5, 1.0)
    inverse = 27.0 * np.kron(half(rows_y), half(plane))
    out = np.zeros((width, 5 * width), jnp.bfloat16)
    out[: 3 * (width // 4)] = np.concatenate([np.concatenate([t * inverse for t in full], 1)] * 3, 0)
    return out


def pieces(values):
    out = []
    for _ in range(3):
        out.append(values.astype(jnp.bfloat16).astype(jnp.float32))
        values = values - out[-1]
    return out


def advance(plane, even, odd, heat_even, heat_odd, kappa, spread):
    rows, width = even.shape
    up = lambda v: pltpu.roll(v, rows - 1, 0)
    down = lambda v: pltpu.roll(v, 1, 0)
    turn = lambda v, by: pltpu.roll(v, by % width, 1)
    lane = lax.broadcasted_iota(jnp.int32, (rows, width), 1)
    row_y, deep = split_index(lane, plane)
    even_y, even_z = row_y & 1 == 0, deep & 1 == 0
    first, second, third = pieces(kappa)
    joined = first + turn(second, width // 4) + turn(third, 2 * (width // 4))
    lines = jnp.dot(joined.astype(jnp.bfloat16), spread, preferred_element_type=jnp.float32)
    lines = lines * (STEP / 108.0)
    along_x, *others = (lines[:, i * width : (i + 1) * width] for i in range(5))
    behind_x = down(along_x)
    scale = STEP * 27.0 * jnp.where(even_y, 1.0, 0.5) * jnp.where(even_z, 1.0, 0.5)
    heat_even, heat_odd = scale * heat_even, (0.5 * scale) * heat_odd

    def in_plane(parts):
        after_y, before_y, after_z, before_z = parts
        own = jnp.where(even_y, 7.0 * (after_y + before_y), 16.0 * after_y)
        own = own + jnp.where(even_z, 7.0 * (after_z + before_z), 16.0 * after_z)
        far = [jnp.where(even_y, v, 0.0) for v in parts[:2]] + [
            jnp.where(even_z, v, 0.0) for v in parts[2:]
        ]
        return own, [-8.0 * v for v in parts], far

    own_even, near_even, far_even = in_plane([v + down(v) for v in others])
    own_odd, near_odd, far_odd = in_plane([2.0 * v for v in others])
    own_even = own_even + 7.0 * (along_x + behind_x)
    own_odd = own_odd + 8.0 * along_x
    near_x, near_behind, near_odd_x = -8.0 * along_x, -8.0 * behind_x, -4.0 * along_x

    def moved(values, by):
        if by > 0:
            return jnp.where(deep + by >= plane, turn(values, plane - by), turn(values, -by))
        return jnp.where(deep + by < 0, turn(values, -by - plane), turn(values, -by))

    def neighbours(values, near, far):
        ahead_y, back_y = turn(values, -plane), turn(values, plane)
        total = near[0] * ahead_y + near[1] * back_y
        total += near[2] * moved(values, 1) + near[3] * moved(values, -1)
        total += far[0] * turn(values, -2 * plane) + far[1] * turn(values, 2 * plane)
        if plane == 4:
            return total + (far[2] + far[3]) * moved(values, 2)
        return total + far[2] * moved(values, 2) + far[3] * moved(values, -2)

    def change(v_even, v_odd):
        following = up(v_even)
        k_even = own_even * v_even + along_x * following + behind_x * down(v_even)
        k_even += near_x * v_odd + near_behind * down(v_odd)
        k_odd = own_odd * v_odd + near_odd_x * (v_even + following)
        k_even += neighbours(v_even, near_even, far_even)
        k_odd += neighbours(v_odd, near_odd, far_odd)
        return heat_even - k_even, heat_odd - k_odd

    one_even, one_odd = change(even, odd)
    two_even, two_odd = change(even + one_even, odd + one_odd)
    return even + 0.5 * (one_even + two_even), odd + 0.5 * (one_odd + two_odd)


def heat_kernel(plane, layers, first_row, state_ref, spread_ref, new_ref, even_ref, odd_ref):
    even, odd = advance(plane, *(state_ref[i] for i in range(5)), spread_ref[...])
    even_ref[...] = even
    odd_ref[...] = odd
    start = first_row()
    for layer in range(layers):
        new_ref[2 * layer : 2 * layer + 1, :] = even_ref[pl.ds(start + layer, 1), :]
        new_ref[2 * layer + 1 : 2 * layer + 2, :] = odd_ref[pl.ds(start + layer, 1), :]


def basis(step):
    point = (step.astype(jnp.float32) + 0.5) / CPC
    return (
        2.0 * (point - 0.5) * (point - 1.0),
        -4.0 * point * (point - 1.0),
        2.0 * point * (point - 0.5),
    )


def finish_kernel(
    plane, depth, flat, layers, group_lanes, sizes, first_layer, first_row, cell_row, first_lane,
    wraps, mine_ref, theirs_ref, across_ref, passing_ref, edge_ref, kept_ref, spread_ref, weave_ref,
    packed_ref, gathered_ref, nucleation_ref, frozen_ref, *refs,
):
    solid_out, state_ref, even_ref, odd_ref, side_ref, extra_ref, solid_ref, new_ref, sems = refs[-9:]
    edge_x, wide = frozen_ref.shape
    _, all_rows, width = state_ref.shape
    rows = even_ref.shape[0]
    heat_rows, across_row, passing_row, edge_row, devices = sizes
    core = lax.axis_index("slab") & 1
    if heat_rows:
        me = lax.axis_index("grp") * lax.axis_size("slab") + lax.axis_index("slab")
        for p, off in enumerate(arrival_order(devices)):
            source, block = (mine_ref, p) if p < devices // 2 else (theirs_ref, p - devices // 2)
            row = lax.rem((me ^ off) * layers + (all_rows - first_layer()), all_rows)
            for c in range(5):
                for layer in range(layers):
                    state_ref[c, pl.ds(row + layer, 1), :] = source[
                        block * 5 + c : block * 5 + c + 1, layer * width : (layer + 1) * width
                    ]
        state = [state_ref[i, 0:rows, :] for i in range(5)]
    else:
        state = [mine_ref[i] for i in range(5)]
    side_ref[...] = jnp.zeros(side_ref.shape, jnp.float32)
    there = jnp.where(core == 0, 0, flat - depth)
    side_ref[pl.ds(pl.multiple_of(there, 8), depth), :] = (
        kept_ref[...] + passing_ref[passing_row : passing_row + depth, :]
    )
    side_ref[pl.ds(pl.multiple_of(flat - depth - there, 8), depth), :] = across_ref[
        across_row : across_row + depth, :
    ]
    extra_ref[...] = gathered_ref[...] + jnp.transpose(side_ref[...])
    extra_ref[0:1, :] += edge_ref[edge_row : edge_row + 1, 0:wide]
    extra_ref[edge_x - 1 : edge_x, :] += edge_ref[edge_row + 1 : edge_row + 2, 0:wide]
    even, odd = advance(plane, *state, spread_ref[...])
    if first_row is not None:
        even_ref[:, 0:width] = even
        odd_ref[:, 0:width] = odd
        start = first_row()
        for layer in range(layers):
            new_ref[2 * layer : 2 * layer + 1, :] = even_ref[pl.ds(start + layer, 1), 0:width]
            new_ref[2 * layer + 1 : 2 * layer + 2, :] = odd_ref[pl.ds(start + layer, 1), 0:width]
        new_copy = pltpu.make_async_copy(new_ref, refs[0], sems.at[CHUNKS])
        new_copy.start()
    both = jnp.concatenate([even, odd], 0)
    if group_lanes:
        lane = lax.broadcasted_iota(jnp.int32, both.shape, 1)
        first_node = first_lane()
        inside = (lane >= first_node) & (lane < first_node + group_lanes)
        inside |= lane + width < first_node + group_lanes
        first, second, third = pieces(jnp.where(inside, both, 0.0))
        joined = first
        for i, piece in enumerate((second, third, first, second)):
            joined = joined + pltpu.roll(piece, (i + 1) * group_lanes, 1)
    else:
        first, second, third = pieces(both)
        joined = jnp.concatenate([first, second, third, first, second], 1)
    woven = jnp.dot(
        joined.astype(jnp.bfloat16), weave_ref[...], preferred_element_type=jnp.float32
    )
    even_ref[:, 0:wide] = woven[:rows]
    odd_ref[:, 0:wide] = woven[rows:]
    first, middle, last = basis(lax.broadcasted_iota(jnp.int32, (CPC, wide), 0))
    base = cell_row()
    elements = edge_x // CPC
    copies = []
    for a in range(elements):
        cells = slice(a * CPC, (a + 1) * CPC)
        later = base + (a + 1)
        if wraps:
            later = lax.rem(later, rows)
        temperature = (
            first * even_ref[pl.ds(base + a, 1), 0:wide]
            + middle * odd_ref[pl.ds(base + a, 1), 0:wide]
            + last * even_ref[pl.ds(later, 1), 0:wide]
        )
        under = jnp.maximum(-temperature, 0.0)
        rate = under * (under * extra_ref[cells, :] + nucleation_ref[cells, :])
        frozen = frozen_ref[cells, :]
        solid_ref[cells, :] = frozen + (1.0 - frozen) * (1.0 - jnp.exp(-rate))
        done = (a + 1) * CHUNKS // elements
        if done > len(copies):
            low = copies[-1][1] if copies else 0
            part = pl.ds(low, (a + 1) * CPC - low)
            copy = pltpu.make_async_copy(
                solid_ref.at[part, :], solid_out.at[part, :], sems.at[len(copies)]
            )
            copy.start()
            copies.append((copy, (a + 1) * CPC))
    for copy, _ in copies:
        copy.wait()
    if first_row is not None:
        new_copy.wait()


def weave_table(group_lanes, width, plane, depth, edge_y, first_step, first_node, wide):
    span = group_lanes or width
    row = jnp.arange(width if group_lanes else 5 * width)[:, None]
    cell = jnp.arange(wide)[None, :]
    if group_lanes:
        row = (row - first_node) % width
        copy, node = row // span, row % span
    else:
        copy, node = row // span, (row % span - first_node) % width
    cell_y, cell_z = first_step + cell // depth, cell % depth
    step_y = node // plane - 2 * (cell_y // CPC)
    step_z = (node % plane - 2 * (cell_z // CPC)) % plane
    take = lambda step, at: sum(jnp.where(step == i, v, 0.0) for i, v in enumerate(basis(at % CPC)))
    full = take(step_y, cell_y) * take(step_z, cell_z)
    high = jnp.floor(full * 128.0) * (1.0 / 128.0)
    part = jnp.where(copy < 3, high, full - high)
    return jnp.where((copy < 5) & (cell < edge_y * depth), part, 0.0).astype(jnp.bfloat16)


def arrival_order(devices):
    offs = [0]
    for bit in reversed(range(1, devices.bit_length() - 1)):
        offs += [off ^ (1 << bit) ^ 1 for off in offs]
    return offs + [off ^ 1 for off in offs]


def lines(values, width):
    flat = values.reshape(-1)
    return jnp.pad(flat, (0, -flat.shape[0] % width)).reshape(-1, width)


def body(
    thermal_state_values,
    thermal_kappa_values,
    nodal_heating_input,
    frozen_share_map,
    crystal_label_map,
    growth_reach_table,
    seed_site_slots,
    seed_crystal_label,
):
    groups, slabs = lax.axis_size("grp"), lax.axis_size("slab")
    devices = groups * slabs
    group, slab = lax.axis_index("grp"), lax.axis_index("slab")
    me = group * slabs + slab
    layers, elements = thermal_kappa_values.shape
    plane = 2 * HEX_COUNT_LATER
    depth = CPC * HEX_COUNT_LATER
    flat = thermal_state_values.shape[1]
    rows_y = flat // plane
    edge_x, flat_cells = frozen_share_map.shape
    edge_y = flat_cells // depth
    wide = up_to(flat_cells, LANES)
    all_layers = layers * devices

    def exchanged(parts, flips, sent=None):
        at = [0]
        for part in parts[:-1]:
            at.append(at[-1] + part.shape[0])
        total = at[-1] + parts[-1].shape[0]
        if sent is None:
            sent = sum(
                jnp.pad(part, ((row, total - row - part.shape[0]), (0, 0)))
                for row, part in zip(at, parts)
            )
        return sent, lax.ppermute(sent, AXES, [(i, i ^ flips) for i in range(devices)]), at

    def widened(array):
        return jnp.pad(array, ((0, 0), (0, wide - flat_cells)))

    unit = layers * flat
    count = growth_reach_table.shape[0]
    frozen, label = widened(frozen_share_map), widened(crystal_label_map)
    joined = groups == 2 and wide == unit
    packed_rows = pl.pallas_call(
        pack_kernel,
        out_shape=[jax.ShapeDtypeStruct((9, unit), jnp.float32)]
        if joined
        else [
            jax.ShapeDtypeStruct((5, unit), jnp.float32),
            jax.ShapeDtypeStruct((4, wide), jnp.float32),
        ],
        in_specs=[HBM] * 5,
        out_specs=[VMEM] * (1 if joined else 2),
        scratch_shapes=[
            pltpu.VMEM(thermal_state_values.shape, jnp.float32),
            pltpu.VMEM(nodal_heating_input.shape, jnp.float32),
            pltpu.VMEM(thermal_kappa_values.shape, jnp.float32),
            pltpu.VMEM((2, 8, wide), jnp.float32),
            pltpu.VMEM((2, 8, wide), jnp.int32),
            pltpu.SemaphoreType.DMA((7,)),
        ],
        compiler_params=PARAMS,
        name="pack",
    )(*map(in_hbm, (thermal_state_values, nodal_heating_input, thermal_kappa_values, frozen, label)))
    held, edge_rows = packed_rows[0][:5], packed_rows[0][5:] if joined else packed_rows[1]
    high_edge, low_edge = edge_rows[:2], edge_rows[2:]

    brick_layers = edge_x // CPC
    need_y = (edge_y + CPC - 2) // CPC + 6
    width = up_to(need_y * 2 * plane, LANES)
    if 2 * width > flat:
        width = flat
    table_lanes = up_to(count, 2 * LANES)
    packed, label, frozen, faces = pl.pallas_call(
        functools.partial(faces_kernel, depth, flat_cells),
        out_shape=(
            jax.ShapeDtypeStruct((table_lanes // (2 * LANES), LANES), jnp.int32),
            jax.ShapeDtypeStruct((edge_x, wide), jnp.int32),
            jax.ShapeDtypeStruct((edge_x, wide), jnp.float32),
            jax.ShapeDtypeStruct((2 * depth, edge_x), jnp.float32),
        ),
        in_specs=[HBM] * 3,
        out_specs=[VMEM] * 4,
        scratch_shapes=[
            pltpu.VMEM((8, table_lanes), jnp.int32),
            pltpu.VMEM((growth_reach_table.shape[1], count), jnp.int32),
            pltpu.SemaphoreType.DMA((3,)),
        ],
        compiler_params=PARAMS,
        name="faces",
    )(in_hbm(growth_reach_table.T), in_hbm(label), in_hbm(frozen))
    gathered, faces_later = pl.pallas_call(
        functools.partial(cells_kernel, depth, flat_cells),
        out_shape=(
            jax.ShapeDtypeStruct((edge_x, wide), jnp.float32),
            jax.ShapeDtypeStruct((2 * depth, edge_x), jnp.float32),
        ),
        in_specs=[VMEM] * 4,
        out_specs=[VMEM] * 2,
        scratch_shapes=[pltpu.VMEM((edge_x, wide), jnp.int32)],
        compiler_params=PARAMS,
        name="cells",
    )(packed, label, frozen, faces)
    seeds = up_to(seed_site_slots.shape[0], LANES)
    short = seeds - seed_site_slots.shape[0]

    def sites(edges):
        return pl.pallas_call(
            functools.partial(sites_kernel, flat_cells),
            out_shape=(
                jax.ShapeDtypeStruct((edge_x, wide), jnp.float32),
                jax.ShapeDtypeStruct((2, wide), jnp.float32),
                jax.ShapeDtypeStruct((width, 5 * width), jnp.bfloat16),
                jax.ShapeDtypeStruct((2 * depth, edge_x), jnp.float32),
            ),
            in_specs=[VMEM] * 3 + [HBM] * 3,
            out_specs=[VMEM] * 4,
            scratch_shapes=[
                pltpu.VMEM((seeds // LANES, LANES), jnp.int32),
                pltpu.VMEM((seeds // LANES, LANES), jnp.int32),
                pltpu.SemaphoreType.DMA((3,)),
            ],
            compiler_params=PARAMS,
            name="sites",
        )(
            packed,
            edges,
            faces_later,
            in_hbm(jnp.pad(seed_site_slots, (0, short), constant_values=-1).reshape(-1, LANES)),
            in_hbm(jnp.pad(seed_crystal_label, (0, short)).reshape(-1, LANES)),
            in_hbm(jnp.asarray(spread_tables(width, plane))),
        )

    core, pair = me & 1, slab >> 1

    def packets(faces):
        return jnp.where(core == 1, faces[depth:], 0.0), jnp.where(core == 0, faces[:depth], 0.0)

    onward, backward = packets(faces)
    heat, edges = [held], None
    if groups > 2:
        ring = [(i, (i + 1) % groups) for i in range(groups)]
        edges = jnp.concatenate(
            [
                lax.ppermute(high_edge, "grp", ring),
                lax.ppermute(low_edge, "grp", [(j, i) for i, j in ring]),
            ]
        )
    moved, ends = 0, None
    as_face = lambda part: part.reshape(-1)[: depth * edge_x].reshape(depth, edge_x)
    for bit in reversed(range(1, devices.bit_length() - 1)):
        rides = 1 << bit < slabs
        low = (1 << (bit - 1)) - 1
        moves_on, moves_back = (pair & low) == low, (pair & low) == 0
        extra = []
        if groups == 2 and 1 << bit == slabs:
            extra = [lines(edge_rows, unit)]
        elif rides and low:
            extra = [lines(jnp.where(moves_on, onward, backward), unit)]
        elif rides:
            extra = [lines(onward, unit), lines(backward, unit)]
        first_sent = packed_rows[0] if joined and 1 << bit == slabs else None
        sent, got, at = exchanged(heat + extra, (1 << bit) | 1, first_sent)
        heat_rows = sum(part.shape[0] for part in heat)
        heat = heat + [got[:heat_rows]]
        parts = [got[row : row + part.shape[0]] for row, part in zip(at[len(at) - len(extra) :], extra)]
        if groups == 2 and 1 << bit == slabs:
            edges = parts[0].reshape(-1)[: 4 * wide].reshape(4, wide)
        elif rides and low:
            if moved == 0:
                onward, backward = packets(faces_later)
            onward = jnp.where(moves_on, as_face(parts[0]), onward)
            backward = jnp.where(moves_back, as_face(parts[0]), backward)
            moved += 1
        elif rides:
            onward, backward = as_face(parts[0]), as_face(parts[1])
        if edges is not None and ends is None:
            nucleation, ends, spread, faces_last = sites(edges)
    extra = [
        lines(jnp.where(core == 0, faces_last[depth:], faces_last[:depth]), unit),
        lines(jnp.where(core == 1, onward, backward), unit),
    ]
    if groups == 2:
        extra.append(lines(ends, unit))
    kept = jnp.where(core == 0, onward, backward)
    sent, got, at = exchanged(heat + extra, 1)
    heat_rows = sum(part.shape[0] for part in heat)
    at = at[len(heat) :]
    across, passing = (as_face(got[row : row + part.shape[0]]) for row, part in zip(at, extra[:2]))
    if groups == 2:
        ends = got[at[2] : at[2] + extra[2].shape[0]].reshape(-1)[: 2 * wide].reshape(2, wide)
    brick_layers = edge_x // CPC
    first_cell = slab * edge_y
    first_element = first_cell // CPC
    need_layers = brick_layers + 5
    whole = width == flat and 2 * up_to(need_layers, 8) > all_layers
    direct = whole and edge_x == unit and wide == unit and groups == 2
    if direct:
        inputs = (sent, got, got, got, got)
        sizes = (heat_rows, *at, devices)
        start_layer, start_y = group * brick_layers - 2, 0
        rows = min(up_to(need_layers, 8), all_layers)
    else:
        order = np.argsort(arrival_order(devices))
        blocks = jnp.concatenate([sent[:heat_rows], got[:heat_rows]], 0).reshape(devices, 5, layers, flat)
        blocks = jnp.take(blocks, jnp.asarray(order)[jnp.arange(devices) ^ me], axis=0)
        held = jnp.moveaxis(blocks, 1, 0).reshape(5, all_layers, flat)

        def window(first_layer, need_layers, first_element, need_elements):
            rows, lanes = up_to(need_layers, 8), up_to(need_elements * 2 * plane, LANES)
            part, start_layer, start_y = held, 0, 0
            if 2 * rows <= all_layers:
                start_layer = first_layer
                part = lax.dynamic_slice_in_dim(
                    jnp.concatenate([part, part[:, :rows]], 1),
                    jnp.remainder(start_layer, all_layers), rows, 1,
                )
            if 2 * lanes <= flat:
                start_y = 2 * first_element
                shifted = lambda v, by, size: lax.dynamic_slice_in_dim(
                    jnp.concatenate([v, v[..., :size]], -1), by, size, v.ndim - 1
                )
                start = jnp.remainder(first_element, rows_y // 2)
                part = jnp.concatenate(
                    [
                        shifted(part[:4], start * 2 * plane, lanes),
                        jnp.pad(
                            shifted(part[4:, :, :elements], start * HEX_COUNT_LATER, lanes // 4),
                            ((0, 0), (0, 0), (0, lanes - lanes // 4)),
                        ),
                    ],
                    0,
                )
            return part, start_layer, start_y

        state, start_layer, start_y = window(
            group * brick_layers - 2, need_layers, first_element - 2, need_y
        )
        inputs = (state, state, across, passing, ends)
        sizes = (0, 0, 0, 0, devices)
        rows = state.shape[1]
    if edge_y % CPC == 0 or CPC % edge_y == 0:
        covered = max(edge_y // CPC, 1)
    else:
        covered = (edge_y + CPC - 2) // CPC + 1
    group_lanes = up_to((2 * covered + 1) * plane, 16)
    if 5 * group_lanes > width:
        group_lanes = 0
    if isinstance(start_y, int):
        first_lane = lambda: lax.rem(
            lax.div(lax.axis_index("slab") * edge_y, CPC) * (2 * plane), width
        )
    else:
        first_lane = lambda: 4 * plane
    weave = weave_table(
        group_lanes, width, plane, depth, edge_y, first_cell % CPC, first_lane(), wide
    )

    def place(start, layer):
        if not isinstance(start, int):
            return lambda: 2
        return lambda: layer(lax.axis_index("grp"), lax.axis_index("slab"))

    def first_layer():
        return lax.rem(lax.axis_index("grp") * brick_layers + (all_layers - 2), all_layers)

    own_layer = lambda g, s: (g * slabs + s) * layers
    cell_row = place(start_layer, lambda g, s: g * brick_layers)
    own_row = place(start_layer, own_layer)
    if direct:
        own_row = lambda: lax.axis_index("slab") * layers + 2
    new_shape = jax.ShapeDtypeStruct((2 * layers, flat), jnp.float32)
    solid_shape = jax.ShapeDtypeStruct((edge_x, wide), jnp.float32)
    span = max(width, wide)
    results = pl.pallas_call(
        functools.partial(
            finish_kernel, plane, depth, flat_cells, layers, group_lanes, sizes,
            first_layer, own_row if whole else None, cell_row, first_lane,
            isinstance(start_layer, int),
        ),
        out_shape=(new_shape, solid_shape) if whole else (solid_shape,),
        in_specs=[VMEM] * 12,
        out_specs=(HBM,) * (1 + whole),
        scratch_shapes=[
            pltpu.VMEM((5, all_layers if direct else rows, width), jnp.float32),
            pltpu.VMEM((rows, span), jnp.float32),
            pltpu.VMEM((rows, span), jnp.float32),
            pltpu.VMEM((wide, edge_x), jnp.float32),
            pltpu.VMEM((edge_x, wide), jnp.float32),
            pltpu.VMEM((edge_x, wide), jnp.float32),
            pltpu.VMEM(new_shape.shape, jnp.float32),
            pltpu.SemaphoreType.DMA((CHUNKS + 1,)),
        ],
        compiler_params=PARAMS,
        name="finish",
    )(*inputs, kept, spread, weave, packed, gathered, nucleation, frozen)
    if whole:
        new_field, new_solid = results
    else:
        (new_solid,) = results
        state, start_layer, _ = window(me * layers - 2, layers + 4, 0, rows_y // 2)
        own_row = place(start_layer, own_layer)
        new_field = pl.pallas_call(
            functools.partial(heat_kernel, plane, layers, own_row),
            out_shape=new_shape,
            in_specs=[VMEM] * 2,
            out_specs=VMEM,
            scratch_shapes=[pltpu.VMEM(state.shape[1:], jnp.float32)] * 2,
            compiler_params=PARAMS,
            name="heat",
        )(state, jnp.asarray(spread_tables(flat, plane)))
    return new_field, new_solid[:, :flat_cells]


def solution(mesh):
    in_specs = (
        P(("grp", "slab"), None),
        P(("grp", "slab"), None),
        P(("grp", "slab"), None),
        P("grp", "slab"),
        P("grp", "slab"),
        P(),
        P(("grp", "slab")),
        P(("grp", "slab")),
    )
    out_specs = (P(("grp", "slab"), None), P("grp", "slab"))
    return jax.shard_map(body, mesh=mesh, in_specs=in_specs, out_specs=out_specs, check_vma=False)
```

```python
import functools

import jax
import jax.numpy as jnp
import numpy as np
from jax import lax
from jax.experimental import pallas as pl
from jax.experimental.pallas import tpu as pltpu
from jax.sharding import PartitionSpec as P

HEX_COUNT_LATER = 2
CPC = 8
LANES = 128
CHUNKS = 4
HIGHEST = lax.Precision.HIGHEST
STEP = 0.004
AXES = ("grp", "slab")
VMEM = pl.BlockSpec(memory_space=pltpu.VMEM)
HBM = pl.BlockSpec(memory_space=pltpu.HBM)
PARAMS = pltpu.CompilerParams(vmem_limit_bytes=48 * 1024 * 1024)


def in_hbm(array):
    return pltpu.with_memory_space_constraint(array, pltpu.HBM)


def up_to(value, unit):
    return -(-value // unit) * unit


def split_index(value, by):
    if by & (by - 1) == 0:
        return value >> (by.bit_length() - 1), value & (by - 1)
    quotient = lax.div(value, jnp.full_like(value, by))
    return quotient, value - quotient * by


def pack_kernel(
    state_ref, heat_ref, kappa_ref, frozen_ref, label_ref, held_ref, *refs
):
    state, heat, kappa, frozen, label, sems = refs[-6:]
    edge_ref = refs[0] if len(refs) > 6 else held_ref.at[5:9, :]
    layers, elements = kappa.shape
    flat = state.shape[1]
    edge_x = frozen_ref.shape[0]
    top, bottom = pl.ds(0, 8), pl.ds(edge_x - 8, 8)
    copies = started(
        [
            (state_ref, state),
            (heat_ref, heat),
            (kappa_ref, kappa),
            (frozen_ref.at[top, :], frozen.at[0]),
            (frozen_ref.at[bottom, :], frozen.at[1]),
            (label_ref.at[top, :], label.at[0]),
            (label_ref.at[bottom, :], label.at[1]),
        ],
        sems,
    )
    held_ref[4:5, :] = jnp.zeros((1, held_ref.shape[1]), jnp.float32)
    for copy in copies:
        copy.wait()
    for layer in range(layers):
        lanes = slice(layer * flat, (layer + 1) * flat)
        for parity in range(2):
            row = slice(2 * layer + parity, 2 * layer + parity + 1)
            held_ref[parity : parity + 1, lanes] = state[row, :]
            held_ref[2 + parity : 3 + parity, lanes] = heat[row, :]
        held_ref[4:5, layer * flat : layer * flat + elements] = kappa[layer : layer + 1, :]
    edge_ref[0:1, :] = frozen[1, 7:8, :]
    edge_ref[1:2, :] = label[1, 7:8, :].astype(jnp.float32)
    edge_ref[2:3, :] = frozen[0, 0:1, :]
    edge_ref[3:4, :] = label[0, 0:1, :].astype(jnp.float32)


def pick_codes(table_ref, labels):
    half = table_ref.shape[0]
    tile, lane = labels >> 7, labels & (LANES - 1)
    upper = tile >= half
    row = jnp.where(upper, tile - half, tile)
    found = jnp.zeros(labels.shape, jnp.int32)
    for r in range(half):
        line = jnp.broadcast_to(table_ref[r : r + 1, :], labels.shape)
        here = jnp.take_along_axis(line, lane, axis=1, mode="promise_in_bounds")
        found = jnp.where(row == r, here, found)
    return jnp.where(upper, found >> 12, found) & 4095


def level(code, direction):
    return (((code >> (2 * direction)) & 3) + 1).astype(jnp.float32)


def started(pairs, sems):
    copies = [pltpu.make_async_copy(*pair, sems.at[i]) for i, pair in enumerate(pairs)]
    for copy in copies:
        copy.start()
    return copies


def faces_kernel(
    depth, flat, table_hbm, label_hbm, frozen_hbm,
    packed_ref, label_ref, frozen_ref, faces_ref, table_ref, sems,
):
    count = table_ref.shape[1]
    half = packed_ref.shape[0]
    edge_x = frozen_ref.shape[0]
    chunk = up_to(half, 4) // 4 * LANES
    order = [at for low in range(0, half * LANES, chunk) for at in (low, low + half * LANES)]
    order = [at for at in order if at < count]
    parts = [pl.ds(at, min(chunk, count - at)) for at in order]
    get_label, get_frozen, *get_table = started(
        [(label_hbm, label_ref), (frozen_hbm, frozen_ref)]
        + [(table_hbm.at[:, part], table_ref.at[:, part]) for part in parts],
        sems,
    )
    get_label.wait()
    get_frozen.wait()
    label = jnp.transpose(label_ref[...])
    label = jnp.concatenate([label[0:depth], label[flat - depth : flat]], 0)
    frozen = jnp.transpose(frozen_ref[...])
    frozen = 0.25 * jnp.concatenate([frozen[0:depth], frozen[flat - depth : flat]], 0)
    directions = table_ref.shape[0]
    place = 2 * lax.broadcasted_iota(jnp.int32, (directions, LANES), 0)

    def tile(number):
        size = max(min(LANES, count - number * LANES), 0)
        here = table_ref[:, number * LANES : number * LANES + size] if size else None
        if size == LANES:
            return here
        blank = jnp.ones((directions, LANES - size), jnp.int32)
        return jnp.concatenate([here, blank], 1) if size else blank

    waiting = dict(zip(order, get_table))
    for r in range(half):
        for at in (r * LANES, (r + half) * LANES):
            if at in waiting:
                waiting.pop(at).wait()
        bits = ((tile(r) - 1) << place) | ((tile(r + half) - 1) << (place + 12))
        packed_ref[r : r + 1, :] = jnp.sum(bits, axis=0, keepdims=True)
    short = -edge_x % LANES
    if short:
        label = jnp.concatenate([label, jnp.zeros((2 * depth, short), jnp.int32)], 1)
    for t in range(up_to(edge_x, LANES) // LANES):
        size = min(LANES, edge_x - t * LANES)
        lanes = slice(t * LANES, t * LANES + size)
        for part in range(2 * depth // 8):
            rows = slice(part * 8, part * 8 + 8)
            code = pick_codes(packed_ref, label[rows, t * LANES : (t + 1) * LANES])[:, :size]
            faces_ref[rows, lanes] = frozen[rows, lanes] * level(code, 2 if part * 8 < depth else 3)


def cells_kernel(
    depth, flat, packed_ref, label_ref, frozen_ref, faces_ref, gathered_ref, onward_ref, code_ref
):
    onward_ref[...] = faces_ref[...]
    edge_x, wide = frozen_ref.shape

    def look_up(chunk, carry):
        rows = pl.ds(pl.multiple_of(chunk * 8, 8), 8)
        for t in range(wide // LANES):
            lanes = pl.ds(t * LANES, LANES)
            code_ref[rows, lanes] = pick_codes(packed_ref, label_ref[rows, lanes])
        return carry

    lax.fori_loop(0, edge_x // 8, look_up, 0, unroll=16)
    frozen = frozen_ref[...] * 0.25
    code = code_ref[...]
    shares = [frozen * level(code, d) for d in range(6)]
    line_x = lax.broadcasted_iota(jnp.int32, (edge_x, wide), 0)
    lane = lax.broadcasted_iota(jnp.int32, (edge_x, wide), 1)
    deep = split_index(lane, depth)[1]
    total = jnp.where(line_x == edge_x - 1, 0.0, pltpu.roll(shares[0], edge_x - 1, 0))
    total += jnp.where(line_x == 0, 0.0, pltpu.roll(shares[1], 1, 0))
    total += jnp.where(lane >= flat - depth, 0.0, pltpu.roll(shares[2], wide - depth, 1))
    total += jnp.where(lane < depth, 0.0, pltpu.roll(shares[3], depth, 1))
    total += jnp.where(
        deep == depth - 1, pltpu.roll(shares[4], depth - 1, 1), pltpu.roll(shares[4], wide - 1, 1)
    )
    total += jnp.where(
        deep == 0, pltpu.roll(shares[5], wide - (depth - 1), 1), pltpu.roll(shares[5], 1, 1)
    )
    gathered_ref[...] = total


def sites_kernel(
    flat, packed_ref, edge_ref, faces_ref, slot_hbm, seed_hbm, spread_hbm,
    nucleation_ref, ends_ref, spread_ref, onward_ref, slot_ref, seed_ref, sems,
):
    copies = started([(slot_hbm, slot_ref), (seed_hbm, seed_ref), (spread_hbm, spread_ref)], sems)
    onward_ref[...] = faces_ref[...]
    edge_x, wide = nucleation_ref.shape
    for t in range(wide // LANES):
        lanes = slice(t * LANES, (t + 1) * LANES)
        rough = jnp.concatenate([edge_ref[:, lanes], jnp.zeros((4, LANES), jnp.float32)], 0)
        codes = pick_codes(packed_ref, rough.astype(jnp.int32))
        ends_ref[0:1, lanes] = rough[0:1] * level(codes[1:2], 1) * 0.25
        ends_ref[1:2, lanes] = rough[2:3] * level(codes[3:4], 0) * 0.25
    for copy in copies:
        copy.wait()
    sites = seed_ref.shape[0]
    codes = pick_codes(packed_ref, seed_ref[...])
    worth = sum(level(codes, d) for d in range(6))
    site_x, site_lane = split_index(slot_ref[...], flat)
    at_x = lax.broadcasted_iota(jnp.int32, (edge_x, LANES), 0)
    at_lane = lax.broadcasted_iota(jnp.int32, (wide, LANES), 0)
    added = jnp.zeros((edge_x, wide), jnp.float32)
    for r in range(sites):
        left = jnp.where(at_x == site_x[r : r + 1], worth[r : r + 1], 0.0).astype(jnp.bfloat16)
        right = jnp.where(at_lane == site_lane[r : r + 1], 1.0, 0.0).astype(jnp.bfloat16)
        added += lax.dot_general(
            left, right, (((1,), (1,)), ((), ())), preferred_element_type=jnp.float32
        )
    nucleation_ref[...] = added * (1.0 / 6.0)


def spread_tables(width, plane):
    rows_y, deep = width // plane, plane // 2

    def tables(count):
        spread, after, before = (np.zeros((count // 2, count), np.float32) for _ in range(3))
        for element in range(count // 2):
            for local, weight in enumerate((1, 4, 1)):
                spread[element, (2 * element + local) % count] += weight
            for local in range(2):
                after[element, (2 * element + local) % count] += 1
                before[element, (2 * element + local + 1) % count] += 1
        return spread, after, before

    spread_y, after_y, before_y = tables(rows_y)
    spread_z, after_z, before_z = tables(plane)
    full = [
        np.kron(spread_y, spread_z),
        np.kron(after_y, spread_z),
        np.kron(before_y, spread_z),
        np.kron(spread_y, after_z),
        np.kron(spread_y, before_z),
    ]
    half = lambda count: np.where(np.arange(count) % 2 == 1, 0.5, 1.0)
    inverse = 27.0 * np.kron(half(rows_y), half(plane))
    out = np.zeros((width, 5 * width), jnp.bfloat16)
    out[: 3 * (width // 4)] = np.concatenate([np.concatenate([t * inverse for t in full], 1)] * 3, 0)
    return out


def pieces(values):
    out = []
    for _ in range(3):
        out.append(values.astype(jnp.bfloat16).astype(jnp.float32))
        values = values - out[-1]
    return out


def advance(plane, even, odd, heat_even, heat_odd, kappa, spread):
    rows, width = even.shape
    up = lambda v: pltpu.roll(v, rows - 1, 0)
    down = lambda v: pltpu.roll(v, 1, 0)
    turn = lambda v, by: pltpu.roll(v, by % width, 1)
    lane = lax.broadcasted_iota(jnp.int32, (rows, width), 1)
    row_y, deep = split_index(lane, plane)
    even_y, even_z = row_y & 1 == 0, deep & 1 == 0
    first, second, third = pieces(kappa)
    joined = first + turn(second, width // 4) + turn(third, 2 * (width // 4))
    lines = jnp.dot(joined.astype(jnp.bfloat16), spread, preferred_element_type=jnp.float32)
    lines = lines * (STEP / 108.0)
    along_x, *others = (lines[:, i * width : (i + 1) * width] for i in range(5))
    behind_x = down(along_x)
    scale = STEP * 27.0 * jnp.where(even_y, 1.0, 0.5) * jnp.where(even_z, 1.0, 0.5)
    heat_even, heat_odd = scale * heat_even, (0.5 * scale) * heat_odd

    def in_plane(parts):
        after_y, before_y, after_z, before_z = parts
        own = jnp.where(even_y, 7.0 * (after_y + before_y), 16.0 * after_y)
        own = own + jnp.where(even_z, 7.0 * (after_z + before_z), 16.0 * after_z)
        far = [jnp.where(even_y, v, 0.0) for v in parts[:2]] + [
            jnp.where(even_z, v, 0.0) for v in parts[2:]
        ]
        return own, [-8.0 * v for v in parts], far

    own_even, near_even, far_even = in_plane([v + down(v) for v in others])
    own_odd, near_odd, far_odd = in_plane([2.0 * v for v in others])
    own_even = own_even + 7.0 * (along_x + behind_x)
    own_odd = own_odd + 8.0 * along_x
    near_x, near_behind, near_odd_x = -8.0 * along_x, -8.0 * behind_x, -4.0 * along_x

    def moved(values, by):
        if by > 0:
            return jnp.where(deep + by >= plane, turn(values, plane - by), turn(values, -by))
        return jnp.where(deep + by < 0, turn(values, -by - plane), turn(values, -by))

    def neighbours(values, near, far):
        ahead_y, back_y = turn(values, -plane), turn(values, plane)
        total = near[0] * ahead_y + near[1] * back_y
        total += near[2] * moved(values, 1) + near[3] * moved(values, -1)
        total += far[0] * turn(values, -2 * plane) + far[1] * turn(values, 2 * plane)
        if plane == 4:
            return total + (far[2] + far[3]) * moved(values, 2)
        return total + far[2] * moved(values, 2) + far[3] * moved(values, -2)

    def change(v_even, v_odd):
        following = up(v_even)
        k_even = own_even * v_even + along_x * following + behind_x * down(v_even)
        k_even += near_x * v_odd + near_behind * down(v_odd)
        k_odd = own_odd * v_odd + near_odd_x * (v_even + following)
        k_even += neighbours(v_even, near_even, far_even)
        k_odd += neighbours(v_odd, near_odd, far_odd)
        return heat_even - k_even, heat_odd - k_odd

    one_even, one_odd = change(even, odd)
    two_even, two_odd = change(even + one_even, odd + one_odd)
    return even + 0.5 * (one_even + two_even), odd + 0.5 * (one_odd + two_odd)


def heat_kernel(plane, layers, first_row, state_ref, spread_ref, new_ref, even_ref, odd_ref):
    even, odd = advance(plane, *(state_ref[i] for i in range(5)), spread_ref[...])
    even_ref[...] = even
    odd_ref[...] = odd
    start = first_row()
    for layer in range(layers):
        new_ref[2 * layer : 2 * layer + 1, :] = even_ref[pl.ds(start + layer, 1), :]
        new_ref[2 * layer + 1 : 2 * layer + 2, :] = odd_ref[pl.ds(start + layer, 1), :]


def basis(step):
    point = (step.astype(jnp.float32) + 0.5) / CPC
    return (
        2.0 * (point - 0.5) * (point - 1.0),
        -4.0 * point * (point - 1.0),
        2.0 * point * (point - 0.5),
    )


def finish_kernel(
    plane, depth, flat, layers, group_lanes, sizes, first_layer, first_row, cell_row, first_lane,
    wraps, mine_ref, theirs_ref, across_ref, passing_ref, edge_ref, kept_ref, spread_ref, weave_ref,
    packed_ref, gathered_ref, nucleation_ref, frozen_ref, *refs,
):
    solid_out, state_ref, even_ref, odd_ref, side_ref, extra_ref, solid_ref, new_ref, sems = refs[-9:]
    edge_x, wide = frozen_ref.shape
    _, all_rows, width = state_ref.shape
    rows = even_ref.shape[0]
    heat_rows, across_row, passing_row, edge_row = sizes
    core = lax.axis_index("slab") & 1
    if heat_rows:
        slabs = lax.axis_size("slab")
        me = lax.axis_index("grp") * slabs + lax.axis_index("slab")
        state_ref[:, rows - 8 : rows, :] = jnp.zeros((5, 8, width), jnp.float32)
        numbers = [me ^ off for off in arrival_order(slabs)[: slabs // 2]]
        numbers += beyond_order(me, slabs)
        numbers += [me ^ 1 ^ off for off in arrival_order(slabs)[: slabs // 2]]
        numbers += beyond_order(me ^ 1, slabs)
        blocks = len(numbers) // 2
        for p, number in enumerate(numbers):
            source, block = (mine_ref, p) if p < blocks else (theirs_ref, p - blocks)
            row = lax.rem(number * layers + (all_rows - first_layer()), all_rows)
            for c in range(5):
                for layer in range(layers):
                    state_ref[c, pl.ds(row + layer, 1), :] = source[
                        block * 5 + c : block * 5 + c + 1, layer * width : (layer + 1) * width
                    ]
        state = [state_ref[i, 0:rows, :] for i in range(5)]
    else:
        state = [mine_ref[i] for i in range(5)]
    side_ref[...] = jnp.zeros(side_ref.shape, jnp.float32)
    there = jnp.where(core == 0, 0, flat - depth)
    side_ref[pl.ds(pl.multiple_of(there, 8), depth), :] = (
        kept_ref[...] + passing_ref[passing_row : passing_row + depth, :]
    )
    side_ref[pl.ds(pl.multiple_of(flat - depth - there, 8), depth), :] = across_ref[
        across_row : across_row + depth, :
    ]
    extra_ref[...] = gathered_ref[...] + jnp.transpose(side_ref[...])
    extra_ref[0:1, :] += edge_ref[edge_row : edge_row + 1, 0:wide]
    extra_ref[edge_x - 1 : edge_x, :] += edge_ref[edge_row + 1 : edge_row + 2, 0:wide]
    even, odd = advance(plane, *state, spread_ref[...])
    if first_row is not None:
        even_ref[:, 0:width] = even
        odd_ref[:, 0:width] = odd
        start = first_row()
        for layer in range(layers):
            new_ref[2 * layer : 2 * layer + 1, :] = even_ref[pl.ds(start + layer, 1), 0:width]
            new_ref[2 * layer + 1 : 2 * layer + 2, :] = odd_ref[pl.ds(start + layer, 1), 0:width]
        new_copy = pltpu.make_async_copy(new_ref, refs[0], sems.at[CHUNKS])
        new_copy.start()
    both = jnp.concatenate([even, odd], 0)
    if group_lanes:
        lane = lax.broadcasted_iota(jnp.int32, both.shape, 1)
        first_node = first_lane()
        inside = (lane >= first_node) & (lane < first_node + group_lanes)
        inside |= lane + width < first_node + group_lanes
        first, second, third = pieces(jnp.where(inside, both, 0.0))
        joined = first
        for i, piece in enumerate((second, third, first, second)):
            joined = joined + pltpu.roll(piece, (i + 1) * group_lanes, 1)
    else:
        first, second, third = pieces(both)
        joined = jnp.concatenate([first, second, third, first, second], 1)
    woven = jnp.dot(
        joined.astype(jnp.bfloat16), weave_ref[...], preferred_element_type=jnp.float32
    )
    even_ref[:, 0:wide] = woven[:rows]
    odd_ref[:, 0:wide] = woven[rows:]
    first, middle, last = basis(lax.broadcasted_iota(jnp.int32, (CPC, wide), 0))
    base = cell_row()
    elements = edge_x // CPC
    copies = []
    for a in range(elements):
        cells = slice(a * CPC, (a + 1) * CPC)
        later = base + (a + 1)
        if wraps:
            later = lax.rem(later, rows)
        temperature = (
            first * even_ref[pl.ds(base + a, 1), 0:wide]
            + middle * odd_ref[pl.ds(base + a, 1), 0:wide]
            + last * even_ref[pl.ds(later, 1), 0:wide]
        )
        under = jnp.maximum(-temperature, 0.0)
        rate = under * (under * extra_ref[cells, :] + nucleation_ref[cells, :])
        frozen = frozen_ref[cells, :]
        solid_ref[cells, :] = frozen + (1.0 - frozen) * (1.0 - jnp.exp(-rate))
        done = (a + 1) * CHUNKS // elements
        if done > len(copies):
            low = copies[-1][1] if copies else 0
            part = pl.ds(low, (a + 1) * CPC - low)
            copy = pltpu.make_async_copy(
                solid_ref.at[part, :], solid_out.at[part, :], sems.at[len(copies)]
            )
            copy.start()
            copies.append((copy, (a + 1) * CPC))
    for copy, _ in copies:
        copy.wait()
    if first_row is not None:
        new_copy.wait()


def weave_table(group_lanes, width, plane, depth, edge_y, first_step, first_node, wide):
    span = group_lanes or width
    row = jnp.arange(width if group_lanes else 5 * width)[:, None]
    cell = jnp.arange(wide)[None, :]
    if group_lanes:
        row = (row - first_node) % width
        copy, node = row // span, row % span
    else:
        copy, node = row // span, (row % span - first_node) % width
    cell_y, cell_z = first_step + cell // depth, cell % depth
    step_y = node // plane - 2 * (cell_y // CPC)
    step_z = (node % plane - 2 * (cell_z // CPC)) % plane
    take = lambda step, at: sum(jnp.where(step == i, v, 0.0) for i, v in enumerate(basis(at % CPC)))
    full = take(step_y, cell_y) * take(step_z, cell_z)
    high = jnp.floor(full * 128.0) * (1.0 / 128.0)
    part = jnp.where(copy < 3, high, full - high)
    return jnp.where((copy < 5) & (cell < edge_y * depth), part, 0.0).astype(jnp.bfloat16)


def beyond_order(me, slabs):
    top = slabs.bit_length() - 2

    def kept(number, bit):
        if bit > top:
            return [number ^ slabs ^ 1]
        flips = (1 << bit) | 1
        if bit == 1:
            return kept(number, 2) + kept(number ^ flips, 2)
        return [picked(number, bit), picked(number ^ flips, bit)]

    def picked(number, bit):
        held = kept(number, bit + 1)
        if len(held) == 1:
            return held[0]
        same = ((number >> bit) ^ (number >> (bit + 1))) & 1 == 0
        return jnp.where(same, held[0], held[1])

    return kept(me, 1)


def arrival_order(devices):
    offs = [0]
    for bit in reversed(range(1, devices.bit_length() - 1)):
        offs += [off ^ (1 << bit) ^ 1 for off in offs]
    return offs + [off ^ 1 for off in offs]


def lines(values, width):
    flat = values.reshape(-1)
    return jnp.pad(flat, (0, -flat.shape[0] % width)).reshape(-1, width)


def body(
    thermal_state_values,
    thermal_kappa_values,
    nodal_heating_input,
    frozen_share_map,
    crystal_label_map,
    growth_reach_table,
    seed_site_slots,
    seed_crystal_label,
):
    groups, slabs = lax.axis_size("grp"), lax.axis_size("slab")
    devices = groups * slabs
    group, slab = lax.axis_index("grp"), lax.axis_index("slab")
    me = group * slabs + slab
    layers, elements = thermal_kappa_values.shape
    plane = 2 * HEX_COUNT_LATER
    depth = CPC * HEX_COUNT_LATER
    flat = thermal_state_values.shape[1]
    rows_y = flat // plane
    edge_x, flat_cells = frozen_share_map.shape
    edge_y = flat_cells // depth
    wide = up_to(flat_cells, LANES)
    all_layers = layers * devices

    def exchanged(parts, flips, sent=None):
        at = [0]
        for part in parts[:-1]:
            at.append(at[-1] + part.shape[0])
        total = at[-1] + parts[-1].shape[0]
        if sent is None:
            sent = sum(
                jnp.pad(part, ((row, total - row - part.shape[0]), (0, 0)))
                for row, part in zip(at, parts)
            )
        return sent, lax.ppermute(sent, AXES, [(i, i ^ flips) for i in range(devices)]), at

    def widened(array):
        return jnp.pad(array, ((0, 0), (0, wide - flat_cells)))

    unit = layers * flat
    count = growth_reach_table.shape[0]
    frozen, label = widened(frozen_share_map), widened(crystal_label_map)
    joined = groups == 2 and wide == unit
    packed_rows = pl.pallas_call(
        pack_kernel,
        out_shape=[jax.ShapeDtypeStruct((9, unit), jnp.float32)]
        if joined
        else [
            jax.ShapeDtypeStruct((5, unit), jnp.float32),
            jax.ShapeDtypeStruct((4, wide), jnp.float32),
        ],
        in_specs=[HBM] * 5,
        out_specs=[VMEM] * (1 if joined else 2),
        scratch_shapes=[
            pltpu.VMEM(thermal_state_values.shape, jnp.float32),
            pltpu.VMEM(nodal_heating_input.shape, jnp.float32),
            pltpu.VMEM(thermal_kappa_values.shape, jnp.float32),
            pltpu.VMEM((2, 8, wide), jnp.float32),
            pltpu.VMEM((2, 8, wide), jnp.int32),
            pltpu.SemaphoreType.DMA((7,)),
        ],
        compiler_params=PARAMS,
        name="pack",
    )(*map(in_hbm, (thermal_state_values, nodal_heating_input, thermal_kappa_values, frozen, label)))
    held, edge_rows = packed_rows[0][:5], packed_rows[0][5:] if joined else packed_rows[1]
    high_edge, low_edge = edge_rows[:2], edge_rows[2:]

    brick_layers = edge_x // CPC
    need_y = (edge_y + CPC - 2) // CPC + 6
    width = up_to(need_y * 2 * plane, LANES)
    if 2 * width > flat:
        width = flat
    need_layers = brick_layers + 5
    whole = width == flat and 2 * up_to(need_layers, 8) > all_layers
    direct = whole and edge_x == unit and wide == unit and groups == 2 and slabs > 2
    table_lanes = up_to(count, 2 * LANES)
    packed, label, frozen, faces = pl.pallas_call(
        functools.partial(faces_kernel, depth, flat_cells),
        out_shape=(
            jax.ShapeDtypeStruct((table_lanes // (2 * LANES), LANES), jnp.int32),
            jax.ShapeDtypeStruct((edge_x, wide), jnp.int32),
            jax.ShapeDtypeStruct((edge_x, wide), jnp.float32),
            jax.ShapeDtypeStruct((2 * depth, edge_x), jnp.float32),
        ),
        in_specs=[HBM] * 3,
        out_specs=[VMEM] * 4,
        scratch_shapes=[
            pltpu.VMEM((growth_reach_table.shape[1], count), jnp.int32),
            pltpu.SemaphoreType.DMA((10,)),
        ],
        compiler_params=PARAMS,
        name="faces",
    )(in_hbm(growth_reach_table.T), in_hbm(label), in_hbm(frozen))
    gathered, faces_later = pl.pallas_call(
        functools.partial(cells_kernel, depth, flat_cells),
        out_shape=(
            jax.ShapeDtypeStruct((edge_x, wide), jnp.float32),
            jax.ShapeDtypeStruct((2 * depth, edge_x), jnp.float32),
        ),
        in_specs=[VMEM] * 4,
        out_specs=[VMEM] * 2,
        scratch_shapes=[pltpu.VMEM((edge_x, wide), jnp.int32)],
        compiler_params=PARAMS,
        name="cells",
    )(packed, label, frozen, faces)
    seeds = up_to(seed_site_slots.shape[0], LANES)
    short = seeds - seed_site_slots.shape[0]

    def sites(edges):
        return pl.pallas_call(
            functools.partial(sites_kernel, flat_cells),
            out_shape=(
                jax.ShapeDtypeStruct((edge_x, wide), jnp.float32),
                jax.ShapeDtypeStruct((2, wide), jnp.float32),
                jax.ShapeDtypeStruct((width, 5 * width), jnp.bfloat16),
                jax.ShapeDtypeStruct((2 * depth, edge_x), jnp.float32),
            ),
            in_specs=[VMEM] * 3 + [HBM] * 3,
            out_specs=[VMEM] * 4,
            scratch_shapes=[
                pltpu.VMEM((seeds // LANES, LANES), jnp.int32),
                pltpu.VMEM((seeds // LANES, LANES), jnp.int32),
                pltpu.SemaphoreType.DMA((3,)),
            ],
            compiler_params=PARAMS,
            name="sites",
        )(
            packed,
            edges,
            faces_later,
            in_hbm(jnp.pad(seed_site_slots, (0, short), constant_values=-1).reshape(-1, LANES)),
            in_hbm(jnp.pad(seed_crystal_label, (0, short)).reshape(-1, LANES)),
            in_hbm(jnp.asarray(spread_tables(width, plane))),
        )

    core, pair = me & 1, slab >> 1

    def packets(faces):
        return jnp.where(core == 1, faces[depth:], 0.0), jnp.where(core == 0, faces[:depth], 0.0)

    onward, backward = packets(faces)
    heat, edges = [held], None
    beyond = []
    if groups > 2:
        ring = [(i, (i + 1) % groups) for i in range(groups)]
        edges = jnp.concatenate(
            [
                lax.ppermute(high_edge, "grp", ring),
                lax.ppermute(low_edge, "grp", [(j, i) for i, j in ring]),
            ]
        )
    moved, ends = 0, None
    as_face = lambda part: part.reshape(-1)[: depth * edge_x].reshape(depth, edge_x)
    for bit in reversed(range(1, devices.bit_length() - 1)):
        rides = 1 << bit < slabs
        low = (1 << (bit - 1)) - 1
        moves_on, moves_back = (pair & low) == low, (pair & low) == 0
        extra = []
        if groups == 2 and 1 << bit == slabs:
            extra = [lines(edge_rows, unit)]
        elif rides and low:
            extra = [lines(jnp.where(moves_on, onward, backward), unit)]
        elif rides:
            extra = [lines(onward, unit), lines(backward, unit)]
        first_sent = packed_rows[0] if joined and 1 << bit == slabs else None
        if bit > 1 and len(beyond) == 2:
            same = ((me >> bit) ^ (me >> (bit + 1))) & 1 == 0
            beyond = [jnp.where(same, *beyond)]
        sent, got, at = exchanged(heat + beyond + extra, (1 << bit) | 1, first_sent)
        heat_rows = sum(part.shape[0] for part in heat)
        if direct and 1 << bit == slabs:
            beyond = [got[:heat_rows]]
        else:
            beyond = beyond + [
                got[row : row + part.shape[0]] for row, part in zip(at[len(heat) :], beyond)
            ]
            heat = heat + [got[:heat_rows]]
        parts = [got[row : row + part.shape[0]] for row, part in zip(at[len(at) - len(extra) :], extra)]
        if groups == 2 and 1 << bit == slabs:
            edges = parts[0].reshape(-1)[: 4 * wide].reshape(4, wide)
        elif rides and low:
            if moved == 0:
                onward, backward = packets(faces_later)
            onward = jnp.where(moves_on, as_face(parts[0]), onward)
            backward = jnp.where(moves_back, as_face(parts[0]), backward)
            moved += 1
        elif rides:
            onward, backward = as_face(parts[0]), as_face(parts[1])
        if edges is not None and ends is None:
            nucleation, ends, spread, faces_last = sites(edges)
    extra = [
        lines(jnp.where(core == 0, faces_last[depth:], faces_last[:depth]), unit),
        lines(jnp.where(core == 1, onward, backward), unit),
    ]
    if groups == 2:
        extra.append(lines(ends, unit))
    kept = jnp.where(core == 0, onward, backward)
    heat = heat + beyond
    sent, got, at = exchanged(heat + extra, 1)
    heat_rows = sum(part.shape[0] for part in heat)
    at = at[len(heat) :]
    across, passing = (as_face(got[row : row + part.shape[0]]) for row, part in zip(at, extra[:2]))
    if groups == 2:
        ends = got[at[2] : at[2] + extra[2].shape[0]].reshape(-1)[: 2 * wide].reshape(2, wide)
    first_cell = slab * edge_y
    first_element = first_cell // CPC
    if direct:
        inputs = (sent, got, got, got, got)
        sizes = (heat_rows, *at)
        start_layer, start_y = group * brick_layers - 2, 0
        rows = min(up_to(need_layers, 8), all_layers)
    else:
        order = np.argsort(arrival_order(devices))
        blocks = jnp.concatenate([sent[:heat_rows], got[:heat_rows]], 0).reshape(devices, 5, layers, flat)
        blocks = jnp.take(blocks, jnp.asarray(order)[jnp.arange(devices) ^ me], axis=0)
        held = jnp.moveaxis(blocks, 1, 0).reshape(5, all_layers, flat)

        def window(first_layer, need_layers, first_element, need_elements):
            rows, lanes = up_to(need_layers, 8), up_to(need_elements * 2 * plane, LANES)
            part, start_layer, start_y = held, 0, 0
            if 2 * rows <= all_layers:
                start_layer = first_layer
                part = lax.dynamic_slice_in_dim(
                    jnp.concatenate([part, part[:, :rows]], 1),
                    jnp.remainder(start_layer, all_layers), rows, 1,
                )
            if 2 * lanes <= flat:
                start_y = 2 * first_element
                shifted = lambda v, by, size: lax.dynamic_slice_in_dim(
                    jnp.concatenate([v, v[..., :size]], -1), by, size, v.ndim - 1
                )
                start = jnp.remainder(first_element, rows_y // 2)
                part = jnp.concatenate(
                    [
                        shifted(part[:4], start * 2 * plane, lanes),
                        jnp.pad(
                            shifted(part[4:, :, :elements], start * HEX_COUNT_LATER, lanes // 4),
                            ((0, 0), (0, 0), (0, lanes - lanes // 4)),
                        ),
                    ],
                    0,
                )
            return part, start_layer, start_y

        state, start_layer, start_y = window(
            group * brick_layers - 2, need_layers, first_element - 2, need_y
        )
        inputs = (state, state, across, passing, ends)
        sizes = (0, 0, 0, 0)
        rows = state.shape[1]
    if edge_y % CPC == 0 or CPC % edge_y == 0:
        covered = max(edge_y // CPC, 1)
    else:
        covered = (edge_y + CPC - 2) // CPC + 1
    group_lanes = up_to((2 * covered + 1) * plane, 16)
    if 5 * group_lanes > width:
        group_lanes = 0
    if isinstance(start_y, int):
        first_lane = lambda: lax.rem(
            lax.div(lax.axis_index("slab") * edge_y, CPC) * (2 * plane), width
        )
    else:
        first_lane = lambda: 4 * plane
    weave = weave_table(
        group_lanes, width, plane, depth, edge_y, first_cell % CPC, first_lane(), wide
    )

    def place(start, layer):
        if not isinstance(start, int):
            return lambda: 2
        return lambda: layer(lax.axis_index("grp"), lax.axis_index("slab"))

    def first_layer():
        return lax.rem(lax.axis_index("grp") * brick_layers + (all_layers - 2), all_layers)

    own_layer = lambda g, s: (g * slabs + s) * layers
    cell_row = place(start_layer, lambda g, s: g * brick_layers)
    own_row = place(start_layer, own_layer)
    if direct:
        own_row = lambda: lax.axis_index("slab") * layers + 2
    new_shape = jax.ShapeDtypeStruct((2 * layers, flat), jnp.float32)
    solid_shape = jax.ShapeDtypeStruct((edge_x, wide), jnp.float32)
    span = max(width, wide)
    results = pl.pallas_call(
        functools.partial(
            finish_kernel, plane, depth, flat_cells, layers, group_lanes, sizes,
            first_layer, own_row if whole else None, cell_row, first_lane,
            isinstance(start_layer, int),
        ),
        out_shape=(new_shape, solid_shape) if whole else (solid_shape,),
        in_specs=[VMEM] * 12,
        out_specs=(HBM,) * (1 + whole),
        scratch_shapes=[
            pltpu.VMEM((5, all_layers if direct else rows, width), jnp.float32),
            pltpu.VMEM((rows, span), jnp.float32),
            pltpu.VMEM((rows, span), jnp.float32),
            pltpu.VMEM((wide, edge_x), jnp.float32),
            pltpu.VMEM((edge_x, wide), jnp.float32),
            pltpu.VMEM((edge_x, wide), jnp.float32),
            pltpu.VMEM(new_shape.shape, jnp.float32),
            pltpu.SemaphoreType.DMA((CHUNKS + 1,)),
        ],
        compiler_params=PARAMS,
        name="finish",
    )(*inputs, kept, spread, weave, packed, gathered, nucleation, frozen)
    if whole:
        new_field, new_solid = results
    else:
        (new_solid,) = results
        state, start_layer, _ = window(me * layers - 2, layers + 4, 0, rows_y // 2)
        own_row = place(start_layer, own_layer)
        new_field = pl.pallas_call(
            functools.partial(heat_kernel, plane, layers, own_row),
            out_shape=new_shape,
            in_specs=[VMEM] * 2,
            out_specs=VMEM,
            scratch_shapes=[pltpu.VMEM(state.shape[1:], jnp.float32)] * 2,
            compiler_params=PARAMS,
            name="heat",
        )(state, jnp.asarray(spread_tables(flat, plane)))
    return new_field, new_solid[:, :flat_cells]


def solution(mesh):
    in_specs = (
        P(("grp", "slab"), None),
        P(("grp", "slab"), None),
        P(("grp", "slab"), None),
        P("grp", "slab"),
        P("grp", "slab"),
        P(),
        P(("grp", "slab")),
        P(("grp", "slab")),
    )
    out_specs = (P(("grp", "slab"), None), P("grp", "slab"))
    return jax.shard_map(body, mesh=mesh, in_specs=in_specs, out_specs=out_specs, check_vma=False)
```

```python
import functools

import jax
import jax.numpy as jnp
import numpy as np
from jax import lax
from jax.experimental import pallas as pl
from jax.experimental.pallas import tpu as pltpu
from jax.sharding import PartitionSpec as P

HEX_COUNT_LATER = 2
CPC = 8
LANES = 128
CHUNKS = 4
HIGHEST = lax.Precision.HIGHEST
STEP = 0.004
AXES = ("grp", "slab")
VMEM = pl.BlockSpec(memory_space=pltpu.VMEM)
HBM = pl.BlockSpec(memory_space=pltpu.HBM)
PARAMS = pltpu.CompilerParams(vmem_limit_bytes=48 * 1024 * 1024)


def in_hbm(array):
    return pltpu.with_memory_space_constraint(array, pltpu.HBM)


def up_to(value, unit):
    return -(-value // unit) * unit


def split_index(value, by):
    if by & (by - 1) == 0:
        return value >> (by.bit_length() - 1), value & (by - 1)
    quotient = lax.div(value, jnp.full_like(value, by))
    return quotient, value - quotient * by


def pieces(values):
    out = []
    for _ in range(3):
        out.append(values.astype(jnp.bfloat16).astype(jnp.float32))
        values = values - out[-1]
    return out


def side_by_side(values, lanes):
    first, second, third = pieces(values)
    return first + pltpu.roll(second, lanes, 1) + pltpu.roll(third, 2 * lanes, 1)


def pack_kernel(
    state_ref, heat_ref, kappa_ref, frozen_ref, label_ref, held_ref, *refs
):
    state, heat, kappa, frozen, label, sems = refs[-6:]
    edge_ref = refs[0] if len(refs) > 6 else held_ref.at[5:9, :]
    layers, elements = kappa.shape
    flat = state.shape[1]
    edge_x = frozen_ref.shape[0]
    top, bottom = pl.ds(0, 8), pl.ds(edge_x - 8, 8)
    copies = started(
        [
            (state_ref, state),
            (heat_ref, heat),
            (kappa_ref, kappa),
            (frozen_ref.at[top, :], frozen.at[0]),
            (frozen_ref.at[bottom, :], frozen.at[1]),
            (label_ref.at[top, :], label.at[0]),
            (label_ref.at[bottom, :], label.at[1]),
        ],
        sems,
    )
    for copy in copies[:3]:
        copy.wait()
    for layer in range(layers):
        lanes = slice(layer * flat, (layer + 1) * flat)
        for parity in range(2):
            row = slice(2 * layer + parity, 2 * layer + parity + 1)
            held_ref[parity : parity + 1, lanes] = state[row, :]
            held_ref[2 + parity : 3 + parity, lanes] = heat[row, :]
        wide = jnp.broadcast_to(kappa[layer : layer + 1, :], (8, elements))
        wide = jnp.concatenate([wide, jnp.zeros((8, flat - elements), jnp.float32)], 1)
        held_ref[4:5, lanes] = side_by_side(wide, elements)[0:1]
    for copy in copies[3:]:
        copy.wait()
    edge_ref[0:1, :] = frozen[1, 7:8, :]
    edge_ref[1:2, :] = label[1, 7:8, :].astype(jnp.float32)
    edge_ref[2:3, :] = frozen[0, 0:1, :]
    edge_ref[3:4, :] = label[0, 0:1, :].astype(jnp.float32)


def pick_codes(table_ref, labels):
    half = table_ref.shape[0]
    tile, lane = labels >> 7, labels & (LANES - 1)
    upper = tile >= half
    row = jnp.where(upper, tile - half, tile)
    found = jnp.zeros(labels.shape, jnp.int32)
    for r in range(half):
        line = jnp.broadcast_to(table_ref[r : r + 1, :], labels.shape)
        here = jnp.take_along_axis(line, lane, axis=1, mode="promise_in_bounds")
        found = jnp.where(row == r, here, found)
    return jnp.where(upper, found >> 12, found) & 4095


def level(code, direction):
    return (((code >> (2 * direction)) & 3) + 1).astype(jnp.float32)


def started(pairs, sems):
    copies = [pltpu.make_async_copy(*pair, sems.at[i]) for i, pair in enumerate(pairs)]
    for copy in copies:
        copy.start()
    return copies


def faces_kernel(
    depth, flat, table_hbm, label_hbm, frozen_hbm,
    packed_ref, label_ref, frozen_ref, faces_ref, table_ref, sems,
):
    count = table_ref.shape[1]
    half = packed_ref.shape[0]
    edge_x = frozen_ref.shape[0]
    chunk = up_to(half, 4) // 4 * LANES
    order = [at for low in range(0, half * LANES, chunk) for at in (low, low + half * LANES)]
    order = [at for at in order if at < count]
    parts = [pl.ds(at, min(chunk, count - at)) for at in order]
    get_label, get_frozen, *get_table = started(
        [(label_hbm, label_ref), (frozen_hbm, frozen_ref)]
        + [(table_hbm.at[:, part], table_ref.at[:, part]) for part in parts],
        sems,
    )
    get_label.wait()
    get_frozen.wait()
    label = jnp.transpose(label_ref[...])
    label = jnp.concatenate([label[0:depth], label[flat - depth : flat]], 0)
    frozen = jnp.transpose(frozen_ref[...])
    frozen = 0.25 * jnp.concatenate([frozen[0:depth], frozen[flat - depth : flat]], 0)
    directions = table_ref.shape[0]
    place = 2 * lax.broadcasted_iota(jnp.int32, (directions, LANES), 0)

    def tile(number):
        size = max(min(LANES, count - number * LANES), 0)
        here = table_ref[:, number * LANES : number * LANES + size] if size else None
        if size == LANES:
            return here
        blank = jnp.ones((directions, LANES - size), jnp.int32)
        return jnp.concatenate([here, blank], 1) if size else blank

    waiting = dict(zip(order, get_table))
    for r in range(half):
        for at in (r * LANES, (r + half) * LANES):
            if at in waiting:
                waiting.pop(at).wait()
        bits = ((tile(r) - 1) << place) | ((tile(r + half) - 1) << (place + 12))
        packed_ref[r : r + 1, :] = jnp.sum(bits, axis=0, keepdims=True)
    short = -edge_x % LANES
    if short:
        label = jnp.concatenate([label, jnp.zeros((2 * depth, short), jnp.int32)], 1)
    for t in range(up_to(edge_x, LANES) // LANES):
        size = min(LANES, edge_x - t * LANES)
        lanes = slice(t * LANES, t * LANES + size)
        for part in range(2 * depth // 8):
            rows = slice(part * 8, part * 8 + 8)
            code = pick_codes(packed_ref, label[rows, t * LANES : (t + 1) * LANES])[:, :size]
            faces_ref[rows, lanes] = frozen[rows, lanes] * level(code, 2 if part * 8 < depth else 3)


def cells_kernel(
    depth, flat, packed_ref, label_ref, frozen_ref, faces_ref, gathered_ref, onward_ref, code_ref
):
    onward_ref[...] = faces_ref[...]
    edge_x, wide = frozen_ref.shape

    def look_up(chunk, carry):
        rows = pl.ds(pl.multiple_of(chunk * 8, 8), 8)
        for t in range(wide // LANES):
            lanes = pl.ds(t * LANES, LANES)
            code_ref[rows, lanes] = pick_codes(packed_ref, label_ref[rows, lanes])
        return carry

    lax.fori_loop(0, edge_x // 8, look_up, 0, unroll=16)
    frozen = frozen_ref[...] * 0.25
    code = code_ref[...]
    shares = [frozen * level(code, d) for d in range(6)]
    line_x = lax.broadcasted_iota(jnp.int32, (edge_x, wide), 0)
    lane = lax.broadcasted_iota(jnp.int32, (edge_x, wide), 1)
    deep = split_index(lane, depth)[1]
    total = jnp.where(line_x == edge_x - 1, 0.0, pltpu.roll(shares[0], edge_x - 1, 0))
    total += jnp.where(line_x == 0, 0.0, pltpu.roll(shares[1], 1, 0))
    total += jnp.where(lane >= flat - depth, 0.0, pltpu.roll(shares[2], wide - depth, 1))
    total += jnp.where(lane < depth, 0.0, pltpu.roll(shares[3], depth, 1))
    total += jnp.where(
        deep == depth - 1, pltpu.roll(shares[4], depth - 1, 1), pltpu.roll(shares[4], wide - 1, 1)
    )
    total += jnp.where(
        deep == 0, pltpu.roll(shares[5], wide - (depth - 1), 1), pltpu.roll(shares[5], 1, 1)
    )
    gathered_ref[...] = total


def sites_kernel(
    flat, packed_ref, edge_ref, faces_ref, slot_hbm, seed_hbm, spread_hbm,
    nucleation_ref, ends_ref, spread_ref, onward_ref, slot_ref, seed_ref, sems,
):
    copies = started([(slot_hbm, slot_ref), (seed_hbm, seed_ref), (spread_hbm, spread_ref)], sems)
    onward_ref[...] = faces_ref[...]
    edge_x, wide = nucleation_ref.shape
    for t in range(wide // LANES):
        lanes = slice(t * LANES, (t + 1) * LANES)
        rough = jnp.concatenate([edge_ref[:, lanes], jnp.zeros((4, LANES), jnp.float32)], 0)
        codes = pick_codes(packed_ref, rough.astype(jnp.int32))
        ends_ref[0:1, lanes] = rough[0:1] * level(codes[1:2], 1) * 0.25
        ends_ref[1:2, lanes] = rough[2:3] * level(codes[3:4], 0) * 0.25
    for copy in copies:
        copy.wait()
    sites = seed_ref.shape[0]
    codes = pick_codes(packed_ref, seed_ref[...])
    worth = sum(level(codes, d) for d in range(6))
    site_x, site_lane = split_index(slot_ref[...], flat)
    at_x = lax.broadcasted_iota(jnp.int32, (edge_x, LANES), 0)
    at_lane = lax.broadcasted_iota(jnp.int32, (wide, LANES), 0)
    added = jnp.zeros((edge_x, wide), jnp.float32)
    for r in range(sites):
        left = jnp.where(at_x == site_x[r : r + 1], worth[r : r + 1], 0.0).astype(jnp.bfloat16)
        right = jnp.where(at_lane == site_lane[r : r + 1], 1.0, 0.0).astype(jnp.bfloat16)
        added += lax.dot_general(
            left, right, (((1,), (1,)), ((), ())), preferred_element_type=jnp.float32
        )
    nucleation_ref[...] = added * (1.0 / 6.0)


def spread_tables(width, plane):
    rows_y, deep = width // plane, plane // 2

    def tables(count):
        spread, after, before = (np.zeros((count // 2, count), np.float32) for _ in range(3))
        for element in range(count // 2):
            for local, weight in enumerate((1, 4, 1)):
                spread[element, (2 * element + local) % count] += weight
            for local in range(2):
                after[element, (2 * element + local) % count] += 1
                before[element, (2 * element + local + 1) % count] += 1
        return spread, after, before

    spread_y, after_y, before_y = tables(rows_y)
    spread_z, after_z, before_z = tables(plane)
    full = [
        np.kron(spread_y, spread_z),
        np.kron(after_y, spread_z),
        np.kron(before_y, spread_z),
        np.kron(spread_y, after_z),
        np.kron(spread_y, before_z),
    ]
    half = lambda count: np.where(np.arange(count) % 2 == 1, 0.5, 1.0)
    inverse = 27.0 * np.kron(half(rows_y), half(plane))
    out = np.zeros((width, 5 * width), jnp.bfloat16)
    out[: 3 * (width // 4)] = np.concatenate([np.concatenate([t * inverse for t in full], 1)] * 3, 0)
    return out


def advance(plane, even, odd, heat_even, heat_odd, kappa, spread):
    rows, width = even.shape
    up = lambda v: pltpu.roll(v, rows - 1, 0)
    down = lambda v: pltpu.roll(v, 1, 0)
    turn = lambda v, by: pltpu.roll(v, by % width, 1)
    lane = lax.broadcasted_iota(jnp.int32, (rows, width), 1)
    row_y, deep = split_index(lane, plane)
    even_y, even_z = row_y & 1 == 0, deep & 1 == 0
    lines = jnp.dot(kappa.astype(jnp.bfloat16), spread, preferred_element_type=jnp.float32)
    lines = lines * (STEP / 108.0)
    along_x, *others = (lines[:, i * width : (i + 1) * width] for i in range(5))
    behind_x = down(along_x)
    scale = STEP * 27.0 * jnp.where(even_y, 1.0, 0.5) * jnp.where(even_z, 1.0, 0.5)
    heat_even, heat_odd = scale * heat_even, (0.5 * scale) * heat_odd

    def in_plane(parts):
        after_y, before_y, after_z, before_z = parts
        own = jnp.where(even_y, 7.0 * (after_y + before_y), 16.0 * after_y)
        own = own + jnp.where(even_z, 7.0 * (after_z + before_z), 16.0 * after_z)
        far = [jnp.where(even_y, v, 0.0) for v in parts[:2]] + [
            jnp.where(even_z, v, 0.0) for v in parts[2:]
        ]
        return own, [-8.0 * v for v in parts], far

    own_even, near_even, far_even = in_plane([v + down(v) for v in others])
    own_odd, near_odd, far_odd = in_plane([2.0 * v for v in others])
    own_even = own_even + 7.0 * (along_x + behind_x)
    own_odd = own_odd + 8.0 * along_x
    near_x, near_behind, near_odd_x = -8.0 * along_x, -8.0 * behind_x, -4.0 * along_x

    def moved(values, by):
        if by > 0:
            return jnp.where(deep + by >= plane, turn(values, plane - by), turn(values, -by))
        return jnp.where(deep + by < 0, turn(values, -by - plane), turn(values, -by))

    def neighbours(values, near, far):
        ahead_y, back_y = turn(values, -plane), turn(values, plane)
        total = near[0] * ahead_y + near[1] * back_y
        total += near[2] * moved(values, 1) + near[3] * moved(values, -1)
        total += far[0] * turn(values, -2 * plane) + far[1] * turn(values, 2 * plane)
        if plane == 4:
            return total + (far[2] + far[3]) * moved(values, 2)
        return total + far[2] * moved(values, 2) + far[3] * moved(values, -2)

    def change(v_even, v_odd):
        following = up(v_even)
        k_even = own_even * v_even + along_x * following + behind_x * down(v_even)
        k_even += near_x * v_odd + near_behind * down(v_odd)
        k_odd = own_odd * v_odd + near_odd_x * (v_even + following)
        k_even += neighbours(v_even, near_even, far_even)
        k_odd += neighbours(v_odd, near_odd, far_odd)
        return heat_even - k_even, heat_odd - k_odd

    one_even, one_odd = change(even, odd)
    two_even, two_odd = change(even + one_even, odd + one_odd)
    return even + 0.5 * (one_even + two_even), odd + 0.5 * (one_odd + two_odd)


def heat_kernel(plane, layers, first_row, state_ref, spread_ref, new_ref, even_ref, odd_ref):
    state = [state_ref[i] for i in range(5)]
    state[4] = side_by_side(state[4], state[4].shape[1] // 4)
    even, odd = advance(plane, *state, spread_ref[...])
    even_ref[...] = even
    odd_ref[...] = odd
    start = first_row()
    for layer in range(layers):
        new_ref[2 * layer : 2 * layer + 1, :] = even_ref[pl.ds(start + layer, 1), :]
        new_ref[2 * layer + 1 : 2 * layer + 2, :] = odd_ref[pl.ds(start + layer, 1), :]


def basis(step):
    point = (step.astype(jnp.float32) + 0.5) / CPC
    return (
        2.0 * (point - 0.5) * (point - 1.0),
        -4.0 * point * (point - 1.0),
        2.0 * point * (point - 0.5),
    )


def finish_kernel(
    plane, depth, flat, layers, sizes, first_layer, first_row, cell_row, wraps,
    mine_ref, theirs_ref, across_ref, passing_ref, edge_ref, kept_ref, spread_ref, weave_ref,
    packed_ref, gathered_ref, nucleation_ref, frozen_ref, *refs,
):
    solid_out, state_ref, even_ref, odd_ref, side_ref, extra_ref, solid_ref, new_ref, sems = refs[-9:]
    edge_x, wide = frozen_ref.shape
    _, all_rows, width = state_ref.shape
    rows = even_ref.shape[0]
    heat_rows, across_row, passing_row, edge_row = sizes
    core = lax.axis_index("slab") & 1
    if heat_rows:
        slabs = lax.axis_size("slab")
        me = lax.axis_index("grp") * slabs + lax.axis_index("slab")
        state_ref[:, rows - 8 : rows, :] = jnp.zeros((5, 8, width), jnp.float32)
        numbers = [me ^ off for off in arrival_order(slabs)[: slabs // 2]]
        numbers += beyond_order(me, slabs)
        numbers += [me ^ 1 ^ off for off in arrival_order(slabs)[: slabs // 2]]
        numbers += beyond_order(me ^ 1, slabs)
        blocks = len(numbers) // 2
        for p, number in enumerate(numbers):
            source, block = (mine_ref, p) if p < blocks else (theirs_ref, p - blocks)
            row = lax.rem(number * layers + (all_rows - first_layer()), all_rows)
            for c in range(5):
                for layer in range(layers):
                    state_ref[c, pl.ds(row + layer, 1), :] = source[
                        block * 5 + c : block * 5 + c + 1, layer * width : (layer + 1) * width
                    ]
        state = [state_ref[i, 0:rows, :] for i in range(5)]
    else:
        state = [mine_ref[i] for i in range(5)]
        state[4] = side_by_side(state[4], width // 4)
    side_ref[...] = jnp.zeros(side_ref.shape, jnp.float32)
    there = jnp.where(core == 0, 0, flat - depth)
    side_ref[pl.ds(pl.multiple_of(there, 8), depth), :] = (
        kept_ref[...] + passing_ref[passing_row : passing_row + depth, :]
    )
    side_ref[pl.ds(pl.multiple_of(flat - depth - there, 8), depth), :] = across_ref[
        across_row : across_row + depth, :
    ]
    extra_ref[...] = gathered_ref[...] + jnp.transpose(side_ref[...])
    extra_ref[0:1, :] += edge_ref[edge_row : edge_row + 1, 0:wide]
    extra_ref[edge_x - 1 : edge_x, :] += edge_ref[edge_row + 1 : edge_row + 2, 0:wide]
    even, odd = advance(plane, *state, spread_ref[...])
    if first_row is not None:
        even_ref[:, 0:width] = even
        odd_ref[:, 0:width] = odd
        start = first_row()
        for layer in range(layers):
            new_ref[2 * layer : 2 * layer + 1, :] = even_ref[pl.ds(start + layer, 1), 0:width]
            new_ref[2 * layer + 1 : 2 * layer + 2, :] = odd_ref[pl.ds(start + layer, 1), 0:width]
        new_copy = pltpu.make_async_copy(new_ref, refs[0], sems.at[CHUNKS])
        new_copy.start()
    both = jnp.concatenate([even, odd], 0)
    first, second, third = pieces(both)
    joined = jnp.concatenate([first, second, third, first, second], 1)
    high, low = weave_ref[0:width, :], weave_ref[width : 2 * width, :]
    woven = jnp.dot(
        joined.astype(jnp.bfloat16),
        jnp.concatenate([high, high, high, low, low], 0),
        preferred_element_type=jnp.float32,
    )
    even_ref[:, 0:wide] = woven[:rows]
    odd_ref[:, 0:wide] = woven[rows:]
    first, middle, last = basis(lax.broadcasted_iota(jnp.int32, (CPC, wide), 0))
    base = cell_row()
    elements = edge_x // CPC
    copies = []
    for a in range(elements):
        cells = slice(a * CPC, (a + 1) * CPC)
        later = base + (a + 1)
        if wraps:
            later = lax.rem(later, rows)
        temperature = (
            first * even_ref[pl.ds(base + a, 1), 0:wide]
            + middle * odd_ref[pl.ds(base + a, 1), 0:wide]
            + last * even_ref[pl.ds(later, 1), 0:wide]
        )
        under = jnp.maximum(-temperature, 0.0)
        rate = under * (under * extra_ref[cells, :] + nucleation_ref[cells, :])
        frozen = frozen_ref[cells, :]
        solid_ref[cells, :] = frozen + (1.0 - frozen) * (1.0 - jnp.exp(-rate))
        done = (a + 1) * CHUNKS // elements
        if done > len(copies):
            low = copies[-1][1] if copies else 0
            part = pl.ds(low, (a + 1) * CPC - low)
            copy = pltpu.make_async_copy(
                solid_ref.at[part, :], solid_out.at[part, :], sems.at[len(copies)]
            )
            copy.start()
            copies.append((copy, (a + 1) * CPC))
    for copy, _ in copies:
        copy.wait()
    if first_row is not None:
        new_copy.wait()


def weave_table(width, plane, depth, edge_y, first_step, first_node, wide):
    row, cell = jnp.arange(2 * width)[:, None], jnp.arange(wide)[None, :]
    node = (row - first_node) % width
    cell_y, cell_z = first_step + cell // depth, cell % depth
    step_y = node // plane - 2 * (cell_y // CPC)
    step_z = (node % plane - 2 * (cell_z // CPC)) % plane
    take = lambda step, at: sum(jnp.where(step == i, v, 0.0) for i, v in enumerate(basis(at % CPC)))
    full = take(step_y, cell_y) * take(step_z, cell_z)
    high = jnp.floor(full * 128.0) * (1.0 / 128.0)
    part = jnp.where(row < width, high, full - high)
    return jnp.where(cell < edge_y * depth, part, 0.0).astype(jnp.bfloat16)


def beyond_order(me, slabs):
    top = slabs.bit_length() - 2

    def kept(number, bit):
        if bit > top:
            return [number ^ slabs ^ 1]
        flips = (1 << bit) | 1
        if bit == 1:
            return kept(number, 2) + kept(number ^ flips, 2)
        return [picked(number, bit), picked(number ^ flips, bit)]

    def picked(number, bit):
        held = kept(number, bit + 1)
        if len(held) == 1:
            return held[0]
        same = ((number >> bit) ^ (number >> (bit + 1))) & 1 == 0
        return jnp.where(same, held[0], held[1])

    return kept(me, 1)


def arrival_order(devices):
    offs = [0]
    for bit in reversed(range(1, devices.bit_length() - 1)):
        offs += [off ^ (1 << bit) ^ 1 for off in offs]
    return offs + [off ^ 1 for off in offs]


def lines(values, width):
    flat = values.reshape(-1)
    return jnp.pad(flat, (0, -flat.shape[0] % width)).reshape(-1, width)


def body(
    thermal_state_values,
    thermal_kappa_values,
    nodal_heating_input,
    frozen_share_map,
    crystal_label_map,
    growth_reach_table,
    seed_site_slots,
    seed_crystal_label,
):
    groups, slabs = lax.axis_size("grp"), lax.axis_size("slab")
    devices = groups * slabs
    group, slab = lax.axis_index("grp"), lax.axis_index("slab")
    me = group * slabs + slab
    layers, elements = thermal_kappa_values.shape
    plane = 2 * HEX_COUNT_LATER
    depth = CPC * HEX_COUNT_LATER
    flat = thermal_state_values.shape[1]
    rows_y = flat // plane
    edge_x, flat_cells = frozen_share_map.shape
    edge_y = flat_cells // depth
    wide = up_to(flat_cells, LANES)
    all_layers = layers * devices

    def exchanged(parts, flips, sent=None):
        at = [0]
        for part in parts[:-1]:
            at.append(at[-1] + part.shape[0])
        total = at[-1] + parts[-1].shape[0]
        if sent is None:
            sent = sum(
                jnp.pad(part, ((row, total - row - part.shape[0]), (0, 0)))
                for row, part in zip(at, parts)
            )
        return sent, lax.ppermute(sent, AXES, [(i, i ^ flips) for i in range(devices)]), at

    def widened(array):
        return jnp.pad(array, ((0, 0), (0, wide - flat_cells)))

    unit = layers * flat
    count = growth_reach_table.shape[0]
    frozen, label = widened(frozen_share_map), widened(crystal_label_map)
    joined = groups == 2 and wide == unit
    packed_rows = pl.pallas_call(
        pack_kernel,
        out_shape=[jax.ShapeDtypeStruct((9, unit), jnp.float32)]
        if joined
        else [
            jax.ShapeDtypeStruct((5, unit), jnp.float32),
            jax.ShapeDtypeStruct((4, wide), jnp.float32),
        ],
        in_specs=[HBM] * 5,
        out_specs=[VMEM] * (1 if joined else 2),
        scratch_shapes=[
            pltpu.VMEM(thermal_state_values.shape, jnp.float32),
            pltpu.VMEM(nodal_heating_input.shape, jnp.float32),
            pltpu.VMEM(thermal_kappa_values.shape, jnp.float32),
            pltpu.VMEM((2, 8, wide), jnp.float32),
            pltpu.VMEM((2, 8, wide), jnp.int32),
            pltpu.SemaphoreType.DMA((7,)),
        ],
        compiler_params=PARAMS,
        name="pack",
    )(*map(in_hbm, (thermal_state_values, nodal_heating_input, thermal_kappa_values, frozen, label)))
    held, edge_rows = packed_rows[0][:5], packed_rows[0][5:] if joined else packed_rows[1]
    high_edge, low_edge = edge_rows[:2], edge_rows[2:]

    brick_layers = edge_x // CPC
    need_y = (edge_y + CPC - 2) // CPC + 6
    width = up_to(need_y * 2 * plane, LANES)
    if 2 * width > flat:
        width = flat
    need_layers = brick_layers + 5
    whole = width == flat and 2 * up_to(need_layers, 8) > all_layers
    direct = whole and edge_x == unit and wide == unit and groups == 2 and slabs > 2
    table_lanes = up_to(count, 2 * LANES)
    packed, label, frozen, faces = pl.pallas_call(
        functools.partial(faces_kernel, depth, flat_cells),
        out_shape=(
            jax.ShapeDtypeStruct((table_lanes // (2 * LANES), LANES), jnp.int32),
            jax.ShapeDtypeStruct((edge_x, wide), jnp.int32),
            jax.ShapeDtypeStruct((edge_x, wide), jnp.float32),
            jax.ShapeDtypeStruct((2 * depth, edge_x), jnp.float32),
        ),
        in_specs=[HBM] * 3,
        out_specs=[VMEM] * 4,
        scratch_shapes=[
            pltpu.VMEM((growth_reach_table.shape[1], count), jnp.int32),
            pltpu.SemaphoreType.DMA((10,)),
        ],
        compiler_params=PARAMS,
        name="faces",
    )(in_hbm(growth_reach_table.T), in_hbm(label), in_hbm(frozen))
    gathered, faces_later = pl.pallas_call(
        functools.partial(cells_kernel, depth, flat_cells),
        out_shape=(
            jax.ShapeDtypeStruct((edge_x, wide), jnp.float32),
            jax.ShapeDtypeStruct((2 * depth, edge_x), jnp.float32),
        ),
        in_specs=[VMEM] * 4,
        out_specs=[VMEM] * 2,
        scratch_shapes=[pltpu.VMEM((edge_x, wide), jnp.int32)],
        compiler_params=PARAMS,
        name="cells",
    )(packed, label, frozen, faces)
    seeds = up_to(seed_site_slots.shape[0], LANES)
    short = seeds - seed_site_slots.shape[0]

    def sites(edges):
        return pl.pallas_call(
            functools.partial(sites_kernel, flat_cells),
            out_shape=(
                jax.ShapeDtypeStruct((edge_x, wide), jnp.float32),
                jax.ShapeDtypeStruct((2, wide), jnp.float32),
                jax.ShapeDtypeStruct((width, 5 * width), jnp.bfloat16),
                jax.ShapeDtypeStruct((2 * depth, edge_x), jnp.float32),
            ),
            in_specs=[VMEM] * 3 + [HBM] * 3,
            out_specs=[VMEM] * 4,
            scratch_shapes=[
                pltpu.VMEM((seeds // LANES, LANES), jnp.int32),
                pltpu.VMEM((seeds // LANES, LANES), jnp.int32),
                pltpu.SemaphoreType.DMA((3,)),
            ],
            compiler_params=PARAMS,
            name="sites",
        )(
            packed,
            edges,
            faces_later,
            in_hbm(jnp.pad(seed_site_slots, (0, short), constant_values=-1).reshape(-1, LANES)),
            in_hbm(jnp.pad(seed_crystal_label, (0, short)).reshape(-1, LANES)),
            in_hbm(jnp.asarray(spread_tables(width, plane))),
        )

    core, pair = me & 1, slab >> 1

    def packets(faces):
        return jnp.where(core == 1, faces[depth:], 0.0), jnp.where(core == 0, faces[:depth], 0.0)

    onward, backward = packets(faces)
    heat, edges = [held], None
    beyond = []
    if groups > 2:
        ring = [(i, (i + 1) % groups) for i in range(groups)]
        edges = jnp.concatenate(
            [
                lax.ppermute(high_edge, "grp", ring),
                lax.ppermute(low_edge, "grp", [(j, i) for i, j in ring]),
            ]
        )
    moved, ends = 0, None
    as_face = lambda part: part.reshape(-1)[: depth * edge_x].reshape(depth, edge_x)
    for bit in reversed(range(1, devices.bit_length() - 1)):
        rides = 1 << bit < slabs
        low = (1 << (bit - 1)) - 1
        moves_on, moves_back = (pair & low) == low, (pair & low) == 0
        extra = []
        if groups == 2 and 1 << bit == slabs:
            extra = [lines(edge_rows, unit)]
        elif rides and low:
            extra = [lines(jnp.where(moves_on, onward, backward), unit)]
        elif rides:
            extra = [lines(onward, unit), lines(backward, unit)]
        first_sent = packed_rows[0] if joined and 1 << bit == slabs else None
        if bit > 1 and len(beyond) == 2:
            same = ((me >> bit) ^ (me >> (bit + 1))) & 1 == 0
            beyond = [jnp.where(same, *beyond)]
        sent, got, at = exchanged(heat + beyond + extra, (1 << bit) | 1, first_sent)
        heat_rows = sum(part.shape[0] for part in heat)
        if direct and 1 << bit == slabs:
            beyond = [got[:heat_rows]]
        else:
            beyond = beyond + [
                got[row : row + part.shape[0]] for row, part in zip(at[len(heat) :], beyond)
            ]
            heat = heat + [got[:heat_rows]]
        parts = [got[row : row + part.shape[0]] for row, part in zip(at[len(at) - len(extra) :], extra)]
        if groups == 2 and 1 << bit == slabs:
            edges = parts[0].reshape(-1)[: 4 * wide].reshape(4, wide)
        elif rides and low:
            if moved == 0:
                onward, backward = packets(faces_later)
            onward = jnp.where(moves_on, as_face(parts[0]), onward)
            backward = jnp.where(moves_back, as_face(parts[0]), backward)
            moved += 1
        elif rides:
            onward, backward = as_face(parts[0]), as_face(parts[1])
        if edges is not None and ends is None:
            nucleation, ends, spread, faces_last = sites(edges)
    extra = [
        lines(jnp.where(core == 0, faces_last[depth:], faces_last[:depth]), unit),
        lines(jnp.where(core == 1, onward, backward), unit),
    ]
    if groups == 2:
        extra.append(lines(ends, unit))
    kept = jnp.where(core == 0, onward, backward)
    heat = heat + beyond
    sent, got, at = exchanged(heat + extra, 1)
    heat_rows = sum(part.shape[0] for part in heat)
    at = at[len(heat) :]
    across, passing = (as_face(got[row : row + part.shape[0]]) for row, part in zip(at, extra[:2]))
    if groups == 2:
        ends = got[at[2] : at[2] + extra[2].shape[0]].reshape(-1)[: 2 * wide].reshape(2, wide)
    first_cell = slab * edge_y
    first_element = first_cell // CPC
    if direct:
        inputs = (sent, got, got, got, got)
        sizes = (heat_rows, *at)
        start_layer, start_y = group * brick_layers - 2, 0
        rows = min(up_to(need_layers, 8), all_layers)
    else:
        order = np.argsort(arrival_order(devices))
        blocks = jnp.concatenate([sent[:heat_rows], got[:heat_rows]], 0).reshape(devices, 5, layers, flat)
        blocks = jnp.take(blocks, jnp.asarray(order)[jnp.arange(devices) ^ me], axis=0)
        held = jnp.moveaxis(blocks, 1, 0).reshape(5, all_layers, flat)
        kappa = sum(held[4:, :, i * elements : (i + 1) * elements] for i in range(3))
        held = jnp.concatenate([held[:4], jnp.pad(kappa, ((0, 0), (0, 0), (0, flat - elements)))])

        def window(first_layer, need_layers, first_element, need_elements):
            rows, lanes = up_to(need_layers, 8), up_to(need_elements * 2 * plane, LANES)
            part, start_layer, start_y = held, 0, 0
            if 2 * rows <= all_layers:
                start_layer = first_layer
                part = lax.dynamic_slice_in_dim(
                    jnp.concatenate([part, part[:, :rows]], 1),
                    jnp.remainder(start_layer, all_layers), rows, 1,
                )
            if 2 * lanes <= flat:
                start_y = 2 * first_element
                shifted = lambda v, by, size: lax.dynamic_slice_in_dim(
                    jnp.concatenate([v, v[..., :size]], -1), by, size, v.ndim - 1
                )
                start = jnp.remainder(first_element, rows_y // 2)
                part = jnp.concatenate(
                    [
                        shifted(part[:4], start * 2 * plane, lanes),
                        jnp.pad(
                            shifted(part[4:, :, :elements], start * HEX_COUNT_LATER, lanes // 4),
                            ((0, 0), (0, 0), (0, lanes - lanes // 4)),
                        ),
                    ],
                    0,
                )
            return part, start_layer, start_y

        state, start_layer, start_y = window(
            group * brick_layers - 2, need_layers, first_element - 2, need_y
        )
        inputs = (state, state, across, passing, ends)
        sizes = (0, 0, 0, 0)
        rows = state.shape[1]
    if isinstance(start_y, int):
        first_lane = lambda: lax.rem(
            lax.div(lax.axis_index("slab") * edge_y, CPC) * (2 * plane), width
        )
    else:
        first_lane = lambda: 4 * plane
    weave = weave_table(width, plane, depth, edge_y, first_cell % CPC, first_lane(), wide)

    def place(start, layer):
        if not isinstance(start, int):
            return lambda: 2
        return lambda: layer(lax.axis_index("grp"), lax.axis_index("slab"))

    def first_layer():
        return lax.rem(lax.axis_index("grp") * brick_layers + (all_layers - 2), all_layers)

    own_layer = lambda g, s: (g * slabs + s) * layers
    cell_row = place(start_layer, lambda g, s: g * brick_layers)
    own_row = place(start_layer, own_layer)
    if direct:
        own_row = lambda: lax.axis_index("slab") * layers + 2
    new_shape = jax.ShapeDtypeStruct((2 * layers, flat), jnp.float32)
    solid_shape = jax.ShapeDtypeStruct((edge_x, wide), jnp.float32)
    span = max(width, wide)
    results = pl.pallas_call(
        functools.partial(
            finish_kernel, plane, depth, flat_cells, layers, sizes, first_layer,
            own_row if whole else None, cell_row, isinstance(start_layer, int),
        ),
        out_shape=(new_shape, solid_shape) if whole else (solid_shape,),
        in_specs=[VMEM] * 12,
        out_specs=(HBM,) * (1 + whole),
        scratch_shapes=[
            pltpu.VMEM((5, all_layers if direct else rows, width), jnp.float32),
            pltpu.VMEM((rows, span), jnp.float32),
            pltpu.VMEM((rows, span), jnp.float32),
            pltpu.VMEM((wide, edge_x), jnp.float32),
            pltpu.VMEM((edge_x, wide), jnp.float32),
            pltpu.VMEM((edge_x, wide), jnp.float32),
            pltpu.VMEM(new_shape.shape, jnp.float32),
            pltpu.SemaphoreType.DMA((CHUNKS + 1,)),
        ],
        compiler_params=PARAMS,
        name="finish",
    )(*inputs, kept, spread, weave, packed, gathered, nucleation, frozen)
    if whole:
        new_field, new_solid = results
    else:
        (new_solid,) = results
        state, start_layer, _ = window(me * layers - 2, layers + 4, 0, rows_y // 2)
        own_row = place(start_layer, own_layer)
        new_field = pl.pallas_call(
            functools.partial(heat_kernel, plane, layers, own_row),
            out_shape=new_shape,
            in_specs=[VMEM] * 2,
            out_specs=VMEM,
            scratch_shapes=[pltpu.VMEM(state.shape[1:], jnp.float32)] * 2,
            compiler_params=PARAMS,
            name="heat",
        )(state, jnp.asarray(spread_tables(flat, plane)))
    return new_field, new_solid[:, :flat_cells]


def solution(mesh):
    in_specs = (
        P(("grp", "slab"), None),
        P(("grp", "slab"), None),
        P(("grp", "slab"), None),
        P("grp", "slab"),
        P("grp", "slab"),
        P(),
        P(("grp", "slab")),
        P(("grp", "slab")),
    )
    out_specs = (P(("grp", "slab"), None), P("grp", "slab"))
    return jax.shard_map(body, mesh=mesh, in_specs=in_specs, out_specs=out_specs, check_vma=False)
```

```python
import functools

import jax
import jax.numpy as jnp
import numpy as np
from jax import lax
from jax.experimental import pallas as pl
from jax.experimental.pallas import tpu as pltpu
from jax.sharding import PartitionSpec as P

HEX_COUNT_LATER = 2
CPC = 8
LANES = 128
CHUNKS = 4
HIGHEST = lax.Precision.HIGHEST
STEP = 0.004
AXES = ("grp", "slab")
VMEM = pl.BlockSpec(memory_space=pltpu.VMEM)
HBM = pl.BlockSpec(memory_space=pltpu.HBM)
PARAMS = pltpu.CompilerParams(vmem_limit_bytes=48 * 1024 * 1024)


def in_hbm(array):
    return pltpu.with_memory_space_constraint(array, pltpu.HBM)


def up_to(value, unit):
    return -(-value // unit) * unit


def split_index(value, by):
    if by & (by - 1) == 0:
        return value >> (by.bit_length() - 1), value & (by - 1)
    quotient = lax.div(value, jnp.full_like(value, by))
    return quotient, value - quotient * by


def pieces(values):
    out = []
    for _ in range(3):
        out.append(values.astype(jnp.bfloat16).astype(jnp.float32))
        values = values - out[-1]
    return out


def at_nodes(plane, flat, row):
    elements = row.shape[1]
    wide = up_to(elements, LANES)
    row = jnp.broadcast_to(row, (8, elements))
    if wide > elements:
        row = jnp.concatenate([row, jnp.zeros((8, wide - elements), jnp.float32)], 1)
    parts = []
    for start in range(0, flat, LANES):
        node_y, deep = split_index(lax.broadcasted_iota(jnp.int32, (8, LANES), 1) + start, plane)
        element = (node_y >> 1) * (plane // 2) + (deep >> 1)
        tile = start // 4 // LANES * LANES
        here = row[:, tile : tile + LANES]
        parts.append(jnp.take_along_axis(here, element - tile, axis=1, mode="promise_in_bounds"))
    return jnp.concatenate(parts, 1)[0:1] if len(parts) > 1 else parts[0][0:1]


def pack_kernel(
    plane, state_ref, heat_ref, kappa_ref, frozen_ref, label_ref, held_ref, *refs
):
    state, heat, kappa, frozen, label, sems = refs[-6:]
    edge_ref = refs[0] if len(refs) > 6 else held_ref.at[5:9, :]
    layers, elements = kappa.shape
    flat = state.shape[1]
    edge_x = frozen_ref.shape[0]
    top, bottom = pl.ds(0, 8), pl.ds(edge_x - 8, 8)
    copies = started(
        [
            (state_ref, state),
            (heat_ref, heat),
            (kappa_ref, kappa),
            (frozen_ref.at[top, :], frozen.at[0]),
            (frozen_ref.at[bottom, :], frozen.at[1]),
            (label_ref.at[top, :], label.at[0]),
            (label_ref.at[bottom, :], label.at[1]),
        ],
        sems,
    )
    for copy in copies[:3]:
        copy.wait()
    for layer in range(layers):
        lanes = slice(layer * flat, (layer + 1) * flat)
        for parity in range(2):
            row = slice(2 * layer + parity, 2 * layer + parity + 1)
            held_ref[parity : parity + 1, lanes] = state[row, :]
            held_ref[2 + parity : 3 + parity, lanes] = heat[row, :]
        held_ref[4:5, lanes] = at_nodes(plane, flat, kappa[layer : layer + 1, :])
    for copy in copies[3:]:
        copy.wait()
    edge_ref[0:1, :] = frozen[1, 7:8, :]
    edge_ref[1:2, :] = label[1, 7:8, :].astype(jnp.float32)
    edge_ref[2:3, :] = frozen[0, 0:1, :]
    edge_ref[3:4, :] = label[0, 0:1, :].astype(jnp.float32)


def pick_codes(table_ref, labels):
    half = table_ref.shape[0]
    tile, lane = labels >> 7, labels & (LANES - 1)
    upper = tile >= half
    row = jnp.where(upper, tile - half, tile)
    found = jnp.zeros(labels.shape, jnp.int32)
    for r in range(half):
        line = jnp.broadcast_to(table_ref[r : r + 1, :], labels.shape)
        here = jnp.take_along_axis(line, lane, axis=1, mode="promise_in_bounds")
        found = jnp.where(row == r, here, found)
    return jnp.where(upper, found >> 12, found) & 4095


def level(code, direction):
    return (((code >> (2 * direction)) & 3) + 1).astype(jnp.float32)


def started(pairs, sems):
    copies = [pltpu.make_async_copy(*pair, sems.at[i]) for i, pair in enumerate(pairs)]
    for copy in copies:
        copy.start()
    return copies


def faces_kernel(
    depth, flat, table_hbm, label_hbm, frozen_hbm,
    packed_ref, label_ref, frozen_ref, faces_ref, table_ref, sems,
):
    count = table_ref.shape[1]
    half = packed_ref.shape[0]
    edge_x = frozen_ref.shape[0]
    chunk = up_to(half, 4) // 4 * LANES
    order = [at for low in range(0, half * LANES, chunk) for at in (low, low + half * LANES)]
    order = [at for at in order if at < count]
    parts = [pl.ds(at, min(chunk, count - at)) for at in order]
    get_label, get_frozen, *get_table = started(
        [(label_hbm, label_ref), (frozen_hbm, frozen_ref)]
        + [(table_hbm.at[:, part], table_ref.at[:, part]) for part in parts],
        sems,
    )
    get_label.wait()
    get_frozen.wait()
    label = jnp.transpose(label_ref[...])
    label = jnp.concatenate([label[0:depth], label[flat - depth : flat]], 0)
    frozen = jnp.transpose(frozen_ref[...])
    frozen = 0.25 * jnp.concatenate([frozen[0:depth], frozen[flat - depth : flat]], 0)
    directions = table_ref.shape[0]
    place = 2 * lax.broadcasted_iota(jnp.int32, (directions, LANES), 0)

    def tile(number):
        size = max(min(LANES, count - number * LANES), 0)
        here = table_ref[:, number * LANES : number * LANES + size] if size else None
        if size == LANES:
            return here
        blank = jnp.ones((directions, LANES - size), jnp.int32)
        return jnp.concatenate([here, blank], 1) if size else blank

    waiting = dict(zip(order, get_table))
    for r in range(half):
        for at in (r * LANES, (r + half) * LANES):
            if at in waiting:
                waiting.pop(at).wait()
        bits = ((tile(r) - 1) << place) | ((tile(r + half) - 1) << (place + 12))
        packed_ref[r : r + 1, :] = jnp.sum(bits, axis=0, keepdims=True)
    short = -edge_x % LANES
    if short:
        label = jnp.concatenate([label, jnp.zeros((2 * depth, short), jnp.int32)], 1)
    for t in range(up_to(edge_x, LANES) // LANES):
        size = min(LANES, edge_x - t * LANES)
        lanes = slice(t * LANES, t * LANES + size)
        for part in range(2 * depth // 8):
            rows = slice(part * 8, part * 8 + 8)
            code = pick_codes(packed_ref, label[rows, t * LANES : (t + 1) * LANES])[:, :size]
            faces_ref[rows, lanes] = frozen[rows, lanes] * level(code, 2 if part * 8 < depth else 3)


def cells_kernel(
    depth, flat, packed_ref, label_ref, frozen_ref, faces_ref, gathered_ref, onward_ref, code_ref
):
    onward_ref[...] = faces_ref[...]
    edge_x, wide = frozen_ref.shape

    def look_up(chunk, carry):
        rows = pl.ds(pl.multiple_of(chunk * 8, 8), 8)
        for t in range(wide // LANES):
            lanes = pl.ds(t * LANES, LANES)
            code_ref[rows, lanes] = pick_codes(packed_ref, label_ref[rows, lanes])
        return carry

    lax.fori_loop(0, edge_x // 8, look_up, 0, unroll=16)
    frozen = frozen_ref[...] * 0.25
    code = code_ref[...]
    shares = [frozen * level(code, d) for d in range(6)]
    line_x = lax.broadcasted_iota(jnp.int32, (edge_x, wide), 0)
    lane = lax.broadcasted_iota(jnp.int32, (edge_x, wide), 1)
    deep = split_index(lane, depth)[1]
    total = jnp.where(line_x == edge_x - 1, 0.0, pltpu.roll(shares[0], edge_x - 1, 0))
    total += jnp.where(line_x == 0, 0.0, pltpu.roll(shares[1], 1, 0))
    total += jnp.where(lane >= flat - depth, 0.0, pltpu.roll(shares[2], wide - depth, 1))
    total += jnp.where(lane < depth, 0.0, pltpu.roll(shares[3], depth, 1))
    total += jnp.where(
        deep == depth - 1, pltpu.roll(shares[4], depth - 1, 1), pltpu.roll(shares[4], wide - 1, 1)
    )
    total += jnp.where(
        deep == 0, pltpu.roll(shares[5], wide - (depth - 1), 1), pltpu.roll(shares[5], 1, 1)
    )
    gathered_ref[...] = total


def sites_kernel(
    flat, packed_ref, edge_ref, faces_ref, slot_hbm, seed_hbm,
    nucleation_ref, ends_ref, onward_ref, slot_ref, seed_ref, sems,
):
    copies = started([(slot_hbm, slot_ref), (seed_hbm, seed_ref)], sems)
    onward_ref[...] = faces_ref[...]
    edge_x, wide = nucleation_ref.shape
    for t in range(wide // LANES):
        lanes = slice(t * LANES, (t + 1) * LANES)
        rough = jnp.concatenate([edge_ref[:, lanes], jnp.zeros((4, LANES), jnp.float32)], 0)
        codes = pick_codes(packed_ref, rough.astype(jnp.int32))
        ends_ref[0:1, lanes] = rough[0:1] * level(codes[1:2], 1) * 0.25
        ends_ref[1:2, lanes] = rough[2:3] * level(codes[3:4], 0) * 0.25
    for copy in copies:
        copy.wait()
    sites = seed_ref.shape[0]
    codes = pick_codes(packed_ref, seed_ref[...])
    worth = sum(level(codes, d) for d in range(6))
    site_x, site_lane = split_index(slot_ref[...], flat)
    at_x = lax.broadcasted_iota(jnp.int32, (edge_x, LANES), 0)
    at_lane = lax.broadcasted_iota(jnp.int32, (wide, LANES), 0)
    added = jnp.zeros((edge_x, wide), jnp.float32)
    for r in range(sites):
        left = jnp.where(at_x == site_x[r : r + 1], worth[r : r + 1], 0.0).astype(jnp.bfloat16)
        right = jnp.where(at_lane == site_lane[r : r + 1], 1.0, 0.0).astype(jnp.bfloat16)
        added += lax.dot_general(
            left, right, (((1,), (1,)), ((), ())), preferred_element_type=jnp.float32
        )
    nucleation_ref[...] = added * (1.0 / 6.0)


def advance(plane, even, odd, heat_even, heat_odd, kappa):
    rows, width = even.shape
    up = lambda v: pltpu.roll(v, rows - 1, 0)
    down = lambda v: pltpu.roll(v, 1, 0)
    turn = lambda v, by: pltpu.roll(v, by % width, 1)
    lane = lax.broadcasted_iota(jnp.int32, (rows, width), 1)
    row_y, deep = split_index(lane, plane)
    even_y, even_z = row_y & 1 == 0, deep & 1 == 0
    back = turn(kappa, 1)
    low_y = turn(kappa, plane)
    low_z = jnp.where(deep == 0, turn(kappa, 1 - plane), back)
    low = jnp.where(deep == 0, back, turn(kappa, plane + 1))
    spread_z = jnp.where(even_z, kappa + low_z, 4.0 * kappa)
    spread_z_low = jnp.where(even_z, low_y + low, 4.0 * low_y)
    spread_y = jnp.where(even_y, kappa + low_y, 4.0 * kappa)
    spread_y_low = jnp.where(even_y, low_z + low, 4.0 * low_z)
    scale = STEP * 27.0 * jnp.where(even_y, 1.0, 0.5) * jnp.where(even_z, 1.0, 0.5)
    share = scale * (1.0 / 108.0)
    along_x = share * jnp.where(even_y, spread_z + spread_z_low, 4.0 * spread_z)
    others = [
        share * spread_z,
        share * jnp.where(even_y, spread_z_low, spread_z),
        share * spread_y,
        share * jnp.where(even_z, spread_y_low, spread_y),
    ]
    behind_x = down(along_x)
    heat_even, heat_odd = scale * heat_even, (0.5 * scale) * heat_odd

    def in_plane(parts):
        after_y, before_y, after_z, before_z = parts
        own = jnp.where(even_y, 7.0 * (after_y + before_y), 16.0 * after_y)
        own = own + jnp.where(even_z, 7.0 * (after_z + before_z), 16.0 * after_z)
        far = [jnp.where(even_y, v, 0.0) for v in parts[:2]] + [
            jnp.where(even_z, v, 0.0) for v in parts[2:]
        ]
        return own, [-8.0 * v for v in parts], far

    own_even, near_even, far_even = in_plane([v + down(v) for v in others])
    own_odd, near_odd, far_odd = in_plane([2.0 * v for v in others])
    own_even = own_even + 7.0 * (along_x + behind_x)
    own_odd = own_odd + 8.0 * along_x
    near_x, near_behind, near_odd_x = -8.0 * along_x, -8.0 * behind_x, -4.0 * along_x

    def moved(values, by):
        if by > 0:
            return jnp.where(deep + by >= plane, turn(values, plane - by), turn(values, -by))
        return jnp.where(deep + by < 0, turn(values, -by - plane), turn(values, -by))

    def neighbours(values, near, far):
        ahead_y, back_y = turn(values, -plane), turn(values, plane)
        total = near[0] * ahead_y + near[1] * back_y
        total += near[2] * moved(values, 1) + near[3] * moved(values, -1)
        total += far[0] * turn(values, -2 * plane) + far[1] * turn(values, 2 * plane)
        if plane == 4:
            return total + (far[2] + far[3]) * moved(values, 2)
        return total + far[2] * moved(values, 2) + far[3] * moved(values, -2)

    def change(v_even, v_odd):
        following = up(v_even)
        k_even = own_even * v_even + along_x * following + behind_x * down(v_even)
        k_even += near_x * v_odd + near_behind * down(v_odd)
        k_odd = own_odd * v_odd + near_odd_x * (v_even + following)
        k_even += neighbours(v_even, near_even, far_even)
        k_odd += neighbours(v_odd, near_odd, far_odd)
        return heat_even - k_even, heat_odd - k_odd

    one_even, one_odd = change(even, odd)
    two_even, two_odd = change(even + one_even, odd + one_odd)
    return even + 0.5 * (one_even + two_even), odd + 0.5 * (one_odd + two_odd)


def heat_kernel(plane, layers, first_row, state_ref, new_ref, even_ref, odd_ref):
    even, odd = advance(plane, *(state_ref[i] for i in range(5)))
    even_ref[...] = even
    odd_ref[...] = odd
    start = first_row()
    for layer in range(layers):
        new_ref[2 * layer : 2 * layer + 1, :] = even_ref[pl.ds(start + layer, 1), :]
        new_ref[2 * layer + 1 : 2 * layer + 2, :] = odd_ref[pl.ds(start + layer, 1), :]


def basis(step):
    point = (step.astype(jnp.float32) + 0.5) / CPC
    return (
        2.0 * (point - 0.5) * (point - 1.0),
        -4.0 * point * (point - 1.0),
        2.0 * point * (point - 0.5),
    )


def finish_kernel(
    plane, depth, flat, layers, sizes, first_layer, first_row, cell_row, wraps,
    mine_ref, theirs_ref, across_ref, passing_ref, edge_ref, kept_ref, weave_ref,
    packed_ref, gathered_ref, nucleation_ref, frozen_ref, *refs,
):
    solid_out, state_ref, even_ref, odd_ref, side_ref, extra_ref, solid_ref, new_ref, sems = refs[-9:]
    edge_x, wide = frozen_ref.shape
    _, all_rows, width = state_ref.shape
    rows = even_ref.shape[0]
    heat_rows, across_row, passing_row, edge_row = sizes
    core = lax.axis_index("slab") & 1
    if heat_rows:
        slabs = lax.axis_size("slab")
        me = lax.axis_index("grp") * slabs + lax.axis_index("slab")
        state_ref[:, rows - 8 : rows, :] = jnp.zeros((5, 8, width), jnp.float32)
        numbers = [me ^ off for off in arrival_order(slabs)[: slabs // 2]]
        numbers += beyond_order(me, slabs)
        numbers += [me ^ 1 ^ off for off in arrival_order(slabs)[: slabs // 2]]
        numbers += beyond_order(me ^ 1, slabs)
        blocks = len(numbers) // 2
        for p, number in enumerate(numbers):
            source, block = (mine_ref, p) if p < blocks else (theirs_ref, p - blocks)
            row = lax.rem(number * layers + (all_rows - first_layer()), all_rows)
            for c in range(5):
                for layer in range(layers):
                    state_ref[c, pl.ds(row + layer, 1), :] = source[
                        block * 5 + c : block * 5 + c + 1, layer * width : (layer + 1) * width
                    ]
        state = [state_ref[i, 0:rows, :] for i in range(5)]
    else:
        state = [mine_ref[i] for i in range(5)]
    side_ref[...] = jnp.zeros(side_ref.shape, jnp.float32)
    there = jnp.where(core == 0, 0, flat - depth)
    side_ref[pl.ds(pl.multiple_of(there, 8), depth), :] = (
        kept_ref[...] + passing_ref[passing_row : passing_row + depth, :]
    )
    side_ref[pl.ds(pl.multiple_of(flat - depth - there, 8), depth), :] = across_ref[
        across_row : across_row + depth, :
    ]
    extra_ref[...] = gathered_ref[...] + jnp.transpose(side_ref[...])
    extra_ref[0:1, :] += edge_ref[edge_row : edge_row + 1, 0:wide]
    extra_ref[edge_x - 1 : edge_x, :] += edge_ref[edge_row + 1 : edge_row + 2, 0:wide]
    even, odd = advance(plane, *state)
    if first_row is not None:
        even_ref[:, 0:width] = even
        odd_ref[:, 0:width] = odd
        start = first_row()
        for layer in range(layers):
            new_ref[2 * layer : 2 * layer + 1, :] = even_ref[pl.ds(start + layer, 1), 0:width]
            new_ref[2 * layer + 1 : 2 * layer + 2, :] = odd_ref[pl.ds(start + layer, 1), 0:width]
        new_copy = pltpu.make_async_copy(new_ref, refs[0], sems.at[CHUNKS])
        new_copy.start()
    both = jnp.concatenate([even, odd], 0)
    first, second, third = pieces(both)
    joined = jnp.concatenate([first, second, third, first, second], 1)
    high, low = weave_ref[0:width, :], weave_ref[width : 2 * width, :]
    woven = jnp.dot(
        joined.astype(jnp.bfloat16),
        jnp.concatenate([high, high, high, low, low], 0),
        preferred_element_type=jnp.float32,
    )
    even_ref[:, 0:wide] = woven[:rows]
    odd_ref[:, 0:wide] = woven[rows:]
    first, middle, last = basis(lax.broadcasted_iota(jnp.int32, (CPC, wide), 0))
    base = cell_row()
    elements = edge_x // CPC
    copies = []
    for a in range(elements):
        cells = slice(a * CPC, (a + 1) * CPC)
        later = base + (a + 1)
        if wraps:
            later = lax.rem(later, rows)
        temperature = (
            first * even_ref[pl.ds(base + a, 1), 0:wide]
            + middle * odd_ref[pl.ds(base + a, 1), 0:wide]
            + last * even_ref[pl.ds(later, 1), 0:wide]
        )
        under = jnp.maximum(-temperature, 0.0)
        rate = under * (under * extra_ref[cells, :] + nucleation_ref[cells, :])
        frozen = frozen_ref[cells, :]
        solid_ref[cells, :] = frozen + (1.0 - frozen) * (1.0 - jnp.exp(-rate))
        done = (a + 1) * CHUNKS // elements
        if done > len(copies):
            low = copies[-1][1] if copies else 0
            part = pl.ds(low, (a + 1) * CPC - low)
            copy = pltpu.make_async_copy(
                solid_ref.at[part, :], solid_out.at[part, :], sems.at[len(copies)]
            )
            copy.start()
            copies.append((copy, (a + 1) * CPC))
    for copy, _ in copies:
        copy.wait()
    if first_row is not None:
        new_copy.wait()


def weave_table(width, plane, depth, edge_y, first_step, first_node, wide):
    row, cell = jnp.arange(2 * width)[:, None], jnp.arange(wide)[None, :]
    node = (row - first_node) % width
    cell_y, cell_z = first_step + cell // depth, cell % depth
    step_y = node // plane - 2 * (cell_y // CPC)
    step_z = (node % plane - 2 * (cell_z // CPC)) % plane
    take = lambda step, at: sum(jnp.where(step == i, v, 0.0) for i, v in enumerate(basis(at % CPC)))
    full = take(step_y, cell_y) * take(step_z, cell_z)
    high = jnp.floor(full * 128.0) * (1.0 / 128.0)
    part = jnp.where(row < width, high, full - high)
    return jnp.where(cell < edge_y * depth, part, 0.0).astype(jnp.bfloat16)


def beyond_order(me, slabs):
    top = slabs.bit_length() - 2

    def kept(number, bit):
        if bit > top:
            return [number ^ slabs ^ 1]
        flips = (1 << bit) | 1
        if bit == 1:
            return kept(number, 2) + kept(number ^ flips, 2)
        return [picked(number, bit), picked(number ^ flips, bit)]

    def picked(number, bit):
        held = kept(number, bit + 1)
        if len(held) == 1:
            return held[0]
        same = ((number >> bit) ^ (number >> (bit + 1))) & 1 == 0
        return jnp.where(same, held[0], held[1])

    return kept(me, 1)


def arrival_order(devices):
    offs = [0]
    for bit in reversed(range(1, devices.bit_length() - 1)):
        offs += [off ^ (1 << bit) ^ 1 for off in offs]
    return offs + [off ^ 1 for off in offs]


def lines(values, width):
    flat = values.reshape(-1)
    return jnp.pad(flat, (0, -flat.shape[0] % width)).reshape(-1, width)


def body(
    thermal_state_values,
    thermal_kappa_values,
    nodal_heating_input,
    frozen_share_map,
    crystal_label_map,
    growth_reach_table,
    seed_site_slots,
    seed_crystal_label,
):
    groups, slabs = lax.axis_size("grp"), lax.axis_size("slab")
    devices = groups * slabs
    group, slab = lax.axis_index("grp"), lax.axis_index("slab")
    me = group * slabs + slab
    layers, elements = thermal_kappa_values.shape
    plane = 2 * HEX_COUNT_LATER
    depth = CPC * HEX_COUNT_LATER
    flat = thermal_state_values.shape[1]
    rows_y = flat // plane
    edge_x, flat_cells = frozen_share_map.shape
    edge_y = flat_cells // depth
    wide = up_to(flat_cells, LANES)
    all_layers = layers * devices

    def exchanged(parts, flips, sent=None):
        at = [0]
        for part in parts[:-1]:
            at.append(at[-1] + part.shape[0])
        total = at[-1] + parts[-1].shape[0]
        if sent is None:
            sent = sum(
                jnp.pad(part, ((row, total - row - part.shape[0]), (0, 0)))
                for row, part in zip(at, parts)
            )
        return sent, lax.ppermute(sent, AXES, [(i, i ^ flips) for i in range(devices)]), at

    def widened(array):
        return jnp.pad(array, ((0, 0), (0, wide - flat_cells)))

    unit = layers * flat
    count = growth_reach_table.shape[0]
    frozen, label = widened(frozen_share_map), widened(crystal_label_map)
    joined = groups == 2 and wide == unit
    packed_rows = pl.pallas_call(
        functools.partial(pack_kernel, plane),
        out_shape=[jax.ShapeDtypeStruct((9, unit), jnp.float32)]
        if joined
        else [
            jax.ShapeDtypeStruct((5, unit), jnp.float32),
            jax.ShapeDtypeStruct((4, wide), jnp.float32),
        ],
        in_specs=[HBM] * 5,
        out_specs=[VMEM] * (1 if joined else 2),
        scratch_shapes=[
            pltpu.VMEM(thermal_state_values.shape, jnp.float32),
            pltpu.VMEM(nodal_heating_input.shape, jnp.float32),
            pltpu.VMEM(thermal_kappa_values.shape, jnp.float32),
            pltpu.VMEM((2, 8, wide), jnp.float32),
            pltpu.VMEM((2, 8, wide), jnp.int32),
            pltpu.SemaphoreType.DMA((7,)),
        ],
        compiler_params=PARAMS,
        name="pack",
    )(*map(in_hbm, (thermal_state_values, nodal_heating_input, thermal_kappa_values, frozen, label)))
    held, edge_rows = packed_rows[0][:5], packed_rows[0][5:] if joined else packed_rows[1]
    high_edge, low_edge = edge_rows[:2], edge_rows[2:]

    brick_layers = edge_x // CPC
    need_y = (edge_y + CPC - 2) // CPC + 6
    width = up_to(need_y * 2 * plane, LANES)
    if 2 * width > flat:
        width = flat
    need_layers = brick_layers + 5
    whole = width == flat and 2 * up_to(need_layers, 8) > all_layers
    direct = whole and edge_x == unit and wide == unit and groups == 2 and slabs > 2
    table_lanes = up_to(count, 2 * LANES)
    packed, label, frozen, faces = pl.pallas_call(
        functools.partial(faces_kernel, depth, flat_cells),
        out_shape=(
            jax.ShapeDtypeStruct((table_lanes // (2 * LANES), LANES), jnp.int32),
            jax.ShapeDtypeStruct((edge_x, wide), jnp.int32),
            jax.ShapeDtypeStruct((edge_x, wide), jnp.float32),
            jax.ShapeDtypeStruct((2 * depth, edge_x), jnp.float32),
        ),
        in_specs=[HBM] * 3,
        out_specs=[VMEM] * 4,
        scratch_shapes=[
            pltpu.VMEM((growth_reach_table.shape[1], count), jnp.int32),
            pltpu.SemaphoreType.DMA((10,)),
        ],
        compiler_params=PARAMS,
        name="faces",
    )(in_hbm(growth_reach_table.T), in_hbm(label), in_hbm(frozen))
    gathered, faces_later = pl.pallas_call(
        functools.partial(cells_kernel, depth, flat_cells),
        out_shape=(
            jax.ShapeDtypeStruct((edge_x, wide), jnp.float32),
            jax.ShapeDtypeStruct((2 * depth, edge_x), jnp.float32),
        ),
        in_specs=[VMEM] * 4,
        out_specs=[VMEM] * 2,
        scratch_shapes=[pltpu.VMEM((edge_x, wide), jnp.int32)],
        compiler_params=PARAMS,
        name="cells",
    )(packed, label, frozen, faces)
    seeds = up_to(seed_site_slots.shape[0], LANES)
    short = seeds - seed_site_slots.shape[0]

    def sites(edges):
        return pl.pallas_call(
            functools.partial(sites_kernel, flat_cells),
            out_shape=(
                jax.ShapeDtypeStruct((edge_x, wide), jnp.float32),
                jax.ShapeDtypeStruct((2, wide), jnp.float32),
                jax.ShapeDtypeStruct((2 * depth, edge_x), jnp.float32),
            ),
            in_specs=[VMEM] * 3 + [HBM] * 2,
            out_specs=[VMEM] * 3,
            scratch_shapes=[
                pltpu.VMEM((seeds // LANES, LANES), jnp.int32),
                pltpu.VMEM((seeds // LANES, LANES), jnp.int32),
                pltpu.SemaphoreType.DMA((2,)),
            ],
            compiler_params=PARAMS,
            name="sites",
        )(
            packed,
            edges,
            faces_later,
            in_hbm(jnp.pad(seed_site_slots, (0, short), constant_values=-1).reshape(-1, LANES)),
            in_hbm(jnp.pad(seed_crystal_label, (0, short)).reshape(-1, LANES)),
        )

    core, pair = me & 1, slab >> 1

    def packets(faces):
        return jnp.where(core == 1, faces[depth:], 0.0), jnp.where(core == 0, faces[:depth], 0.0)

    onward, backward = packets(faces)
    heat, edges = [held], None
    beyond = []
    if groups > 2:
        ring = [(i, (i + 1) % groups) for i in range(groups)]
        edges = jnp.concatenate(
            [
                lax.ppermute(high_edge, "grp", ring),
                lax.ppermute(low_edge, "grp", [(j, i) for i, j in ring]),
            ]
        )
    moved, ends = 0, None
    as_face = lambda part: part.reshape(-1)[: depth * edge_x].reshape(depth, edge_x)
    for bit in reversed(range(1, devices.bit_length() - 1)):
        rides = 1 << bit < slabs
        low = (1 << (bit - 1)) - 1
        moves_on, moves_back = (pair & low) == low, (pair & low) == 0
        extra = []
        if groups == 2 and 1 << bit == slabs:
            extra = [lines(edge_rows, unit)]
        elif rides and low:
            extra = [lines(jnp.where(moves_on, onward, backward), unit)]
        elif rides:
            extra = [lines(onward, unit), lines(backward, unit)]
        first_sent = packed_rows[0] if joined and 1 << bit == slabs else None
        if bit > 1 and len(beyond) == 2:
            same = ((me >> bit) ^ (me >> (bit + 1))) & 1 == 0
            beyond = [jnp.where(same, *beyond)]
        sent, got, at = exchanged(heat + beyond + extra, (1 << bit) | 1, first_sent)
        heat_rows = sum(part.shape[0] for part in heat)
        if direct and 1 << bit == slabs:
            beyond = [got[:heat_rows]]
        else:
            beyond = beyond + [
                got[row : row + part.shape[0]] for row, part in zip(at[len(heat) :], beyond)
            ]
            heat = heat + [got[:heat_rows]]
        parts = [got[row : row + part.shape[0]] for row, part in zip(at[len(at) - len(extra) :], extra)]
        if groups == 2 and 1 << bit == slabs:
            edges = parts[0].reshape(-1)[: 4 * wide].reshape(4, wide)
        elif rides and low:
            if moved == 0:
                onward, backward = packets(faces_later)
            onward = jnp.where(moves_on, as_face(parts[0]), onward)
            backward = jnp.where(moves_back, as_face(parts[0]), backward)
            moved += 1
        elif rides:
            onward, backward = as_face(parts[0]), as_face(parts[1])
        if edges is not None and ends is None:
            nucleation, ends, faces_last = sites(edges)
    extra = [
        lines(jnp.where(core == 0, faces_last[depth:], faces_last[:depth]), unit),
        lines(jnp.where(core == 1, onward, backward), unit),
    ]
    if groups == 2:
        extra.append(lines(ends, unit))
    kept = jnp.where(core == 0, onward, backward)
    heat = heat + beyond
    sent, got, at = exchanged(heat + extra, 1)
    heat_rows = sum(part.shape[0] for part in heat)
    at = at[len(heat) :]
    across, passing = (as_face(got[row : row + part.shape[0]]) for row, part in zip(at, extra[:2]))
    if groups == 2:
        ends = got[at[2] : at[2] + extra[2].shape[0]].reshape(-1)[: 2 * wide].reshape(2, wide)
    first_cell = slab * edge_y
    first_element = first_cell // CPC
    if direct:
        inputs = (sent, got, got, got, got)
        sizes = (heat_rows, *at)
        start_layer, start_y = group * brick_layers - 2, 0
        rows = min(up_to(need_layers, 8), all_layers)
    else:
        order = np.argsort(arrival_order(devices))
        blocks = jnp.concatenate([sent[:heat_rows], got[:heat_rows]], 0).reshape(devices, 5, layers, flat)
        blocks = jnp.take(blocks, jnp.asarray(order)[jnp.arange(devices) ^ me], axis=0)
        held = jnp.moveaxis(blocks, 1, 0).reshape(5, all_layers, flat)

        def window(first_layer, need_layers, first_element, need_elements):
            rows, lanes = up_to(need_layers, 8), up_to(need_elements * 2 * plane, LANES)
            part, start_layer, start_y = held, 0, 0
            if 2 * rows <= all_layers:
                start_layer = first_layer
                part = lax.dynamic_slice_in_dim(
                    jnp.concatenate([part, part[:, :rows]], 1),
                    jnp.remainder(start_layer, all_layers), rows, 1,
                )
            if 2 * lanes <= flat:
                start_y = 2 * first_element
                shifted = lambda v, by, size: lax.dynamic_slice_in_dim(
                    jnp.concatenate([v, v[..., :size]], -1), by, size, v.ndim - 1
                )
                start = jnp.remainder(first_element, rows_y // 2)
                part = shifted(part, start * 2 * plane, lanes)
            return part, start_layer, start_y

        state, start_layer, start_y = window(
            group * brick_layers - 2, need_layers, first_element - 2, need_y
        )
        inputs = (state, state, across, passing, ends)
        sizes = (0, 0, 0, 0)
        rows = state.shape[1]
    if isinstance(start_y, int):
        first_lane = lambda: lax.rem(
            lax.div(lax.axis_index("slab") * edge_y, CPC) * (2 * plane), width
        )
    else:
        first_lane = lambda: 4 * plane
    weave = weave_table(width, plane, depth, edge_y, first_cell % CPC, first_lane(), wide)

    def place(start, layer):
        if not isinstance(start, int):
            return lambda: 2
        return lambda: layer(lax.axis_index("grp"), lax.axis_index("slab"))

    def first_layer():
        return lax.rem(lax.axis_index("grp") * brick_layers + (all_layers - 2), all_layers)

    own_layer = lambda g, s: (g * slabs + s) * layers
    cell_row = place(start_layer, lambda g, s: g * brick_layers)
    own_row = place(start_layer, own_layer)
    if direct:
        own_row = lambda: lax.axis_index("slab") * layers + 2
    new_shape = jax.ShapeDtypeStruct((2 * layers, flat), jnp.float32)
    solid_shape = jax.ShapeDtypeStruct((edge_x, wide), jnp.float32)
    span = max(width, wide)
    results = pl.pallas_call(
        functools.partial(
            finish_kernel, plane, depth, flat_cells, layers, sizes, first_layer,
            own_row if whole else None, cell_row, isinstance(start_layer, int),
        ),
        out_shape=(new_shape, solid_shape) if whole else (solid_shape,),
        in_specs=[VMEM] * 11,
        out_specs=(HBM,) * (1 + whole),
        scratch_shapes=[
            pltpu.VMEM((5, all_layers if direct else rows, width), jnp.float32),
            pltpu.VMEM((rows, span), jnp.float32),
            pltpu.VMEM((rows, span), jnp.float32),
            pltpu.VMEM((wide, edge_x), jnp.float32),
            pltpu.VMEM((edge_x, wide), jnp.float32),
            pltpu.VMEM((edge_x, wide), jnp.float32),
            pltpu.VMEM(new_shape.shape, jnp.float32),
            pltpu.SemaphoreType.DMA((CHUNKS + 1,)),
        ],
        compiler_params=PARAMS,
        name="finish",
    )(*inputs, kept, weave, packed, gathered, nucleation, frozen)
    if whole:
        new_field, new_solid = results
    else:
        (new_solid,) = results
        state, start_layer, _ = window(me * layers - 2, layers + 4, 0, rows_y // 2)
        own_row = place(start_layer, own_layer)
        new_field = pl.pallas_call(
            functools.partial(heat_kernel, plane, layers, own_row),
            out_shape=new_shape,
            in_specs=[VMEM],
            out_specs=VMEM,
            scratch_shapes=[pltpu.VMEM(state.shape[1:], jnp.float32)] * 2,
            compiler_params=PARAMS,
            name="heat",
        )(state)
    return new_field, new_solid[:, :flat_cells]


def solution(mesh):
    in_specs = (
        P(("grp", "slab"), None),
        P(("grp", "slab"), None),
        P(("grp", "slab"), None),
        P("grp", "slab"),
        P("grp", "slab"),
        P(),
        P(("grp", "slab")),
        P(("grp", "slab")),
    )
    out_specs = (P(("grp", "slab"), None), P("grp", "slab"))
    return jax.shard_map(body, mesh=mesh, in_specs=in_specs, out_specs=out_specs, check_vma=False)
```

```python
import functools

import jax
import jax.numpy as jnp
import numpy as np
from jax import lax
from jax.experimental import pallas as pl
from jax.experimental.pallas import tpu as pltpu
from jax.sharding import PartitionSpec as P

HEX_COUNT_LATER = 2
CPC = 8
LANES = 128
CHUNKS = 4
STEP = 0.004
AXES = ("grp", "slab")
VMEM = pl.BlockSpec(memory_space=pltpu.VMEM)
HBM = pl.BlockSpec(memory_space=pltpu.HBM)
PARAMS = pltpu.CompilerParams(vmem_limit_bytes=48 * 1024 * 1024)


def in_hbm(array):
    return pltpu.with_memory_space_constraint(array, pltpu.HBM)


def up_to(value, unit):
    return -(-value // unit) * unit


def split_index(value, by):
    if by & (by - 1) == 0:
        return value >> (by.bit_length() - 1), value & (by - 1)
    quotient = lax.div(value, jnp.full_like(value, by))
    return quotient, value - quotient * by


def pieces(values):
    out = []
    for _ in range(3):
        out.append(values.astype(jnp.bfloat16).astype(jnp.float32))
        values = values - out[-1]
    return out


def at_nodes(plane, flat, row):
    elements = row.shape[1]
    wide = up_to(elements, LANES)
    row = jnp.broadcast_to(row, (8, elements))
    if wide > elements:
        row = jnp.concatenate([row, jnp.zeros((8, wide - elements), jnp.float32)], 1)
    parts = []
    for start in range(0, flat, LANES):
        node_y, deep = split_index(lax.broadcasted_iota(jnp.int32, (8, LANES), 1) + start, plane)
        element = (node_y >> 1) * (plane // 2) + (deep >> 1)
        tile = start // 4 // LANES * LANES
        here = row[:, tile : tile + LANES]
        parts.append(jnp.take_along_axis(here, element - tile, axis=1, mode="promise_in_bounds"))
    return jnp.concatenate(parts, 1)[0:1] if len(parts) > 1 else parts[0][0:1]


def pack_kernel(
    plane, state_ref, heat_ref, kappa_ref, frozen_ref, label_ref, held_ref, *refs
):
    state, heat, kappa, frozen, label, sems = refs[-6:]
    edge_ref = refs[0] if len(refs) > 6 else held_ref.at[5:9, :]
    layers, elements = kappa.shape
    flat = state.shape[1]
    edge_x = frozen_ref.shape[0]
    top, bottom = pl.ds(0, 8), pl.ds(edge_x - 8, 8)
    copies = started(
        [
            (state_ref, state),
            (heat_ref, heat),
            (kappa_ref, kappa),
            (frozen_ref.at[top, :], frozen.at[0]),
            (frozen_ref.at[bottom, :], frozen.at[1]),
            (label_ref.at[top, :], label.at[0]),
            (label_ref.at[bottom, :], label.at[1]),
        ],
        sems,
    )
    for copy in copies[:3]:
        copy.wait()
    for layer in range(layers):
        lanes = slice(layer * flat, (layer + 1) * flat)
        for parity in range(2):
            row = slice(2 * layer + parity, 2 * layer + parity + 1)
            held_ref[parity : parity + 1, lanes] = state[row, :]
            held_ref[2 + parity : 3 + parity, lanes] = heat[row, :]
        held_ref[4:5, lanes] = at_nodes(plane, flat, kappa[layer : layer + 1, :])
    for copy in copies[3:]:
        copy.wait()
    edge_ref[0:1, :] = frozen[1, 7:8, :]
    edge_ref[1:2, :] = label[1, 7:8, :].astype(jnp.float32)
    edge_ref[2:3, :] = frozen[0, 0:1, :]
    edge_ref[3:4, :] = label[0, 0:1, :].astype(jnp.float32)


def pick_codes(table_ref, labels):
    half = table_ref.shape[0]
    tile, lane = labels >> 7, labels & (LANES - 1)
    upper = tile >= half
    row = jnp.where(upper, tile - half, tile)
    found = jnp.zeros(labels.shape, jnp.int32)
    for r in range(half):
        line = jnp.broadcast_to(table_ref[r : r + 1, :], labels.shape)
        here = jnp.take_along_axis(line, lane, axis=1, mode="promise_in_bounds")
        found = jnp.where(row == r, here, found)
    return jnp.where(upper, found >> 12, found) & 4095


def level(code, direction):
    return (((code >> (2 * direction)) & 3) + 1).astype(jnp.float32)


def started(pairs, sems):
    copies = [pltpu.make_async_copy(*pair, sems.at[i]) for i, pair in enumerate(pairs)]
    for copy in copies:
        copy.start()
    return copies


def faces_kernel(
    depth, flat, table_hbm, label_hbm, frozen_hbm,
    packed_ref, label_ref, frozen_ref, faces_ref, table_ref, sems,
):
    count = table_ref.shape[1]
    half = packed_ref.shape[0]
    edge_x = frozen_ref.shape[0]
    chunk = up_to(half, 4) // 4 * LANES
    order = [at for low in range(0, half * LANES, chunk) for at in (low, low + half * LANES)]
    order = [at for at in order if at < count]
    parts = [pl.ds(at, min(chunk, count - at)) for at in order]
    get_label, get_frozen, *get_table = started(
        [(label_hbm, label_ref), (frozen_hbm, frozen_ref)]
        + [(table_hbm.at[:, part], table_ref.at[:, part]) for part in parts],
        sems,
    )
    get_label.wait()
    get_frozen.wait()
    label = jnp.transpose(label_ref[...])
    label = jnp.concatenate([label[0:depth], label[flat - depth : flat]], 0)
    frozen = jnp.transpose(frozen_ref[...])
    frozen = 0.25 * jnp.concatenate([frozen[0:depth], frozen[flat - depth : flat]], 0)
    directions = table_ref.shape[0]
    place = 2 * lax.broadcasted_iota(jnp.int32, (directions, LANES), 0)

    def tile(number):
        size = max(min(LANES, count - number * LANES), 0)
        here = table_ref[:, number * LANES : number * LANES + size] if size else None
        if size == LANES:
            return here
        blank = jnp.ones((directions, LANES - size), jnp.int32)
        return jnp.concatenate([here, blank], 1) if size else blank

    waiting = dict(zip(order, get_table))
    for r in range(half):
        for at in (r * LANES, (r + half) * LANES):
            if at in waiting:
                waiting.pop(at).wait()
        bits = ((tile(r) - 1) << place) | ((tile(r + half) - 1) << (place + 12))
        packed_ref[r : r + 1, :] = jnp.sum(bits, axis=0, keepdims=True)
    short = -edge_x % LANES
    if short:
        label = jnp.concatenate([label, jnp.zeros((2 * depth, short), jnp.int32)], 1)
    for t in range(up_to(edge_x, LANES) // LANES):
        size = min(LANES, edge_x - t * LANES)
        lanes = slice(t * LANES, t * LANES + size)
        for part in range(2 * depth // 8):
            rows = slice(part * 8, part * 8 + 8)
            code = pick_codes(packed_ref, label[rows, t * LANES : (t + 1) * LANES])[:, :size]
            faces_ref[rows, lanes] = frozen[rows, lanes] * level(code, 2 if part * 8 < depth else 3)


def cells_kernel(
    depth, flat, packed_ref, label_ref, frozen_ref, faces_ref, gathered_ref, onward_ref, code_ref
):
    onward_ref[...] = faces_ref[...]
    edge_x, wide = frozen_ref.shape

    def look_up(chunk, carry):
        rows = pl.ds(pl.multiple_of(chunk * 8, 8), 8)
        for t in range(wide // LANES):
            lanes = pl.ds(t * LANES, LANES)
            code_ref[rows, lanes] = pick_codes(packed_ref, label_ref[rows, lanes])
        return carry

    lax.fori_loop(0, edge_x // 8, look_up, 0, unroll=16)
    frozen = frozen_ref[...] * 0.25
    code = code_ref[...]
    shares = [frozen * level(code, d) for d in range(6)]
    line_x = lax.broadcasted_iota(jnp.int32, (edge_x, wide), 0)
    lane = lax.broadcasted_iota(jnp.int32, (edge_x, wide), 1)
    deep = split_index(lane, depth)[1]
    total = jnp.where(line_x == edge_x - 1, 0.0, pltpu.roll(shares[0], edge_x - 1, 0))
    total += jnp.where(line_x == 0, 0.0, pltpu.roll(shares[1], 1, 0))
    total += jnp.where(lane >= flat - depth, 0.0, pltpu.roll(shares[2], wide - depth, 1))
    total += jnp.where(lane < depth, 0.0, pltpu.roll(shares[3], depth, 1))
    total += jnp.where(
        deep == depth - 1, pltpu.roll(shares[4], depth - 1, 1), pltpu.roll(shares[4], wide - 1, 1)
    )
    total += jnp.where(
        deep == 0, pltpu.roll(shares[5], wide - (depth - 1), 1), pltpu.roll(shares[5], 1, 1)
    )
    gathered_ref[...] = total


def sites_kernel(
    flat, packed_ref, edge_ref, faces_ref, slot_hbm, seed_hbm,
    nucleation_ref, ends_ref, onward_ref, slot_ref, seed_ref, sems,
):
    copies = started([(slot_hbm, slot_ref), (seed_hbm, seed_ref)], sems)
    onward_ref[...] = faces_ref[...]
    edge_x, wide = nucleation_ref.shape
    for t in range(wide // LANES):
        lanes = slice(t * LANES, (t + 1) * LANES)
        rough = jnp.concatenate([edge_ref[:, lanes], jnp.zeros((4, LANES), jnp.float32)], 0)
        codes = pick_codes(packed_ref, rough.astype(jnp.int32))
        ends_ref[0:1, lanes] = rough[0:1] * level(codes[1:2], 1) * 0.25
        ends_ref[1:2, lanes] = rough[2:3] * level(codes[3:4], 0) * 0.25
    for copy in copies:
        copy.wait()
    sites = seed_ref.shape[0]
    codes = pick_codes(packed_ref, seed_ref[...])
    worth = sum(level(codes, d) for d in range(6))
    site_x, site_lane = split_index(slot_ref[...], flat)
    at_x = lax.broadcasted_iota(jnp.int32, (edge_x, LANES), 0)
    at_lane = lax.broadcasted_iota(jnp.int32, (wide, LANES), 0)
    added = jnp.zeros((edge_x, wide), jnp.float32)
    for r in range(sites):
        left = jnp.where(at_x == site_x[r : r + 1], worth[r : r + 1], 0.0).astype(jnp.bfloat16)
        right = jnp.where(at_lane == site_lane[r : r + 1], 1.0, 0.0).astype(jnp.bfloat16)
        added += lax.dot_general(
            left, right, (((1,), (1,)), ((), ())), preferred_element_type=jnp.float32
        )
    nucleation_ref[...] = added * (1.0 / 6.0)


def advance(plane, even, odd, heat_even, heat_odd, kappa):
    rows, width = even.shape
    up = lambda v: pltpu.roll(v, rows - 1, 0)
    down = lambda v: pltpu.roll(v, 1, 0)
    turn = lambda v, by: pltpu.roll(v, by % width, 1)
    lane = lax.broadcasted_iota(jnp.int32, (rows, width), 1)
    row_y, deep = split_index(lane, plane)
    even_y, even_z = row_y & 1 == 0, deep & 1 == 0
    back = turn(kappa, 1)
    low_y = turn(kappa, plane)
    low_z = jnp.where(deep == 0, turn(kappa, 1 - plane), back)
    low = jnp.where(deep == 0, back, turn(kappa, plane + 1))
    spread_z = jnp.where(even_z, kappa + low_z, 4.0 * kappa)
    spread_z_low = jnp.where(even_z, low_y + low, 4.0 * low_y)
    spread_y = jnp.where(even_y, kappa + low_y, 4.0 * kappa)
    spread_y_low = jnp.where(even_y, low_z + low, 4.0 * low_z)
    scale = STEP * 27.0 * jnp.where(even_y, 1.0, 0.5) * jnp.where(even_z, 1.0, 0.5)
    share = scale * (1.0 / 108.0)
    along_x = share * jnp.where(even_y, spread_z + spread_z_low, 4.0 * spread_z)
    others = [
        share * spread_z,
        share * jnp.where(even_y, spread_z_low, spread_z),
        share * spread_y,
        share * jnp.where(even_z, spread_y_low, spread_y),
    ]
    behind_x = down(along_x)
    heat_even, heat_odd = scale * heat_even, (0.5 * scale) * heat_odd

    def in_plane(parts):
        after_y, before_y, after_z, before_z = parts
        own = jnp.where(even_y, 7.0 * (after_y + before_y), 16.0 * after_y)
        own = own + jnp.where(even_z, 7.0 * (after_z + before_z), 16.0 * after_z)
        far = [jnp.where(even_y, v, 0.0) for v in parts[:2]] + [
            jnp.where(even_z, v, 0.0) for v in parts[2:]
        ]
        return own, [-8.0 * v for v in parts], far

    own_even, near_even, far_even = in_plane([v + down(v) for v in others])
    own_odd, near_odd, far_odd = in_plane([2.0 * v for v in others])
    own_even = own_even + 7.0 * (along_x + behind_x)
    own_odd = own_odd + 8.0 * along_x
    near_x, near_behind, near_odd_x = -8.0 * along_x, -8.0 * behind_x, -4.0 * along_x

    def moved(values, by):
        if by > 0:
            return jnp.where(deep + by >= plane, turn(values, plane - by), turn(values, -by))
        return jnp.where(deep + by < 0, turn(values, -by - plane), turn(values, -by))

    def neighbours(values, near, far):
        ahead_y, back_y = turn(values, -plane), turn(values, plane)
        total = near[0] * ahead_y + near[1] * back_y
        total += near[2] * moved(values, 1) + near[3] * moved(values, -1)
        total += far[0] * turn(values, -2 * plane) + far[1] * turn(values, 2 * plane)
        if plane == 4:
            return total + (far[2] + far[3]) * moved(values, 2)
        return total + far[2] * moved(values, 2) + far[3] * moved(values, -2)

    def change(v_even, v_odd):
        following = up(v_even)
        k_even = own_even * v_even + along_x * following + behind_x * down(v_even)
        k_even += near_x * v_odd + near_behind * down(v_odd)
        k_odd = own_odd * v_odd + near_odd_x * (v_even + following)
        k_even += neighbours(v_even, near_even, far_even)
        k_odd += neighbours(v_odd, near_odd, far_odd)
        return heat_even - k_even, heat_odd - k_odd

    one_even, one_odd = change(even, odd)
    two_even, two_odd = change(even + one_even, odd + one_odd)
    return even + 0.5 * (one_even + two_even), odd + 0.5 * (one_odd + two_odd)


def heat_kernel(plane, layers, first_row, state_ref, new_ref, even_ref, odd_ref):
    even, odd = advance(plane, *(state_ref[i] for i in range(5)))
    even_ref[...] = even
    odd_ref[...] = odd
    start = first_row()
    for layer in range(layers):
        new_ref[2 * layer : 2 * layer + 1, :] = even_ref[pl.ds(start + layer, 1), :]
        new_ref[2 * layer + 1 : 2 * layer + 2, :] = odd_ref[pl.ds(start + layer, 1), :]


def basis(step):
    point = (step.astype(jnp.float32) + 0.5) / CPC
    return (
        2.0 * (point - 0.5) * (point - 1.0),
        -4.0 * point * (point - 1.0),
        2.0 * point * (point - 0.5),
    )


def finish_kernel(
    plane, depth, flat, layers, sizes, first_layer, first_row, cell_row, wraps,
    mine_ref, theirs_ref, across_ref, passing_ref, edge_ref, kept_ref, weave_ref,
    packed_ref, gathered_ref, nucleation_ref, frozen_ref, *refs,
):
    solid_out, state_ref, even_ref, odd_ref, side_ref, extra_ref, solid_ref, new_ref, sems = refs[-9:]
    edge_x, wide = frozen_ref.shape
    _, all_rows, width = state_ref.shape
    rows = even_ref.shape[0]
    heat_rows, across_row, passing_row, edge_row = sizes
    core = lax.axis_index("slab") & 1
    if heat_rows:
        slabs = lax.axis_size("slab")
        me = lax.axis_index("grp") * slabs + lax.axis_index("slab")
        state_ref[:, rows - 8 : rows, :] = jnp.zeros((5, 8, width), jnp.float32)
        own = arrival_order(bit_order(slabs, slabs))[: slabs // 2]
        numbers = [me ^ off for off in own]
        numbers += beyond_order(me, slabs)
        numbers += [me ^ 1 ^ off for off in own]
        numbers += beyond_order(me ^ 1, slabs)
        blocks = len(numbers) // 2
        for p, number in enumerate(numbers):
            source, block = (mine_ref, p) if p < blocks else (theirs_ref, p - blocks)
            row = lax.rem(number * layers + (all_rows - first_layer()), all_rows)
            for c in range(5):
                for layer in range(layers):
                    state_ref[c, pl.ds(row + layer, 1), :] = source[
                        block * 5 + c : block * 5 + c + 1, layer * width : (layer + 1) * width
                    ]
        state = [state_ref[i, 0:rows, :] for i in range(5)]
    else:
        state = [mine_ref[i] for i in range(5)]
    side_ref[...] = jnp.zeros(side_ref.shape, jnp.float32)
    there = jnp.where(core == 0, 0, flat - depth)
    side_ref[pl.ds(pl.multiple_of(there, 8), depth), :] = (
        kept_ref[...] + passing_ref[passing_row : passing_row + depth, :]
    )
    side_ref[pl.ds(pl.multiple_of(flat - depth - there, 8), depth), :] = across_ref[
        across_row : across_row + depth, :
    ]
    extra_ref[...] = gathered_ref[...] + jnp.transpose(side_ref[...])
    extra_ref[0:1, :] += edge_ref[edge_row : edge_row + 1, 0:wide]
    extra_ref[edge_x - 1 : edge_x, :] += edge_ref[edge_row + 1 : edge_row + 2, 0:wide]
    even, odd = advance(plane, *state)
    if first_row is not None:
        even_ref[:, 0:width] = even
        odd_ref[:, 0:width] = odd
        start = first_row()
        for layer in range(layers):
            new_ref[2 * layer : 2 * layer + 1, :] = even_ref[pl.ds(start + layer, 1), 0:width]
            new_ref[2 * layer + 1 : 2 * layer + 2, :] = odd_ref[pl.ds(start + layer, 1), 0:width]
        new_copy = pltpu.make_async_copy(new_ref, refs[0], sems.at[CHUNKS])
        new_copy.start()
    both = jnp.concatenate([even, odd], 0)
    first, second, third = pieces(both)
    joined = jnp.concatenate([first, second, third, first, second], 1)
    high, low = weave_ref[0:width, :], weave_ref[width : 2 * width, :]
    woven = jnp.dot(
        joined.astype(jnp.bfloat16),
        jnp.concatenate([high, high, high, low, low], 0),
        preferred_element_type=jnp.float32,
    )
    base = cell_row()
    if not isinstance(base, int):
        even_ref[:, 0:wide] = woven[:rows]
        odd_ref[:, 0:wide] = woven[rows:]
    first, middle, last = basis(lax.broadcasted_iota(jnp.int32, (CPC, wide), 0))
    elements = edge_x // CPC
    copies = []
    for a in range(elements):
        cells = slice(a * CPC, (a + 1) * CPC)
        later = base + (a + 1)
        if wraps:
            later = lax.rem(later, rows)
        if isinstance(base, int):
            at = slice(base + a, base + a + 1)
            lower, between, higher = woven[at], woven[rows:][at], woven[base + a + 1 : base + a + 2]
        else:
            lower, between = (ref[pl.ds(base + a, 1), 0:wide] for ref in (even_ref, odd_ref))
            higher = even_ref[pl.ds(later, 1), 0:wide]
        temperature = first * lower + middle * between + last * higher
        under = jnp.maximum(-temperature, 0.0)
        rate = under * (under * extra_ref[cells, :] + nucleation_ref[cells, :])
        frozen = frozen_ref[cells, :]
        solid_ref[cells, :] = frozen + (1.0 - frozen) * (1.0 - jnp.exp(-rate))
        done = (a + 1) * CHUNKS // elements
        if done > len(copies):
            low = copies[-1][1] if copies else 0
            part = pl.ds(low, (a + 1) * CPC - low)
            copy = pltpu.make_async_copy(
                solid_ref.at[part, :], solid_out.at[part, :], sems.at[len(copies)]
            )
            copy.start()
            copies.append((copy, (a + 1) * CPC))
    for copy, _ in copies:
        copy.wait()
    if first_row is not None:
        new_copy.wait()


def weave_table(width, plane, depth, edge_y, first_step, first_node, wide):
    row, cell = jnp.arange(2 * width)[:, None], jnp.arange(wide)[None, :]
    node = (row - first_node) % width
    cell_y, cell_z = first_step + cell // depth, cell % depth
    step_y = node // plane - 2 * (cell_y // CPC)
    step_z = (node % plane - 2 * (cell_z // CPC)) % plane
    take = lambda step, at: sum(jnp.where(step == i, v, 0.0) for i, v in enumerate(basis(at % CPC)))
    full = take(step_y, cell_y) * take(step_z, cell_z)
    high = jnp.floor(full * 128.0) * (1.0 / 128.0)
    part = jnp.where(row < width, high, full - high)
    return jnp.where(cell < edge_y * depth, part, 0.0).astype(jnp.bfloat16)


def bit_order(devices, slabs):
    top, middle = devices.bit_length() - 2, slabs.bit_length() - 2
    return [*range(top, middle, -1), *range(2, middle + 1), *([1] if middle > 0 else [])]


def beyond_order(me, slabs):
    top = slabs.bit_length() - 2

    def kept(number, bit):
        if bit < 2:
            return [number ^ slabs ^ 1]
        flips = (1 << bit) | 1
        return [picked(number, bit), picked(number ^ flips, bit)]

    def picked(number, bit):
        held = kept(number, bit - 1)
        if len(held) == 1:
            return held[0]
        same = ((number >> bit) ^ (number >> (bit - 1))) & 1 == 0
        return jnp.where(same, held[0], held[1])

    return kept(me, top) + kept(me ^ 3, top)


def arrival_order(bits):
    offs = [0]
    for bit in bits:
        offs += [off ^ (1 << bit) ^ 1 for off in offs]
    return offs + [off ^ 1 for off in offs]


def lines(values, width):
    flat = values.reshape(-1)
    return jnp.pad(flat, (0, -flat.shape[0] % width)).reshape(-1, width)


def body(
    thermal_state_values,
    thermal_kappa_values,
    nodal_heating_input,
    frozen_share_map,
    crystal_label_map,
    growth_reach_table,
    seed_site_slots,
    seed_crystal_label,
):
    groups, slabs = lax.axis_size("grp"), lax.axis_size("slab")
    devices = groups * slabs
    group, slab = lax.axis_index("grp"), lax.axis_index("slab")
    me = group * slabs + slab
    layers, elements = thermal_kappa_values.shape
    plane = 2 * HEX_COUNT_LATER
    depth = CPC * HEX_COUNT_LATER
    flat = thermal_state_values.shape[1]
    rows_y = flat // plane
    edge_x, flat_cells = frozen_share_map.shape
    edge_y = flat_cells // depth
    wide = up_to(flat_cells, LANES)
    all_layers = layers * devices

    def exchanged(parts, flips, sent=None):
        at = [0]
        for part in parts[:-1]:
            at.append(at[-1] + part.shape[0])
        total = at[-1] + parts[-1].shape[0]
        if sent is None:
            sent = sum(
                jnp.pad(part, ((row, total - row - part.shape[0]), (0, 0)))
                for row, part in zip(at, parts)
            )
        return sent, lax.ppermute(sent, AXES, [(i, i ^ flips) for i in range(devices)]), at

    def widened(array):
        return jnp.pad(array, ((0, 0), (0, wide - flat_cells)))

    unit = layers * flat
    count = growth_reach_table.shape[0]
    frozen, label = widened(frozen_share_map), widened(crystal_label_map)
    joined = groups == 2 and wide == unit
    packed_rows = pl.pallas_call(
        functools.partial(pack_kernel, plane),
        out_shape=[jax.ShapeDtypeStruct((9, unit), jnp.float32)]
        if joined
        else [
            jax.ShapeDtypeStruct((5, unit), jnp.float32),
            jax.ShapeDtypeStruct((4, wide), jnp.float32),
        ],
        in_specs=[HBM] * 5,
        out_specs=[VMEM] * (1 if joined else 2),
        scratch_shapes=[
            pltpu.VMEM(thermal_state_values.shape, jnp.float32),
            pltpu.VMEM(nodal_heating_input.shape, jnp.float32),
            pltpu.VMEM(thermal_kappa_values.shape, jnp.float32),
            pltpu.VMEM((2, 8, wide), jnp.float32),
            pltpu.VMEM((2, 8, wide), jnp.int32),
            pltpu.SemaphoreType.DMA((7,)),
        ],
        compiler_params=PARAMS,
        name="pack",
    )(*map(in_hbm, (thermal_state_values, nodal_heating_input, thermal_kappa_values, frozen, label)))
    held, edge_rows = packed_rows[0][:5], packed_rows[0][5:] if joined else packed_rows[1]
    high_edge, low_edge = edge_rows[:2], edge_rows[2:]

    brick_layers = edge_x // CPC
    need_y = (edge_y + CPC - 2) // CPC + 6
    width = up_to(need_y * 2 * plane, LANES)
    if 2 * width > flat:
        width = flat
    need_layers = brick_layers + 5
    whole = width == flat and 2 * up_to(need_layers, 8) > all_layers
    direct = whole and edge_x == unit and wide == unit and groups == 2 and slabs > 2
    table_lanes = up_to(count, 2 * LANES)
    packed, label, frozen, faces = pl.pallas_call(
        functools.partial(faces_kernel, depth, flat_cells),
        out_shape=(
            jax.ShapeDtypeStruct((table_lanes // (2 * LANES), LANES), jnp.int32),
            jax.ShapeDtypeStruct((edge_x, wide), jnp.int32),
            jax.ShapeDtypeStruct((edge_x, wide), jnp.float32),
            jax.ShapeDtypeStruct((2 * depth, edge_x), jnp.float32),
        ),
        in_specs=[HBM] * 3,
        out_specs=[VMEM] * 4,
        scratch_shapes=[
            pltpu.VMEM((growth_reach_table.shape[1], count), jnp.int32),
            pltpu.SemaphoreType.DMA((10,)),
        ],
        compiler_params=PARAMS,
        name="faces",
    )(in_hbm(growth_reach_table.T), in_hbm(label), in_hbm(frozen))
    gathered, faces_later = pl.pallas_call(
        functools.partial(cells_kernel, depth, flat_cells),
        out_shape=(
            jax.ShapeDtypeStruct((edge_x, wide), jnp.float32),
            jax.ShapeDtypeStruct((2 * depth, edge_x), jnp.float32),
        ),
        in_specs=[VMEM] * 4,
        out_specs=[VMEM] * 2,
        scratch_shapes=[pltpu.VMEM((edge_x, wide), jnp.int32)],
        compiler_params=PARAMS,
        name="cells",
    )(packed, label, frozen, faces)
    seeds = up_to(seed_site_slots.shape[0], LANES)
    short = seeds - seed_site_slots.shape[0]

    def sites(edges):
        return pl.pallas_call(
            functools.partial(sites_kernel, flat_cells),
            out_shape=(
                jax.ShapeDtypeStruct((edge_x, wide), jnp.float32),
                jax.ShapeDtypeStruct((2, wide), jnp.float32),
                jax.ShapeDtypeStruct((2 * depth, edge_x), jnp.float32),
            ),
            in_specs=[VMEM] * 3 + [HBM] * 2,
            out_specs=[VMEM] * 3,
            scratch_shapes=[
                pltpu.VMEM((seeds // LANES, LANES), jnp.int32),
                pltpu.VMEM((seeds // LANES, LANES), jnp.int32),
                pltpu.SemaphoreType.DMA((2,)),
            ],
            compiler_params=PARAMS,
            name="sites",
        )(
            packed,
            edges,
            faces_later,
            in_hbm(jnp.pad(seed_site_slots, (0, short), constant_values=-1).reshape(-1, LANES)),
            in_hbm(jnp.pad(seed_crystal_label, (0, short)).reshape(-1, LANES)),
        )

    core, pair = me & 1, slab >> 1

    def packets(faces):
        return jnp.where(core == 1, faces[depth:], 0.0), jnp.where(core == 0, faces[:depth], 0.0)

    onward, backward = packets(faces)
    heat, edges = [held], None
    beyond = []
    if groups > 2:
        ring = [(i, (i + 1) % groups) for i in range(groups)]
        edges = jnp.concatenate(
            [
                lax.ppermute(high_edge, "grp", ring),
                lax.ppermute(low_edge, "grp", [(j, i) for i, j in ring]),
            ]
        )
    moved, ends = 0, None
    as_face = lambda part: part.reshape(-1)[: depth * edge_x].reshape(depth, edge_x)
    for bit in bit_order(devices, slabs):
        rides = 1 << bit < slabs
        low = (1 << (bit - 1)) - 1
        moves_on, moves_back = (pair & low) == 1, (pair & low) == low - 1
        extra = []
        if groups == 2 and 1 << bit == slabs:
            extra = [lines(edge_rows, unit)]
        elif rides and low:
            extra = [lines(jnp.where(moves_on, onward, backward), unit)]
        elif rides:
            extra = [lines(onward, unit), lines(backward, unit)]
        first_sent = packed_rows[0] if joined and 1 << bit == slabs else None
        if bit > 1 and len(beyond) == 2:
            same = ((me >> bit) ^ (me >> (bit - 1))) & 1 == 0
            beyond = [jnp.where(same, *beyond)]
        sent, got, at = exchanged(heat + beyond + extra, (1 << bit) | 1, first_sent)
        heat_rows = sum(part.shape[0] for part in heat)
        if direct and 1 << bit == slabs:
            beyond = [got[:heat_rows]]
        else:
            beyond = beyond + [
                got[row : row + part.shape[0]] for row, part in zip(at[len(heat) :], beyond)
            ]
            heat = heat + [got[:heat_rows]]
        parts = [got[row : row + part.shape[0]] for row, part in zip(at[len(at) - len(extra) :], extra)]
        if groups == 2 and 1 << bit == slabs:
            edges = parts[0].reshape(-1)[: 4 * wide].reshape(4, wide)
        elif rides and low:
            if moved == 0:
                onward, backward = packets(faces_later)
            onward = jnp.where(moves_on, as_face(parts[0]), onward)
            backward = jnp.where(moves_back, as_face(parts[0]), backward)
            moved += 1
        elif rides:
            onward, backward = as_face(parts[0]), as_face(parts[1])
        if edges is not None and ends is None:
            nucleation, ends, faces_last = sites(edges)
    extra = [
        lines(jnp.where(core == 0, faces_last[depth:], faces_last[:depth]), unit),
        lines(jnp.where(core == 1, onward, backward), unit),
    ]
    if groups == 2:
        extra.append(lines(ends, unit))
    kept = jnp.where(core == 0, onward, backward)
    heat = heat + beyond
    sent, got, at = exchanged(heat + extra, 1)
    heat_rows = sum(part.shape[0] for part in heat)
    at = at[len(heat) :]
    across, passing = (as_face(got[row : row + part.shape[0]]) for row, part in zip(at, extra[:2]))
    if groups == 2:
        ends = got[at[2] : at[2] + extra[2].shape[0]].reshape(-1)[: 2 * wide].reshape(2, wide)
    first_cell = slab * edge_y
    first_element = first_cell // CPC
    if direct:
        inputs = (sent, got, got, got, got)
        sizes = (heat_rows, *at)
        start_layer, start_y = group * brick_layers - 2, 0
        rows = min(up_to(need_layers, 8), all_layers)
    else:
        order = np.argsort(arrival_order(bit_order(devices, slabs)))
        blocks = jnp.concatenate([sent[:heat_rows], got[:heat_rows]], 0).reshape(devices, 5, layers, flat)
        blocks = jnp.take(blocks, jnp.asarray(order)[jnp.arange(devices) ^ me], axis=0)
        held = jnp.moveaxis(blocks, 1, 0).reshape(5, all_layers, flat)

        def window(first_layer, need_layers, first_element, need_elements):
            rows, lanes = up_to(need_layers, 8), up_to(need_elements * 2 * plane, LANES)
            part, start_layer, start_y = held, 0, 0
            if 2 * rows <= all_layers:
                start_layer = first_layer
                part = lax.dynamic_slice_in_dim(
                    jnp.concatenate([part, part[:, :rows]], 1),
                    jnp.remainder(start_layer, all_layers), rows, 1,
                )
            if 2 * lanes <= flat:
                start_y = 2 * first_element
                shifted = lambda v, by, size: lax.dynamic_slice_in_dim(
                    jnp.concatenate([v, v[..., :size]], -1), by, size, v.ndim - 1
                )
                start = jnp.remainder(first_element, rows_y // 2)
                part = shifted(part, start * 2 * plane, lanes)
            return part, start_layer, start_y

        state, start_layer, start_y = window(
            group * brick_layers - 2, need_layers, first_element - 2, need_y
        )
        inputs = (state, state, across, passing, ends)
        sizes = (0, 0, 0, 0)
        rows = state.shape[1]
    if isinstance(start_y, int):
        first_lane = lambda: lax.rem(
            lax.div(lax.axis_index("slab") * edge_y, CPC) * (2 * plane), width
        )
    else:
        first_lane = lambda: 4 * plane
    weave = weave_table(width, plane, depth, edge_y, first_cell % CPC, first_lane(), wide)

    def place(start, layer):
        if not isinstance(start, int):
            return lambda: 2
        return lambda: layer(lax.axis_index("grp"), lax.axis_index("slab"))

    def first_layer():
        return lax.rem(lax.axis_index("grp") * brick_layers + (all_layers - 2), all_layers)

    own_layer = lambda g, s: (g * slabs + s) * layers
    cell_row = place(start_layer, lambda g, s: g * brick_layers)
    own_row = place(start_layer, own_layer)
    if direct:
        own_row = lambda: lax.axis_index("slab") * layers + 2
    new_shape = jax.ShapeDtypeStruct((2 * layers, flat), jnp.float32)
    solid_shape = jax.ShapeDtypeStruct((edge_x, wide), jnp.float32)
    span = max(width, wide)
    results = pl.pallas_call(
        functools.partial(
            finish_kernel, plane, depth, flat_cells, layers, sizes, first_layer,
            own_row if whole else None, cell_row, isinstance(start_layer, int),
        ),
        out_shape=(new_shape, solid_shape) if whole else (solid_shape,),
        in_specs=[VMEM] * 11,
        out_specs=(HBM,) * (1 + whole),
        scratch_shapes=[
            pltpu.VMEM((5, all_layers if direct else rows, width), jnp.float32),
            pltpu.VMEM((rows, span), jnp.float32),
            pltpu.VMEM((rows, span), jnp.float32),
            pltpu.VMEM((wide, edge_x), jnp.float32),
            pltpu.VMEM((edge_x, wide), jnp.float32),
            pltpu.VMEM((edge_x, wide), jnp.float32),
            pltpu.VMEM(new_shape.shape, jnp.float32),
            pltpu.SemaphoreType.DMA((CHUNKS + 1,)),
        ],
        compiler_params=PARAMS,
        name="finish",
    )(*inputs, kept, weave, packed, gathered, nucleation, frozen)
    if whole:
        new_field, new_solid = results
    else:
        (new_solid,) = results
        state, start_layer, _ = window(me * layers - 2, layers + 4, 0, rows_y // 2)
        own_row = place(start_layer, own_layer)
        new_field = pl.pallas_call(
            functools.partial(heat_kernel, plane, layers, own_row),
            out_shape=new_shape,
            in_specs=[VMEM],
            out_specs=VMEM,
            scratch_shapes=[pltpu.VMEM(state.shape[1:], jnp.float32)] * 2,
            compiler_params=PARAMS,
            name="heat",
        )(state)
    return new_field, new_solid[:, :flat_cells]


def solution(mesh):
    in_specs = (
        P(("grp", "slab"), None),
        P(("grp", "slab"), None),
        P(("grp", "slab"), None),
        P("grp", "slab"),
        P("grp", "slab"),
        P(),
        P(("grp", "slab")),
        P(("grp", "slab")),
    )
    out_specs = (P(("grp", "slab"), None), P("grp", "slab"))
    return jax.shard_map(body, mesh=mesh, in_specs=in_specs, out_specs=out_specs, check_vma=False)
```

```python
import functools

import jax
import jax.numpy as jnp
import numpy as np
from jax import lax
from jax.experimental import pallas as pl
from jax.experimental.pallas import tpu as pltpu
from jax.sharding import PartitionSpec as P

HEX_COUNT_LATER = 2
CPC = 8
LANES = 128
CHUNKS = 2
STEP = 0.004
AXES = ("grp", "slab")
VMEM = pl.BlockSpec(memory_space=pltpu.VMEM)
HBM = pl.BlockSpec(memory_space=pltpu.HBM)
PARAMS = pltpu.CompilerParams(vmem_limit_bytes=48 * 1024 * 1024)


def in_hbm(array):
    return pltpu.with_memory_space_constraint(array, pltpu.HBM)


def up_to(value, unit):
    return -(-value // unit) * unit


def split_index(value, by):
    if by & (by - 1) == 0:
        return value >> (by.bit_length() - 1), value & (by - 1)
    quotient = lax.div(value, jnp.full_like(value, by))
    return quotient, value - quotient * by


def pieces(values):
    out = []
    for _ in range(3):
        out.append(values.astype(jnp.bfloat16).astype(jnp.float32))
        values = values - out[-1]
    return out


def at_nodes(plane, flat, row):
    elements = row.shape[1]
    wide = up_to(elements, LANES)
    row = jnp.broadcast_to(row, (8, elements))
    if wide > elements:
        row = jnp.concatenate([row, jnp.zeros((8, wide - elements), jnp.float32)], 1)
    parts = []
    for start in range(0, flat, LANES):
        node_y, deep = split_index(lax.broadcasted_iota(jnp.int32, (8, LANES), 1) + start, plane)
        element = (node_y >> 1) * (plane // 2) + (deep >> 1)
        tile = start // 4 // LANES * LANES
        here = row[:, tile : tile + LANES]
        parts.append(jnp.take_along_axis(here, element - tile, axis=1, mode="promise_in_bounds"))
    return jnp.concatenate(parts, 1)[0:1] if len(parts) > 1 else parts[0][0:1]


def pack_kernel(
    plane, state_ref, heat_ref, kappa_ref, frozen_ref, label_ref, held_ref, *refs
):
    state, heat, kappa, frozen, label, sems = refs[-6:]
    edge_ref = refs[0] if len(refs) > 6 else held_ref.at[5:9, :]
    layers, elements = kappa.shape
    flat = state.shape[1]
    edge_x = frozen_ref.shape[0]
    top, bottom = pl.ds(0, 8), pl.ds(edge_x - 8, 8)
    copies = started(
        [
            (state_ref, state),
            (heat_ref, heat),
            (kappa_ref, kappa),
            (frozen_ref.at[top, :], frozen.at[0]),
            (frozen_ref.at[bottom, :], frozen.at[1]),
            (label_ref.at[top, :], label.at[0]),
            (label_ref.at[bottom, :], label.at[1]),
        ],
        sems,
    )
    for copy in copies[:3]:
        copy.wait()
    for layer in range(layers):
        lanes = slice(layer * flat, (layer + 1) * flat)
        for parity in range(2):
            row = slice(2 * layer + parity, 2 * layer + parity + 1)
            held_ref[parity : parity + 1, lanes] = state[row, :]
            held_ref[2 + parity : 3 + parity, lanes] = heat[row, :]
        held_ref[4:5, lanes] = at_nodes(plane, flat, kappa[layer : layer + 1, :])
    for copy in copies[3:]:
        copy.wait()
    edge_ref[0:1, :] = frozen[1, 7:8, :]
    edge_ref[1:2, :] = label[1, 7:8, :].astype(jnp.float32)
    edge_ref[2:3, :] = frozen[0, 0:1, :]
    edge_ref[3:4, :] = label[0, 0:1, :].astype(jnp.float32)


def pick_codes(table_ref, labels):
    half = table_ref.shape[0]
    tile, lane = labels >> 7, labels & (LANES - 1)
    upper = tile >= half
    row = jnp.where(upper, tile - half, tile)
    found = jnp.zeros(labels.shape, jnp.int32)
    for r in range(half):
        line = jnp.broadcast_to(table_ref[r : r + 1, :], labels.shape)
        here = jnp.take_along_axis(line, lane, axis=1, mode="promise_in_bounds")
        found = jnp.where(row == r, here, found)
    return jnp.where(upper, found >> 12, found) & 4095


def level(code, direction):
    return (((code >> (2 * direction)) & 3) + 1).astype(jnp.float32)


def started(pairs, sems):
    copies = [pltpu.make_async_copy(*pair, sems.at[i]) for i, pair in enumerate(pairs)]
    for copy in copies:
        copy.start()
    return copies


def faces_kernel(
    depth, flat, table_hbm, label_hbm, frozen_hbm,
    packed_ref, label_ref, frozen_ref, faces_ref, table_ref, sems,
):
    count = table_ref.shape[1]
    half = packed_ref.shape[0]
    edge_x = frozen_ref.shape[0]
    chunk = up_to(half, 4) // 4 * LANES
    order = [at for low in range(0, half * LANES, chunk) for at in (low, low + half * LANES)]
    order = [at for at in order if at < count]
    parts = [pl.ds(at, min(chunk, count - at)) for at in order]
    get_label, get_frozen, *get_table = started(
        [(label_hbm, label_ref), (frozen_hbm, frozen_ref)]
        + [(table_hbm.at[:, part], table_ref.at[:, part]) for part in parts],
        sems,
    )
    get_label.wait()
    get_frozen.wait()
    label = jnp.transpose(label_ref[...])
    label = jnp.concatenate([label[0:depth], label[flat - depth : flat]], 0)
    frozen = jnp.transpose(frozen_ref[...])
    frozen = 0.25 * jnp.concatenate([frozen[0:depth], frozen[flat - depth : flat]], 0)
    directions = table_ref.shape[0]
    place = 2 * lax.broadcasted_iota(jnp.int32, (directions, LANES), 0)

    def tile(number):
        size = max(min(LANES, count - number * LANES), 0)
        here = table_ref[:, number * LANES : number * LANES + size] if size else None
        if size == LANES:
            return here
        blank = jnp.ones((directions, LANES - size), jnp.int32)
        return jnp.concatenate([here, blank], 1) if size else blank

    waiting = dict(zip(order, get_table))
    for r in range(half):
        for at in (r * LANES, (r + half) * LANES):
            if at in waiting:
                waiting.pop(at).wait()
        bits = ((tile(r) - 1) << place) | ((tile(r + half) - 1) << (place + 12))
        packed_ref[r : r + 1, :] = jnp.sum(bits, axis=0, keepdims=True)
    short = -edge_x % LANES
    if short:
        label = jnp.concatenate([label, jnp.zeros((2 * depth, short), jnp.int32)], 1)
    for t in range(up_to(edge_x, LANES) // LANES):
        size = min(LANES, edge_x - t * LANES)
        lanes = slice(t * LANES, t * LANES + size)
        for part in range(2 * depth // 8):
            rows = slice(part * 8, part * 8 + 8)
            code = pick_codes(packed_ref, label[rows, t * LANES : (t + 1) * LANES])[:, :size]
            faces_ref[rows, lanes] = frozen[rows, lanes] * level(code, 2 if part * 8 < depth else 3)


def cells_kernel(
    depth, flat, packed_ref, label_ref, frozen_ref, faces_ref, gathered_ref, onward_ref, code_ref
):
    onward_ref[...] = faces_ref[...]
    edge_x, wide = frozen_ref.shape

    def look_up(chunk, carry):
        rows = pl.ds(pl.multiple_of(chunk * 8, 8), 8)
        for t in range(wide // LANES):
            lanes = pl.ds(t * LANES, LANES)
            code_ref[rows, lanes] = pick_codes(packed_ref, label_ref[rows, lanes])
        return carry

    lax.fori_loop(0, edge_x // 8, look_up, 0, unroll=16)
    frozen = frozen_ref[...] * 0.25
    code = code_ref[...]
    shares = [frozen * level(code, d) for d in range(6)]
    line_x = lax.broadcasted_iota(jnp.int32, (edge_x, wide), 0)
    lane = lax.broadcasted_iota(jnp.int32, (edge_x, wide), 1)
    deep = split_index(lane, depth)[1]
    total = jnp.where(line_x == edge_x - 1, 0.0, pltpu.roll(shares[0], edge_x - 1, 0))
    total += jnp.where(line_x == 0, 0.0, pltpu.roll(shares[1], 1, 0))
    total += jnp.where(lane >= flat - depth, 0.0, pltpu.roll(shares[2], wide - depth, 1))
    total += jnp.where(lane < depth, 0.0, pltpu.roll(shares[3], depth, 1))
    total += jnp.where(
        deep == depth - 1, pltpu.roll(shares[4], depth - 1, 1), pltpu.roll(shares[4], wide - 1, 1)
    )
    total += jnp.where(
        deep == 0, pltpu.roll(shares[5], wide - (depth - 1), 1), pltpu.roll(shares[5], 1, 1)
    )
    gathered_ref[...] = total


def sites_kernel(
    flat, packed_ref, edge_ref, faces_ref, slot_hbm, seed_hbm,
    nucleation_ref, ends_ref, onward_ref, slot_ref, seed_ref, sems,
):
    copies = started([(slot_hbm, slot_ref), (seed_hbm, seed_ref)], sems)
    onward_ref[...] = faces_ref[...]
    edge_x, wide = nucleation_ref.shape
    for t in range(wide // LANES):
        lanes = slice(t * LANES, (t + 1) * LANES)
        rough = jnp.concatenate([edge_ref[:, lanes], jnp.zeros((4, LANES), jnp.float32)], 0)
        codes = pick_codes(packed_ref, rough.astype(jnp.int32))
        ends_ref[0:1, lanes] = rough[0:1] * level(codes[1:2], 1) * 0.25
        ends_ref[1:2, lanes] = rough[2:3] * level(codes[3:4], 0) * 0.25
    for copy in copies:
        copy.wait()
    sites = seed_ref.shape[0]
    codes = pick_codes(packed_ref, seed_ref[...])
    worth = sum(level(codes, d) for d in range(6))
    site_x, site_lane = split_index(slot_ref[...], flat)
    at_x = lax.broadcasted_iota(jnp.int32, (edge_x, LANES), 0)
    at_lane = lax.broadcasted_iota(jnp.int32, (wide, LANES), 0)
    added = jnp.zeros((edge_x, wide), jnp.float32)
    for r in range(sites):
        left = jnp.where(at_x == site_x[r : r + 1], worth[r : r + 1], 0.0).astype(jnp.bfloat16)
        right = jnp.where(at_lane == site_lane[r : r + 1], 1.0, 0.0).astype(jnp.bfloat16)
        added += lax.dot_general(
            left, right, (((1,), (1,)), ((), ())), preferred_element_type=jnp.float32
        )
    nucleation_ref[...] = added * (1.0 / 6.0)


def advance(plane, even, odd, heat_even, heat_odd, kappa):
    rows, width = even.shape
    up = lambda v: pltpu.roll(v, rows - 1, 0)
    down = lambda v: pltpu.roll(v, 1, 0)
    turn = lambda v, by: pltpu.roll(v, by % width, 1)
    lane = lax.broadcasted_iota(jnp.int32, (rows, width), 1)
    row_y, deep = split_index(lane, plane)
    even_y, even_z = row_y & 1 == 0, deep & 1 == 0
    back = turn(kappa, 1)
    low_y = turn(kappa, plane)
    low_z = jnp.where(deep == 0, turn(kappa, 1 - plane), back)
    low = jnp.where(deep == 0, back, turn(kappa, plane + 1))
    spread_z = jnp.where(even_z, kappa + low_z, 4.0 * kappa)
    spread_z_low = jnp.where(even_z, low_y + low, 4.0 * low_y)
    spread_y = jnp.where(even_y, kappa + low_y, 4.0 * kappa)
    spread_y_low = jnp.where(even_y, low_z + low, 4.0 * low_z)
    scale = STEP * 27.0 * jnp.where(even_y, 1.0, 0.5) * jnp.where(even_z, 1.0, 0.5)
    share = scale * (1.0 / 108.0)
    along_x = share * jnp.where(even_y, spread_z + spread_z_low, 4.0 * spread_z)
    others = [
        share * spread_z,
        share * jnp.where(even_y, spread_z_low, spread_z),
        share * spread_y,
        share * jnp.where(even_z, spread_y_low, spread_y),
    ]
    behind_x = down(along_x)
    heat_even, heat_odd = scale * heat_even, (0.5 * scale) * heat_odd

    def in_plane(parts):
        after_y, before_y, after_z, before_z = parts
        own = jnp.where(even_y, 7.0 * (after_y + before_y), 16.0 * after_y)
        own = own + jnp.where(even_z, 7.0 * (after_z + before_z), 16.0 * after_z)
        far = [jnp.where(even_y, v, 0.0) for v in parts[:2]] + [
            jnp.where(even_z, v, 0.0) for v in parts[2:]
        ]
        return own, [-8.0 * v for v in parts], far

    own_even, near_even, far_even = in_plane([v + down(v) for v in others])
    own_odd, near_odd, far_odd = in_plane([2.0 * v for v in others])
    own_even = own_even + 7.0 * (along_x + behind_x)
    own_odd = own_odd + 8.0 * along_x
    near_x, near_behind, near_odd_x = -8.0 * along_x, -8.0 * behind_x, -4.0 * along_x

    def moved(values, by):
        if by > 0:
            return jnp.where(deep + by >= plane, turn(values, plane - by), turn(values, -by))
        return jnp.where(deep + by < 0, turn(values, -by - plane), turn(values, -by))

    def neighbours(values, near, far):
        ahead_y, back_y = turn(values, -plane), turn(values, plane)
        total = near[0] * ahead_y + near[1] * back_y
        total += near[2] * moved(values, 1) + near[3] * moved(values, -1)
        total += far[0] * turn(values, -2 * plane) + far[1] * turn(values, 2 * plane)
        if plane == 4:
            return total + (far[2] + far[3]) * moved(values, 2)
        return total + far[2] * moved(values, 2) + far[3] * moved(values, -2)

    def change(v_even, v_odd):
        following = up(v_even)
        k_even = own_even * v_even + along_x * following + behind_x * down(v_even)
        k_even += near_x * v_odd + near_behind * down(v_odd)
        k_odd = own_odd * v_odd + near_odd_x * (v_even + following)
        k_even += neighbours(v_even, near_even, far_even)
        k_odd += neighbours(v_odd, near_odd, far_odd)
        return heat_even - k_even, heat_odd - k_odd

    one_even, one_odd = change(even, odd)
    two_even, two_odd = change(even + one_even, odd + one_odd)
    return even + 0.5 * (one_even + two_even), odd + 0.5 * (one_odd + two_odd)


def heat_kernel(plane, layers, first_row, state_ref, new_ref, even_ref, odd_ref):
    even, odd = advance(plane, *(state_ref[i] for i in range(5)))
    even_ref[...] = even
    odd_ref[...] = odd
    start = first_row()
    for layer in range(layers):
        new_ref[2 * layer : 2 * layer + 1, :] = even_ref[pl.ds(start + layer, 1), :]
        new_ref[2 * layer + 1 : 2 * layer + 2, :] = odd_ref[pl.ds(start + layer, 1), :]


def basis(step):
    point = (step.astype(jnp.float32) + 0.5) / CPC
    return (
        2.0 * (point - 0.5) * (point - 1.0),
        -4.0 * point * (point - 1.0),
        2.0 * point * (point - 0.5),
    )


def finish_kernel(
    plane, depth, flat, layers, sizes, first_layer, first_row, cell_row, wraps,
    mine_ref, theirs_ref, across_ref, passing_ref, edge_ref, kept_ref, weave_ref,
    packed_ref, gathered_ref, nucleation_ref, frozen_ref, *refs,
):
    solid_out, state_ref, even_ref, odd_ref, side_ref, extra_ref, solid_ref, new_ref, sems = refs[-9:]
    edge_x, wide = frozen_ref.shape
    _, all_rows, width = state_ref.shape
    rows = even_ref.shape[0]
    heat_rows, across_row, passing_row, edge_row = sizes
    core = lax.axis_index("slab") & 1
    if heat_rows:
        slabs = lax.axis_size("slab")
        me = lax.axis_index("grp") * slabs + lax.axis_index("slab")
        state_ref[:, rows - 8 : rows, :] = jnp.zeros((5, 8, width), jnp.float32)
        own = arrival_order(bit_order(slabs, slabs))[: slabs // 2]
        numbers = [me ^ off for off in own]
        numbers += beyond_order(me, slabs)
        numbers += [me ^ 1 ^ off for off in own]
        numbers += beyond_order(me ^ 1, slabs)
        blocks = len(numbers) // 2
        for p, number in enumerate(numbers):
            source, block = (mine_ref, p) if p < blocks else (theirs_ref, p - blocks)
            row = lax.rem(number * layers + (all_rows - first_layer()), all_rows)
            for c in range(5):
                for layer in range(layers):
                    state_ref[c, pl.ds(row + layer, 1), :] = source[
                        block * 5 + c : block * 5 + c + 1, layer * width : (layer + 1) * width
                    ]
        state = [state_ref[i, 0:rows, :] for i in range(5)]
    else:
        state = [mine_ref[i] for i in range(5)]
    side_ref[...] = jnp.zeros(side_ref.shape, jnp.float32)
    there = jnp.where(core == 0, 0, flat - depth)
    side_ref[pl.ds(pl.multiple_of(there, 8), depth), :] = (
        kept_ref[...] + passing_ref[passing_row : passing_row + depth, :]
    )
    side_ref[pl.ds(pl.multiple_of(flat - depth - there, 8), depth), :] = across_ref[
        across_row : across_row + depth, :
    ]
    extra_ref[...] = gathered_ref[...] + jnp.transpose(side_ref[...])
    extra_ref[0:1, :] += edge_ref[edge_row : edge_row + 1, 0:wide]
    extra_ref[edge_x - 1 : edge_x, :] += edge_ref[edge_row + 1 : edge_row + 2, 0:wide]
    even, odd = advance(plane, *state)
    if first_row is not None:
        even_ref[:, 0:width] = even
        odd_ref[:, 0:width] = odd
        start = first_row()
        for layer in range(layers):
            new_ref[2 * layer : 2 * layer + 1, :] = even_ref[pl.ds(start + layer, 1), 0:width]
            new_ref[2 * layer + 1 : 2 * layer + 2, :] = odd_ref[pl.ds(start + layer, 1), 0:width]
        new_copy = pltpu.make_async_copy(new_ref, refs[0], sems.at[CHUNKS])
        new_copy.start()
    both = jnp.concatenate([even, odd], 0)
    first, second, third = pieces(both)
    joined = jnp.concatenate([first, second, third, first, second], 1)
    high, low = weave_ref[0:width, :], weave_ref[width : 2 * width, :]
    woven = jnp.dot(
        joined.astype(jnp.bfloat16),
        jnp.concatenate([high, high, high, low, low], 0),
        preferred_element_type=jnp.float32,
    )
    base = cell_row()
    if not isinstance(base, int):
        even_ref[:, 0:wide] = woven[:rows]
        odd_ref[:, 0:wide] = woven[rows:]
    first, middle, last = basis(lax.broadcasted_iota(jnp.int32, (CPC, wide), 0))
    elements = edge_x // CPC
    copies = []
    for a in range(elements):
        cells = slice(a * CPC, (a + 1) * CPC)
        later = base + (a + 1)
        if wraps:
            later = lax.rem(later, rows)
        if isinstance(base, int):
            at = slice(base + a, base + a + 1)
            lower, between, higher = woven[at], woven[rows:][at], woven[base + a + 1 : base + a + 2]
        else:
            lower, between = (ref[pl.ds(base + a, 1), 0:wide] for ref in (even_ref, odd_ref))
            higher = even_ref[pl.ds(later, 1), 0:wide]
        temperature = first * lower + middle * between + last * higher
        under = jnp.maximum(-temperature, 0.0)
        rate = under * (under * extra_ref[cells, :] + nucleation_ref[cells, :])
        frozen = frozen_ref[cells, :]
        solid_ref[cells, :] = frozen + (1.0 - frozen) * (1.0 - jnp.exp(-rate))
        done = (a + 1) * CHUNKS // elements
        if done > len(copies):
            low = copies[-1][1] if copies else 0
            part = pl.ds(low, (a + 1) * CPC - low)
            copy = pltpu.make_async_copy(
                solid_ref.at[part, :], solid_out.at[part, :], sems.at[len(copies)]
            )
            copy.start()
            copies.append((copy, (a + 1) * CPC))
    for copy, _ in copies:
        copy.wait()
    if first_row is not None:
        new_copy.wait()


def weave_table(width, plane, depth, edge_y, first_step, first_node, wide):
    row, cell = jnp.arange(2 * width)[:, None], jnp.arange(wide)[None, :]
    node = (row - first_node) % width
    cell_y, cell_z = first_step + cell // depth, cell % depth
    step_y = node // plane - 2 * (cell_y // CPC)
    step_z = (node % plane - 2 * (cell_z // CPC)) % plane
    take = lambda step, at: sum(jnp.where(step == i, v, 0.0) for i, v in enumerate(basis(at % CPC)))
    full = take(step_y, cell_y) * take(step_z, cell_z)
    high = jnp.floor(full * 128.0) * (1.0 / 128.0)
    part = jnp.where(row < width, high, full - high)
    return jnp.where(cell < edge_y * depth, part, 0.0).astype(jnp.bfloat16)


def bit_order(devices, slabs):
    top, middle = devices.bit_length() - 2, slabs.bit_length() - 2
    return [*range(top, middle, -1), *range(2, middle + 1), *([1] if middle > 0 else [])]


def beyond_order(me, slabs):
    top = slabs.bit_length() - 2

    def kept(number, bit):
        if bit < 2:
            return [number ^ slabs ^ 1]
        flips = (1 << bit) | 1
        return [picked(number, bit), picked(number ^ flips, bit)]

    def picked(number, bit):
        held = kept(number, bit - 1)
        if len(held) == 1:
            return held[0]
        same = ((number >> bit) ^ (number >> (bit - 1))) & 1 == 0
        return jnp.where(same, held[0], held[1])

    return kept(me, top) + kept(me ^ 3, top)


def arrival_order(bits):
    offs = [0]
    for bit in bits:
        offs += [off ^ (1 << bit) ^ 1 for off in offs]
    return offs + [off ^ 1 for off in offs]


def lines(values, width):
    flat = values.reshape(-1)
    return jnp.pad(flat, (0, -flat.shape[0] % width)).reshape(-1, width)


def body(
    thermal_state_values,
    thermal_kappa_values,
    nodal_heating_input,
    frozen_share_map,
    crystal_label_map,
    growth_reach_table,
    seed_site_slots,
    seed_crystal_label,
):
    groups, slabs = lax.axis_size("grp"), lax.axis_size("slab")
    devices = groups * slabs
    group, slab = lax.axis_index("grp"), lax.axis_index("slab")
    me = group * slabs + slab
    layers, elements = thermal_kappa_values.shape
    plane = 2 * HEX_COUNT_LATER
    depth = CPC * HEX_COUNT_LATER
    flat = thermal_state_values.shape[1]
    rows_y = flat // plane
    edge_x, flat_cells = frozen_share_map.shape
    edge_y = flat_cells // depth
    wide = up_to(flat_cells, LANES)
    all_layers = layers * devices

    def exchanged(parts, flips, sent=None):
        at = [0]
        for part in parts[:-1]:
            at.append(at[-1] + part.shape[0])
        total = at[-1] + parts[-1].shape[0]
        if sent is None:
            sent = sum(
                jnp.pad(part, ((row, total - row - part.shape[0]), (0, 0)))
                for row, part in zip(at, parts)
            )
        return sent, lax.ppermute(sent, AXES, [(i, i ^ flips) for i in range(devices)]), at

    def widened(array):
        return jnp.pad(array, ((0, 0), (0, wide - flat_cells)))

    unit = layers * flat
    count = growth_reach_table.shape[0]
    frozen, label = widened(frozen_share_map), widened(crystal_label_map)
    joined = groups == 2 and wide == unit
    packed_rows = pl.pallas_call(
        functools.partial(pack_kernel, plane),
        out_shape=[jax.ShapeDtypeStruct((9, unit), jnp.float32)]
        if joined
        else [
            jax.ShapeDtypeStruct((5, unit), jnp.float32),
            jax.ShapeDtypeStruct((4, wide), jnp.float32),
        ],
        in_specs=[HBM] * 5,
        out_specs=[VMEM] * (1 if joined else 2),
        scratch_shapes=[
            pltpu.VMEM(thermal_state_values.shape, jnp.float32),
            pltpu.VMEM(nodal_heating_input.shape, jnp.float32),
            pltpu.VMEM(thermal_kappa_values.shape, jnp.float32),
            pltpu.VMEM((2, 8, wide), jnp.float32),
            pltpu.VMEM((2, 8, wide), jnp.int32),
            pltpu.SemaphoreType.DMA((7,)),
        ],
        compiler_params=PARAMS,
        name="pack",
    )(*map(in_hbm, (thermal_state_values, nodal_heating_input, thermal_kappa_values, frozen, label)))
    held, edge_rows = packed_rows[0][:5], packed_rows[0][5:] if joined else packed_rows[1]
    high_edge, low_edge = edge_rows[:2], edge_rows[2:]

    brick_layers = edge_x // CPC
    need_y = (edge_y + CPC - 2) // CPC + 6
    width = up_to(need_y * 2 * plane, LANES)
    if 2 * width > flat:
        width = flat
    need_layers = brick_layers + 5
    whole = width == flat and 2 * up_to(need_layers, 8) > all_layers
    direct = whole and edge_x == unit and wide == unit and groups == 2 and slabs > 2
    table_lanes = up_to(count, 2 * LANES)
    packed, label, frozen, faces = pl.pallas_call(
        functools.partial(faces_kernel, depth, flat_cells),
        out_shape=(
            jax.ShapeDtypeStruct((table_lanes // (2 * LANES), LANES), jnp.int32),
            jax.ShapeDtypeStruct((edge_x, wide), jnp.int32),
            jax.ShapeDtypeStruct((edge_x, wide), jnp.float32),
            jax.ShapeDtypeStruct((2 * depth, edge_x), jnp.float32),
        ),
        in_specs=[HBM] * 3,
        out_specs=[VMEM] * 4,
        scratch_shapes=[
            pltpu.VMEM((growth_reach_table.shape[1], count), jnp.int32),
            pltpu.SemaphoreType.DMA((10,)),
        ],
        compiler_params=PARAMS,
        name="faces",
    )(in_hbm(growth_reach_table.T), in_hbm(label), in_hbm(frozen))
    gathered, faces_later = pl.pallas_call(
        functools.partial(cells_kernel, depth, flat_cells),
        out_shape=(
            jax.ShapeDtypeStruct((edge_x, wide), jnp.float32),
            jax.ShapeDtypeStruct((2 * depth, edge_x), jnp.float32),
        ),
        in_specs=[VMEM] * 4,
        out_specs=[VMEM] * 2,
        scratch_shapes=[pltpu.VMEM((edge_x, wide), jnp.int32)],
        compiler_params=PARAMS,
        name="cells",
    )(packed, label, frozen, faces)
    seeds = up_to(seed_site_slots.shape[0], LANES)
    short = seeds - seed_site_slots.shape[0]

    def sites(edges):
        return pl.pallas_call(
            functools.partial(sites_kernel, flat_cells),
            out_shape=(
                jax.ShapeDtypeStruct((edge_x, wide), jnp.float32),
                jax.ShapeDtypeStruct((2, wide), jnp.float32),
                jax.ShapeDtypeStruct((2 * depth, edge_x), jnp.float32),
            ),
            in_specs=[VMEM] * 3 + [HBM] * 2,
            out_specs=[VMEM] * 3,
            scratch_shapes=[
                pltpu.VMEM((seeds // LANES, LANES), jnp.int32),
                pltpu.VMEM((seeds // LANES, LANES), jnp.int32),
                pltpu.SemaphoreType.DMA((2,)),
            ],
            compiler_params=PARAMS,
            name="sites",
        )(
            packed,
            edges,
            faces_later,
            in_hbm(jnp.pad(seed_site_slots, (0, short), constant_values=-1).reshape(-1, LANES)),
            in_hbm(jnp.pad(seed_crystal_label, (0, short)).reshape(-1, LANES)),
        )

    core, pair = me & 1, slab >> 1

    def packets(faces):
        return jnp.where(core == 1, faces[depth:], 0.0), jnp.where(core == 0, faces[:depth], 0.0)

    onward, backward = packets(faces)
    heat, edges = [held], None
    beyond = []
    if groups > 2:
        ring = [(i, (i + 1) % groups) for i in range(groups)]
        edges = jnp.concatenate(
            [
                lax.ppermute(high_edge, "grp", ring),
                lax.ppermute(low_edge, "grp", [(j, i) for i, j in ring]),
            ]
        )
    moved, ends = 0, None
    as_face = lambda part: part.reshape(-1)[: depth * edge_x].reshape(depth, edge_x)
    for bit in bit_order(devices, slabs):
        rides = 1 << bit < slabs
        low = (1 << (bit - 1)) - 1
        moves_on, moves_back = (pair & low) == 1, (pair & low) == low - 1
        extra = []
        if groups == 2 and 1 << bit == slabs:
            extra = [lines(edge_rows, unit)]
        elif rides and low:
            extra = [lines(jnp.where(moves_on, onward, backward), unit)]
        elif rides:
            extra = [lines(onward, unit), lines(backward, unit)]
        first_sent = packed_rows[0] if joined and 1 << bit == slabs else None
        if bit > 1 and len(beyond) == 2:
            same = ((me >> bit) ^ (me >> (bit - 1))) & 1 == 0
            beyond = [jnp.where(same, *beyond)]
        sent, got, at = exchanged(heat + beyond + extra, (1 << bit) | 1, first_sent)
        heat_rows = sum(part.shape[0] for part in heat)
        if direct and 1 << bit == slabs:
            beyond = [got[:heat_rows]]
        else:
            beyond = beyond + [
                got[row : row + part.shape[0]] for row, part in zip(at[len(heat) :], beyond)
            ]
            heat = heat + [got[:heat_rows]]
        parts = [got[row : row + part.shape[0]] for row, part in zip(at[len(at) - len(extra) :], extra)]
        if groups == 2 and 1 << bit == slabs:
            edges = parts[0].reshape(-1)[: 4 * wide].reshape(4, wide)
        elif rides and low:
            if moved == 0:
                onward, backward = packets(faces_later)
            onward = jnp.where(moves_on, as_face(parts[0]), onward)
            backward = jnp.where(moves_back, as_face(parts[0]), backward)
            moved += 1
        elif rides:
            onward, backward = as_face(parts[0]), as_face(parts[1])
        if edges is not None and ends is None:
            nucleation, ends, faces_last = sites(edges)
    extra = [
        lines(jnp.where(core == 0, faces_last[depth:], faces_last[:depth]), unit),
        lines(jnp.where(core == 1, onward, backward), unit),
    ]
    if groups == 2:
        extra.append(lines(ends, unit))
    kept = jnp.where(core == 0, onward, backward)
    heat = heat + beyond
    sent, got, at = exchanged(heat + extra, 1)
    heat_rows = sum(part.shape[0] for part in heat)
    at = at[len(heat) :]
    across, passing = (as_face(got[row : row + part.shape[0]]) for row, part in zip(at, extra[:2]))
    if groups == 2:
        ends = got[at[2] : at[2] + extra[2].shape[0]].reshape(-1)[: 2 * wide].reshape(2, wide)
    first_cell = slab * edge_y
    first_element = first_cell // CPC
    if direct:
        inputs = (sent, got, got, got, got)
        sizes = (heat_rows, *at)
        start_layer, start_y = group * brick_layers - 2, 0
        rows = min(up_to(need_layers, 8), all_layers)
    else:
        order = np.argsort(arrival_order(bit_order(devices, slabs)))
        blocks = jnp.concatenate([sent[:heat_rows], got[:heat_rows]], 0).reshape(devices, 5, layers, flat)
        blocks = jnp.take(blocks, jnp.asarray(order)[jnp.arange(devices) ^ me], axis=0)
        held = jnp.moveaxis(blocks, 1, 0).reshape(5, all_layers, flat)

        def window(first_layer, need_layers, first_element, need_elements):
            rows, lanes = up_to(need_layers, 8), up_to(need_elements * 2 * plane, LANES)
            part, start_layer, start_y = held, 0, 0
            if 2 * rows <= all_layers:
                start_layer = first_layer
                part = lax.dynamic_slice_in_dim(
                    jnp.concatenate([part, part[:, :rows]], 1),
                    jnp.remainder(start_layer, all_layers), rows, 1,
                )
            if 2 * lanes <= flat:
                start_y = 2 * first_element
                shifted = lambda v, by, size: lax.dynamic_slice_in_dim(
                    jnp.concatenate([v, v[..., :size]], -1), by, size, v.ndim - 1
                )
                start = jnp.remainder(first_element, rows_y // 2)
                part = shifted(part, start * 2 * plane, lanes)
            return part, start_layer, start_y

        state, start_layer, start_y = window(
            group * brick_layers - 2, need_layers, first_element - 2, need_y
        )
        inputs = (state, state, across, passing, ends)
        sizes = (0, 0, 0, 0)
        rows = state.shape[1]
    if isinstance(start_y, int):
        first_lane = lambda: lax.rem(
            lax.div(lax.axis_index("slab") * edge_y, CPC) * (2 * plane), width
        )
    else:
        first_lane = lambda: 4 * plane
    weave = weave_table(width, plane, depth, edge_y, first_cell % CPC, first_lane(), wide)

    def place(start, layer):
        if not isinstance(start, int):
            return lambda: 2
        return lambda: layer(lax.axis_index("grp"), lax.axis_index("slab"))

    def first_layer():
        return lax.rem(lax.axis_index("grp") * brick_layers + (all_layers - 2), all_layers)

    own_layer = lambda g, s: (g * slabs + s) * layers
    cell_row = place(start_layer, lambda g, s: g * brick_layers)
    own_row = place(start_layer, own_layer)
    if direct:
        own_row = lambda: lax.axis_index("slab") * layers + 2
    new_shape = jax.ShapeDtypeStruct((2 * layers, flat), jnp.float32)
    solid_shape = jax.ShapeDtypeStruct((edge_x, wide), jnp.float32)
    span = max(width, wide)
    results = pl.pallas_call(
        functools.partial(
            finish_kernel, plane, depth, flat_cells, layers, sizes, first_layer,
            own_row if whole else None, cell_row, isinstance(start_layer, int),
        ),
        out_shape=(new_shape, solid_shape) if whole else (solid_shape,),
        in_specs=[VMEM] * 11,
        out_specs=(HBM,) * (1 + whole),
        scratch_shapes=[
            pltpu.VMEM((5, all_layers if direct else rows, width), jnp.float32),
            pltpu.VMEM((rows, span), jnp.float32),
            pltpu.VMEM((rows, span), jnp.float32),
            pltpu.VMEM((wide, edge_x), jnp.float32),
            pltpu.VMEM((edge_x, wide), jnp.float32),
            pltpu.VMEM((edge_x, wide), jnp.float32),
            pltpu.VMEM(new_shape.shape, jnp.float32),
            pltpu.SemaphoreType.DMA((CHUNKS + 1,)),
        ],
        compiler_params=PARAMS,
        name="finish",
    )(*inputs, kept, weave, packed, gathered, nucleation, frozen)
    if whole:
        new_field, new_solid = results
    else:
        (new_solid,) = results
        state, start_layer, _ = window(me * layers - 2, layers + 4, 0, rows_y // 2)
        own_row = place(start_layer, own_layer)
        new_field = pl.pallas_call(
            functools.partial(heat_kernel, plane, layers, own_row),
            out_shape=new_shape,
            in_specs=[VMEM],
            out_specs=VMEM,
            scratch_shapes=[pltpu.VMEM(state.shape[1:], jnp.float32)] * 2,
            compiler_params=PARAMS,
            name="heat",
        )(state)
    return new_field, new_solid[:, :flat_cells]


def solution(mesh):
    in_specs = (
        P(("grp", "slab"), None),
        P(("grp", "slab"), None),
        P(("grp", "slab"), None),
        P("grp", "slab"),
        P("grp", "slab"),
        P(),
        P(("grp", "slab")),
        P(("grp", "slab")),
    )
    out_specs = (P(("grp", "slab"), None), P("grp", "slab"))
    return jax.shard_map(body, mesh=mesh, in_specs=in_specs, out_specs=out_specs, check_vma=False)
```
